32 devices in a mesh: gx: 4 (over x, core), gy: 4 (over z), gz: 2 (over y).
Axes of the slice: x: 2, y: 2, z: 4, core: 2. Of those that a mesh axis runs over, the one named last changes fastest.
Arguments:
- fine_blocks: float32 [8, 8, 8, 7, 4096], P('gx', 'gy', 'gz'), may hold values from -0.75 to 0.75
- prolong: float32 [8, 8, 8, 1024], P('gx', 'gy', 'gz'), may hold values from -1.5 to 1.5
- agg_map: int32 [8, 8, 8], replicated, may hold values from 0 to 7, as said below
- owner_map: int32 [4, 4, 16], P('gx', 'gy', 'gz'), may hold values from 0 to 1, as said below
Outputs:
- coarse_rows: float32 [4, 4, 16, 14336], P('gx', 'gy', 'gz')
The draws below stay inside these ranges and needn't reach their ends.
Inputs may be any that keep to these rules, and one draw needn't show every extreme that they name: `agg_map`: every one of the 8 slots of each brick names at least one element of that brick. `owner_map`: owners are devices with the same gx and gy indices as the brick. Each brick gives exactly 4 of its slots to each owner. The elements of one brick whose rows go to one owner number at most 12, and exactly 12 for one owner of every brick.
All inputs are finite; a program needn't handle non-finite values.
Results may differ from the reference program's by a relative error of at most 0.0001.
Values sent between devices are 32-bit elements; how exact they have to be, the bound alone decides.
No kernel may reach another device: no remote copies, remote signals or barrier semaphores. Data moves between devices by JAX's collectives and lax.ppermute only.
A program may use at most 64 MiB of HBM per device.

```python
import jax
import jax.numpy as jnp
from jax import lax

DOF = 64
CDOF = 16
BX = 2
BY = 2
BZ = 4
AGGS = 8
NX = 8
NY = 8
NZ = 8


def layout_plan(key):
    bricks_x = NX // BX
    bricks_y = NY // BY
    bricks_z = NZ // BZ
    group_size = bricks_z
    elements = BX * BY * BZ
    rows_each = AGGS // group_size
    capacity = min(2 * elements // group_size, elements - (group_size - 1) * rows_each)
    extras = elements - capacity - (group_size - 1) * rows_each
    others_count = group_size - 1
    brick_count = bricks_x * bricks_y * bricks_z

    def one_brick(brick):
        brick_key = jax.random.fold_in(jax.random.fold_in(key, 11), brick)
        keys = jax.random.split(brick_key, 5)
        heavy = jax.random.randint(keys[0], (), 0, group_size)
        offset = jax.random.randint(keys[1], (), 0, others_count)
        others = jnp.arange(others_count, dtype=jnp.int32)
        added = extras // others_count + ((others - offset) % others_count < extras % others_count).astype(jnp.int32)
        targets = (heavy + 1 + others) % group_size
        counts = jnp.full((group_size,), rows_each, jnp.int32).at[targets].add(added).at[heavy].set(capacity)
        labels = jnp.repeat(jnp.arange(group_size, dtype=jnp.int32), counts, total_repeat_length=elements)
        starts = jnp.cumsum(counts) - counts
        ranks = jnp.arange(elements, dtype=jnp.int32) - starts[labels]
        extra_sub = jax.random.randint(keys[2], (elements,), 0, rows_each)
        subslot = jnp.where(ranks < rows_each, ranks, extra_sub)
        slot_perm = jax.random.permutation(keys[3], AGGS).astype(jnp.int32)
        agg_ids = slot_perm[labels * rows_each + subslot]
        element_perm = jax.random.permutation(keys[4], elements)
        placed = agg_ids[element_perm]
        inverse = jnp.argsort(slot_perm).astype(jnp.int32)
        owner_ids = inverse // rows_each
        return (placed.reshape(BX, BY, BZ), owner_ids)
    placed_all, owners_all = jax.vmap(one_brick)(jnp.arange(brick_count, dtype=jnp.int32))
    agg_full = placed_all.reshape(bricks_x, bricks_y, bricks_z, BX, BY, BZ).transpose(0, 3, 1, 4, 2, 5).reshape(NX, NY, NZ)
    owner_full = owners_all.reshape(bricks_x, bricks_y, bricks_z * AGGS)
    return (agg_full.astype(jnp.int32), owner_full.astype(jnp.int32))


def draw_agg_map(key, part):
    return layout_plan(key)[0]


def draw_owner_map(key, part):
    return layout_plan(key)[1]


def block_levels(stream_key, extent, pieces, least, high):
    def one(axis_at, blocks):
        draws = jax.random.uniform(jax.random.fold_in(jax.random.fold_in(stream_key, 6), axis_at), (blocks,), jnp.float32, least / len(pieces), high / len(pieces))
        return jnp.repeat(jnp.exp(draws), extent[axis_at] // blocks).reshape((-1,) + (1,) * (len(extent) - axis_at - 1))

    loudness = one(*pieces[0])
    for cut in pieces[1:]:
        loudness = loudness * one(*cut)
    return loudness


def gaussian(key, dims, width, bound, cuts=(), kind=jnp.bfloat16):
    values = width * jax.random.normal(key, dims, jnp.float32)
    if cuts:
        values = values * block_levels(key, dims, cuts, -0.22, 0.18)
    return jnp.clip(values, -bound, bound).astype(kind)


def setup_inputs(seed: int = 0) -> dict:
    arg_keys = jax.random.split(jax.random.key(seed), 5)
    return {
        "fine_blocks": gaussian(arg_keys[0], (NX, NY, NZ, 7, DOF * DOF), DOF ** -0.5, 0.75, ((0, 4), (1, 4), (2, 2)), jnp.float32),
        "prolong": gaussian(arg_keys[1], (NX, NY, NZ, DOF * CDOF), 0.25, 1.5, ((0, 4), (1, 4), (2, 2)), jnp.float32),
        "agg_map": draw_agg_map(jax.random.fold_in(arg_keys[4], 71), 0),
        "owner_map": draw_owner_map(jax.random.fold_in(arg_keys[4], 71), 0),
    }


face_steps = ((0, 0, 0), (-1, 0, 0), (1, 0, 0), (0, -1, 0), (0, 1, 0), (0, 0, -1), (0, 0, 1))


def reference(fine_blocks, prolong, agg_map, owner_map):
    bricks_x = NX // BX
    bricks_y = NY // BY
    bricks_z = NZ // BZ
    rows_each = AGGS // bricks_z
    blocks = fine_blocks.reshape(NX, NY, NZ, 7, DOF, DOF)
    bases = prolong.reshape(NX, NY, NZ, DOF, CDOF)
    padded = jnp.pad(bases, ((1, 1), (1, 1), (1, 1), (0, 0), (0, 0)))

    def plane(index):
        block_plane = lax.dynamic_index_in_dim(blocks, index, 0, keepdims=False)
        window = lax.dynamic_slice_in_dim(padded, index, 3, 0)
        beside = jnp.stack([window[1 + sx, 1 + sy:1 + sy + NY, 1 + sz:1 + sz + NZ] for sx, sy, sz in face_steps], axis=2)
        products = jnp.einsum('yzkij,yzkjc->yzkic', block_plane, beside, precision=lax.Precision.HIGHEST)
        own_base = window[1, 1:NY + 1, 1:NZ + 1]
        coarse = jnp.einsum('yzic,yzkid->yzkcd', own_base, products, precision=lax.Precision.HIGHEST)
        return coarse.reshape(NY, NZ, 7, CDOF * CDOF)

    terms = lax.map(plane, jnp.arange(NX, dtype=jnp.int32))
    padded_agg = jnp.pad(agg_map, 1)
    coord_x = jnp.arange(NX, dtype=jnp.int32)[:, None, None]
    coord_y = jnp.arange(NY, dtype=jnp.int32)[None, :, None]
    coord_z = jnp.arange(NZ, dtype=jnp.int32)[None, None, :]
    columns = []
    for face, (sx, sy, sz) in enumerate(face_steps):
        neighbour = padded_agg[1 + sx:1 + sx + NX, 1 + sy:1 + sy + NY, 1 + sz:1 + sz + NZ]
        inside = ((coord_x % BX + sx >= 0) & (coord_x % BX + sx < BX) & (coord_y % BY + sy >= 0) & (coord_y % BY + sy < BY) & (coord_z % BZ + sz >= 0) & (coord_z % BZ + sz < BZ))
        relation = jnp.where(inside, 0, face).astype(jnp.int32)
        columns.append(relation * AGGS + neighbour)
    column_slot = jnp.stack(columns, axis=3).astype(jnp.int32)
    owners = owner_map.reshape(bricks_x, bricks_y, bricks_z, AGGS)
    slot_ids = jnp.arange(AGGS, dtype=jnp.int32)
    earlier = (owners[..., None, :] == owners[..., :, None]) & (slot_ids[None, :] < slot_ids[:, None])
    rank_in_owner = jnp.sum(earlier.astype(jnp.int32), axis=-1)
    brick_x = jnp.broadcast_to(coord_x // BX, (NX, NY, NZ))
    brick_y = jnp.broadcast_to(coord_y // BY, (NX, NY, NZ))
    brick_z = jnp.broadcast_to(coord_z // BZ, (NX, NY, NZ))
    owner_of = owners[brick_x, brick_y, brick_z, agg_map]
    rank_of = rank_in_owner[brick_x, brick_y, brick_z, agg_map]
    row_slot = ((brick_x * bricks_y + brick_y) * bricks_z + owner_of) * AGGS + brick_z * rows_each + rank_of
    row_slot = row_slot.astype(jnp.int32)
    total_rows = bricks_x * bricks_y * bricks_z * AGGS
    result = jnp.zeros((total_rows, 7 * AGGS, CDOF * CDOF), jnp.float32)
    row_index = jnp.broadcast_to(row_slot[..., None], column_slot.shape)
    result = result.at[row_index, column_slot].add(terms)
    return result.reshape(bricks_x, bricks_y, bricks_z * AGGS, 7 * AGGS * CDOF * CDOF)
```

```python
import functools

import jax
import jax.numpy as jnp
from jax import lax
from jax.experimental import pallas as pl
from jax.experimental.pallas import tpu as pltpu
from jax.sharding import PartitionSpec as P

DOF = 64
CDOF = 16
AGGS = 8
LANES = 128
F32 = jnp.float32
BF16 = jnp.bfloat16
VMEM = pl.BlockSpec(memory_space=pltpu.VMEM)
SMEM = pl.BlockSpec(memory_space=pltpu.SMEM)


def iota(shape, dim):
    return lax.broadcasted_iota(jnp.int32, shape, dim)


def dot(a, b):
    return lax.dot_general(a, b, (((1,), (0,)), ((), ())), preferred_element_type=F32)


def split(x):
    high = x.astype(BF16)
    return high, (x - high.astype(F32)).astype(BF16)


def ones_where(mask):
    return jnp.where(mask, 1.0, 0.0).astype(BF16)


def collapse_matrix():
    same = iota((LANES, LANES), 0) % CDOF == iota((LANES, LANES), 1) % CDOF
    one = ones_where(same)
    return jnp.concatenate([one, one], axis=0)


def prolong_weights(pieces, collapse):
    diag = iota((DOF, LANES), 0) % 8 == iota((DOF, LANES), 1) // CDOF
    rows = []
    for piece in pieces:
        high, low = split(piece)
        parts = []
        for part in (high.astype(F32), low.astype(F32)):
            wide = jnp.broadcast_to(part[:, None, :], (8, 8, LANES)).reshape(DOF, LANES)
            parts.append(jnp.where(diag, wide, 0.0).astype(BF16))
        rows.append(jnp.concatenate(parts, axis=1))
    spread = dot(jnp.concatenate(rows, axis=0), collapse)
    lane = iota((DOF, LANES), 1)
    slot = lane // CDOF % 4
    full = spread[:DOF]
    for i in range(1, 4):
        full = jnp.where(slot == i, spread[i * DOF : (i + 1) * DOF], full)
    high, low = split(full)
    left = lane < DOF
    high, low = high.astype(F32), low.astype(F32)
    both = jnp.where(left, high, low).astype(BF16)
    first = jnp.where(left, high, 0.0).astype(BF16)
    return jnp.concatenate([both, both, first, first], axis=0)


def blocks_of(rows, weights):
    out = dot(rows, weights)
    return out + pltpu.roll(out, DOF, 1)


def diagonal(product, shift):
    keep = iota((DOF, LANES), 0) // CDOF + shift == iota((DOF, LANES), 1) // CDOF % 4
    kept = jnp.where(keep, product, 0.0).reshape(4, CDOF, LANES)
    return (kept[0] + kept[1]) + (kept[2] + kept[3])


def scatter_tools():
    spread = ones_where(iota((LANES, 2 * LANES), 0) % CDOF == iota((LANES, 2 * LANES), 1) % CDOF)
    element = ones_where(iota((LANES, LANES), 0) // CDOF == iota((LANES, LANES), 1) // CDOF)
    row = ones_where(iota((LANES, 2 * LANES), 0) % CDOF == iota((LANES, 2 * LANES), 1) // CDOF)
    return spread, element, jnp.concatenate([row, row], axis=0)


def scatter(pack, labels, base, count, tools):
    spread, element, row = tools
    high, low = split(pack)
    wide = [jnp.concatenate([part] * 8, axis=0) * element for part in (high, low)]
    flat = dot(jnp.concatenate(wide, axis=0), spread).astype(BF16) * row
    choose = ones_where(iota((count, LANES), 0) + base == labels)
    return dot(jnp.concatenate([choose, choose], axis=1), flat)


def lane_row(values):
    group = iota((1, LANES), 1) // CDOF
    row = jnp.full((1, LANES), values[0], jnp.int32)
    for i in range(1, 8):
        row = jnp.where(group == i, values[i], row)
    return row


def local_kernel(shape, group_size, place_ref, agg_ref, owner_ref, prolong_ref, fine_ref,
                 outer_ref, inner_ref, label_ref, rows_scr):
    bx, by, bz = shape
    rows_each = AGGS // group_size
    gx, gy, gz = place_ref[0], place_ref[1], place_ref[2]
    nx, ny, nz = agg_ref.shape
    owners = [owner_ref[0, 0, a] for a in range(AGGS)]
    ranks = []
    for a in range(AGGS):
        rank = jnp.int32(0)
        for b in range(a):
            rank += (owners[b] == owners[a]).astype(jnp.int32)
        ranks.append(rank)

    def look(table, index):
        value = table[0]
        for a in range(1, AGGS):
            value = jnp.where(index == a, table[a], value)
        return value

    def agg_at(x, y, z):
        px, py, pz = gx * bx + x, gy * by + y, gz * bz + z
        inside = (px >= 0) & (px < nx) & (py >= 0) & (py < ny) & (pz >= 0) & (pz < nz)
        cx = jnp.clip(px, 0, nx - 1)
        cy = jnp.clip(py, 0, ny - 1)
        cz = jnp.clip(pz, 0, nz - 1)
        return agg_ref[cx, cy, cz], inside

    own, owner_of, rank_of = {}, {}, {}
    for x in range(bx):
        for y in range(by):
            for z in range(bz):
                own[x, y, z] = agg_at(x, y, z)[0]
                owner_of[x, y, z] = look(owners, own[x, y, z])
                rank_of[x, y, z] = look(ranks, own[x, y, z])

    def outer_label(e, f, slots, extra):
        column, inside = agg_at(*f)
        label = owner_of[e] * slots + extra + column * AGGS + gz * rows_each + rank_of[e]
        return jnp.where(inside, label, -1)

    rows = []
    for face in range(1, 5):
        step = -1 if face % 2 else 1
        edge = 0 if face % 2 else 1
        values = []
        for side in range(2):
            for z in range(bz):
                e = (edge, side, z) if face < 3 else (side, edge, z)
                f = (e[0] + step, e[1], z) if face < 3 else (e[0], e[1] + step, z)
                values.append(outer_label(e, f, 8 * AGGS, 0))
        rows.append(lane_row(values))
    values = []
    for face in range(2):
        for x in range(bx):
            for y in range(by):
                z = 0 if face == 0 else bz - 1
                step = -1 if face == 0 else 1
                values.append(outer_label((x, y, z), (x, y, z + step), 16 * AGGS, face * 8 * AGGS))
    rows.append(lane_row(values))
    rows.append(jnp.full((3, LANES), -1, jnp.int32))
    label_ref[...] = jnp.concatenate(rows, axis=0).astype(F32)

    lane = iota((32, LANES), 1)
    sub = iota((32, LANES), 0) % 4
    p0, p1 = iota((LANES, LANES), 0), iota((LANES, LANES), 1)
    permute = ones_where((p0 % 4 == p1 % 4) & (p0 // 32 == p1 // 4 % 4) & (p0 // 4 % 8 == p1 // 16))
    wide_lane = iota((4, CDOF, 2 * LANES), 2) % LANES
    for xy in range(bx * by):
        raw = prolong_ref[xy]
        rolled = [raw] + [pltpu.roll(raw, 32 * m, 1) for m in range(1, 4)]
        stacked = []
        for tau in range(4):
            part = jnp.zeros_like(raw)
            for z in range(4):
                part = jnp.where((sub == z) & (lane // 32 == z), rolled[(z - tau) % 4], part)
            stacked.append(part)
        turned = jnp.concatenate(stacked, axis=0).T
        high, low = split(turned)
        left = dot(jnp.concatenate([high, low], axis=0), permute).astype(BF16)
        high, low = left[:LANES], left[LANES:]
        left = jnp.concatenate(
            [jnp.concatenate([high, high], axis=1), jnp.concatenate([low, jnp.zeros_like(low)], axis=1)],
            axis=0,
        )
        for first in range(0, 7, 2):
            slabs = [fine_ref[xy * 7 + k] for k in range(first, min(first + 2, 7))]
            halves = [split(slab) for slab in slabs]
            right = jnp.concatenate(
                [jnp.concatenate([h[i] for h in halves], axis=1) for i in range(2)], axis=0
            )
            width = right.shape[1]
            out = dot(left, right).reshape(2, 4, 2, CDOF, width)
            out = out[0] + out[1]
            q = jnp.where(wide_lane[:, :, :width] < DOF, out[:, 0], out[:, 1]).reshape(DOF, width)
            high, low = split(q)
            for i in range(len(slabs)):
                cut = slice(i * LANES, (i + 1) * LANES)
                rows_scr[xy * 7 + first + i] = jnp.concatenate([high[:, cut], low[:, cut]], axis=1)

    for side in range(2):
        outer_ref[side] = rows_scr[side * 7 + 1]
        outer_ref[2 + side] = rows_scr[(2 + side) * 7 + 2]
        outer_ref[4 + side] = rows_scr[2 * side * 7 + 3]
        outer_ref[6 + side] = rows_scr[(2 * side + 1) * 7 + 4]
    for xy in range(4):
        outer_ref[8, xy * CDOF : (xy + 1) * CDOF] = rows_scr[xy * 7 + 5, :CDOF]
        outer_ref[9, xy * CDOF : (xy + 1) * CDOF] = rows_scr[xy * 7 + 6, DOF - CDOF :]

    collapse = collapse_matrix()
    tools = scatter_tools()
    pieces, values = [], []
    for x in range(bx):
        for y in range(by):
            xy = x * by + y
            weights = prolong_weights(
                [prolong_ref[xy, pl.ds(z, 8, stride=4), :] for z in range(4)], collapse
            )
            slabs = [
                (xy * 7, 0, (x, y, 0)),
                (((1 - x) * by + y) * 7 + (2 if x else 1), 0, (1 - x, y, 0)),
                ((x * by + 1 - y) * 7 + (4 if y else 3), 0, (x, 1 - y, 0)),
                (xy * 7 + 5, -1, (x, y, 1)),
                (xy * 7 + 6, 1, (x, y, -1)),
            ]
            for index, shift, (ex, ey, ez) in slabs:
                pieces.append(diagonal(blocks_of(rows_scr[index], weights), shift))
                for z in range(bz):
                    if 0 <= z + ez < bz:
                        e = (ex, ey, z + ez)
                        values.append(
                            (owner_of[e] * AGGS + own[x, y, z]) * rows_each + rank_of[e]
                        )
                    else:
                        values.append(jnp.int32(-1))
    half = iota((CDOF, LANES), 1) < DOF
    total = jnp.zeros((8 * AGGS, 2 * LANES), F32)
    for i in range(0, len(pieces), 2):
        pack = jnp.where(half, pieces[i], pieces[i + 1])
        labels = lane_row(values[4 * i : 4 * i + 8])
        total += scatter(pack, labels, 0, 8 * AGGS, tools)
    inner_ref[...] = total


def outer_kernel(group_size, links, place_ref, outer_ref, inner_ref, label_ref, *refs):
    halos, sends = refs[:links], refs[links:]
    low_x, high_x, low_y, high_y = halos[:4]
    low_z, high_z = halos[4], halos[-1]
    gz = place_ref[2]
    collapse = collapse_matrix()

    def column(ref, xy):
        return [ref[xy, pl.ds(z, 8, stride=4), :] for z in range(4)]

    def layer(ref, z):
        return [ref[xy, pl.ds(z, 8, stride=4), :] for xy in range(4)]

    sources = [column(low_x, 2), column(low_x, 3), column(high_x, 0), column(high_x, 1),
               column(low_y, 1), column(low_y, 3), column(high_y, 0), column(high_y, 2),
               layer(low_z, 3), layer(high_z, 0)]
    half = iota((CDOF, LANES), 1) < DOF
    packs = []
    for i in range(0, 10, 2):
        pair = [
            diagonal(blocks_of(outer_ref[j], prolong_weights(sources[j], collapse)), 0)
            for j in (i, i + 1)
        ]
        packs.append(jnp.where(half, *pair))
    tail = jnp.concatenate(packs + [label_ref[...]], axis=0)
    count = 8 * AGGS // group_size
    for shift, send in enumerate(sends, 1):
        target = lax.rem(gz + shift, group_size)
        block = inner_ref[pl.ds(pl.multiple_of(target * count, count), count)]
        send[:count] = block[:, :LANES]
        send[count : 2 * count] = block[:, LANES:]
        send[2 * count :] = tail


def place_terms(out_ref, tail, gz, tools, add):
    labels = tail[5 * CDOF :].astype(jnp.int32)
    for k in range(5):
        rows = (16 if k == 4 else 8) * AGGS
        sums = scatter(tail[k * CDOF : (k + 1) * CDOF], labels[k : k + 1], gz * rows, rows, tools)
        for c in range(rows // 8):
            at = slice(((k + 1) * 8 + c) * 2 * LANES, ((k + 1) * 8 + c + 1) * 2 * LANES)
            value = sums[c * 8 : (c + 1) * 8]
            out_ref[:, at] = add[:, at] + value if add is not None else value


def own_kernel(group_size, place_ref, inner_ref, send_ref, out_ref):
    gz = place_ref[2]
    rows_each = AGGS // group_size
    count = 8 * AGGS // group_size
    place_terms(out_ref, send_ref[2 * count :], gz, scatter_tools(), None)
    mine = iota((AGGS, 2 * LANES), 0) // rows_each == gz
    block = inner_ref[pl.ds(pl.multiple_of(gz * count, count), count)]
    for c in range(AGGS):
        part = block[c * rows_each : (c + 1) * rows_each]
        part = jnp.concatenate([part] * group_size, axis=0)
        out_ref[:, c * 2 * LANES : (c + 1) * 2 * LANES] = jnp.where(mine, part, 0.0)


def final_kernel(group_size, place_ref, own_ref, *refs):
    received, out_ref = refs[:-1], refs[-1]
    gz = place_ref[2]
    rows_each = AGGS // group_size
    count = 8 * AGGS // group_size
    tools = scatter_tools()
    total = own_ref
    for shift, ref in enumerate(received, 1):
        brick = lax.rem(gz - shift + group_size, group_size)
        place_terms(out_ref, ref[2 * count :], gz, tools, total)
        theirs = iota((AGGS, LANES), 0) // rows_each == brick
        for c in range(AGGS):
            for h in range(2):
                part = ref[h * count + c * rows_each : h * count + (c + 1) * rows_each]
                part = jnp.concatenate([part] * group_size, axis=0)
                at = slice((2 * c + h) * LANES, (2 * c + h + 1) * LANES)
                out_ref[:, at] = jnp.where(theirs, part, total[:, at])
        total = out_ref


def rotation(count, step):
    return [(i, (i + step) % count) for i in range(count)]


def shards(fine_blocks, prolong, agg_map, owner_map):
    bx, by, bz = fine_blocks.shape[:3]
    group_size = lax.axis_size("gz")
    fine = fine_blocks.transpose(0, 1, 3, 2, 4).reshape(bx * by * 7, bz, 32, LANES)
    fine = fine.transpose(0, 2, 1, 3).reshape(bx * by * 7, 32 * bz, LANES)
    base = prolong.reshape(bx * by, bz, 8, LANES).transpose(0, 2, 1, 3).reshape(bx * by, 8 * bz, LANES)
    place = jnp.stack([lax.axis_index(axis) for axis in ("gx", "gy", "gz")]).astype(jnp.int32)
    halos = []
    for axis in ("gx", "gy", "gz"):
        count = lax.axis_size(axis)
        halos.append(lax.ppermute(base, axis, rotation(count, 1)))
        if axis != "gz" or count > 2:
            halos.append(lax.ppermute(base, axis, rotation(count, -1)))
    params = pltpu.CompilerParams(vmem_limit_bytes=32 * 1024 * 1024)
    shape = jax.ShapeDtypeStruct
    outer, inner, labels = pl.pallas_call(
        functools.partial(local_kernel, (bx, by, bz), group_size),
        out_shape=[shape((10, DOF, 2 * LANES), BF16), shape((8 * AGGS, 2 * LANES), F32), shape((8, LANES), F32)],
        in_specs=[SMEM, SMEM, SMEM, VMEM, VMEM],
        out_specs=[VMEM] * 3,
        scratch_shapes=[pltpu.VMEM((bx * by * 7, DOF, 2 * LANES), BF16)],
        compiler_params=params,
        cost_estimate=pl.CostEstimate(flops=int(2e9), bytes_accessed=int(4e6), transcendentals=0),
    )(place, agg_map, owner_map, base, fine)
    count = 8 * AGGS // group_size
    size = 2 * count + 5 * CDOF + 8
    sends = pl.pallas_call(
        functools.partial(outer_kernel, group_size, len(halos)),
        out_shape=[shape((size, LANES), F32)] * (group_size - 1),
        in_specs=[SMEM] + [VMEM] * (3 + len(halos)),
        out_specs=[VMEM] * (group_size - 1),
        compiler_params=params,
    )(place, outer, inner, labels, *halos)
    received = [
        lax.ppermute(send, "gz", rotation(group_size, shift)) for shift, send in enumerate(sends, 1)
    ]
    full = shape((AGGS, 7 * AGGS * CDOF * CDOF), F32)
    own = pl.pallas_call(
        functools.partial(own_kernel, group_size),
        out_shape=full,
        in_specs=[SMEM, VMEM, VMEM],
        out_specs=VMEM,
        compiler_params=params,
        cost_estimate=pl.CostEstimate(flops=int(1e9), bytes_accessed=int(2e6), transcendentals=0),
    )(place, inner, sends[0])
    out = pl.pallas_call(
        functools.partial(final_kernel, group_size),
        out_shape=full,
        in_specs=[SMEM, VMEM] + [VMEM] * (group_size - 1),
        out_specs=VMEM,
        compiler_params=params,
    )(place, own, *received)
    return out[None, None]


def solution(mesh):
    placed = (P("gx", "gy", "gz", None, None), P("gx", "gy", "gz", None), P(), P("gx", "gy", "gz"))
    return jax.shard_map(
        shards, mesh=mesh, in_specs=placed, out_specs=P("gx", "gy", "gz", None), check_vma=False
    )
```

```python
import functools

import jax
import jax.numpy as jnp
from jax import lax
from jax.experimental import pallas as pl
from jax.experimental.pallas import tpu as pltpu
from jax.sharding import PartitionSpec as P

DOF = 64
CDOF = 16
AGGS = 8
FACES = 7
LANES = 128
WIDE = 2 * LANES
F32 = jnp.float32
BF16 = jnp.bfloat16
VMEM = pl.BlockSpec(memory_space=pltpu.VMEM)
HBM = pl.BlockSpec(memory_space=pltpu.HBM)


def iota(shape, dim):
    return lax.broadcasted_iota(jnp.int32, shape, dim)


def dot(a, b):
    return lax.dot_general(a, b, (((1,), (0,)), ((), ())), preferred_element_type=F32)


def split(x):
    high = x.astype(BF16)
    return high, (x - high.astype(F32)).astype(BF16)


def ones_where(mask):
    return jnp.where(mask, 1.0, 0.0).astype(BF16)


def rows_of(parts):
    return jnp.concatenate(parts, axis=0)


def lanes_of(parts):
    return jnp.concatenate(parts, axis=1)


def column_picker():
    r, q = iota((WIDE, 32), 0), iota((WIDE, 32), 1)
    return ones_where(q == r // 8 % 8 * 4 + r // DOF)


def layer_picker(z):
    r, q = iota((WIDE, LANES), 0), iota((WIDE, LANES), 1)
    return ones_where(q == r // DOF * 32 + r // 8 % 8 * 4 + z)


def prolong_weights(picked):
    count = len(picked)
    keep = iota((WIDE, WIDE), 0) % 8 == iota((WIDE, WIDE), 1) // CDOF % 8
    kept = [jnp.where(keep, p, 0.0).astype(BF16) for p in picked]
    collapse = ones_where(iota((WIDE, LANES), 0) % CDOF == iota((WIDE, LANES), 1) % CDOF)
    spread = dot(rows_of(kept), collapse).reshape(count, 4, DOF, LANES)
    lane = iota((DOF, LANES), 1)
    slot = lane // CDOF % 4
    left = lane < DOF
    factors = []
    for c in range(count):
        full = spread[c, 0]
        for i in range(1, 4):
            full = jnp.where(slot == i, spread[c, i], full)
        high = full.astype(BF16).astype(F32)
        both = jnp.where(left, high, full - high).astype(BF16)
        first = jnp.where(left, high, 0.0).astype(BF16)
        factors.append(rows_of([both, both, first, first]))
    return factors


def blocks_of(rows, factor):
    out = dot(rows, factor)
    return out + pltpu.roll(out, DOF, 1)


def diagonal(product, shift):
    keep = iota((DOF, LANES), 0) // CDOF + shift == iota((DOF, LANES), 1) // CDOF % 4
    kept = jnp.where(keep, product, 0.0).reshape(4, CDOF, LANES)
    return (kept[0] + kept[1]) + (kept[2] + kept[3])


def flatten(packs):
    spread = ones_where(iota((LANES, WIDE), 0) % CDOF == iota((LANES, WIDE), 1) % CDOF)
    element = ones_where(iota((LANES, LANES), 0) // CDOF == iota((LANES, LANES), 1) // CDOF)
    row = ones_where(iota((WIDE, WIDE), 0) % CDOF == iota((WIDE, WIDE), 1) // CDOF)
    wide = [rows_of([part] * 8) * element for pack in packs for part in split(pack)]
    flat = dot(rows_of(wide), spread).astype(BF16)
    return [flat[i * WIDE : (i + 1) * WIDE] * row for i in range(len(packs))]


def choose(labels, base, count):
    return ones_where(iota((count, LANES), 0) + base == labels)


def local_kernel(shape, group_size, agg_hbm, owner_hbm, prolong_hbm, fine_hbm, outer_ref, inner_ref, label_ref,
                 agg_ref, owner_ref, prolong_ref, fine_ref, rows_scr, sems):
    bx, by, bz = shape
    columns = bx * by
    rows_each = AGGS // group_size
    copies = [
        pltpu.make_async_copy(prolong_hbm, prolong_ref, sems.at[0]),
        pltpu.make_async_copy(agg_hbm, agg_ref, sems.at[1]),
        pltpu.make_async_copy(owner_hbm, owner_ref, sems.at[2]),
    ]
    for i in range(columns):
        part = pl.ds(i * FACES, FACES)
        copies.append(pltpu.make_async_copy(fine_hbm.at[part], fine_ref.at[part], sems.at[3 + i]))
    for copy in copies:
        copy.start()
    gx, gy, gz = lax.axis_index("gx"), lax.axis_index("gy"), lax.axis_index("gz")
    nx, ny, nz = agg_ref.shape

    copies[0].wait()
    lane = iota((32, LANES), 1)
    sub = iota((32, LANES), 0) % 4
    p0, p1 = iota((LANES, LANES), 0), iota((LANES, LANES), 1)
    permute = ones_where((p0 % 4 == p1 % 4) & (p0 // 32 == p1 // 4 % 4) & (p0 // 4 % 8 == p1 // 16))
    turned = []
    for xy in range(columns):
        raw = prolong_ref[xy]
        rolled = [raw] + [pltpu.roll(raw, 32 * m, 1) for m in range(1, 4)]
        stacked = []
        for tau in range(4):
            part = jnp.zeros_like(raw)
            for z in range(4):
                part = jnp.where((sub == z) & (lane // 32 == z), rolled[(z - tau) % 4], part)
            stacked.append(part)
        turned += split(rows_of(stacked).T)
    lefts = dot(rows_of(turned), permute).astype(BF16)
    picked = dot(column_picker(), lanes_of([h for xy in range(columns) for h in split(prolong_ref[xy])]))
    factors = prolong_weights([picked[:, xy * WIDE : (xy + 1) * WIDE] for xy in range(columns)])

    wide_lane = iota((4, CDOF, WIDE), 2) % LANES
    for xy in range(columns):
        copies[3 + xy].wait()
        high = lefts[xy * WIDE : xy * WIDE + LANES]
        low = lefts[xy * WIDE + LANES : (xy + 1) * WIDE]
        left = rows_of([lanes_of([high, high]), lanes_of([low, jnp.zeros_like(low)])])
        for first in range(0, FACES, 2):
            count = min(2, FACES - first)
            width = count * LANES
            halves = [split(fine_ref[xy * FACES + first + i]) for i in range(count)]
            right = rows_of([lanes_of([h[i] for h in halves]) for i in range(2)])
            out = dot(left, right).reshape(2, 4, 2, CDOF, width)
            out = out[0] + out[1]
            q = jnp.where(wide_lane[:, :, :width] < DOF, out[:, 0], out[:, 1]).reshape(DOF, width)
            high_q, low_q = split(q)
            for i in range(count):
                cut = slice(i * LANES, (i + 1) * LANES)
                rows_scr[xy * FACES + first + i] = lanes_of([high_q[:, cut], low_q[:, cut]])

    for side in range(2):
        outer_ref[side] = rows_scr[side * FACES + 1]
        outer_ref[2 + side] = rows_scr[(2 + side) * FACES + 2]
        outer_ref[4 + side] = rows_scr[2 * side * FACES + 3]
        outer_ref[6 + side] = rows_scr[(2 * side + 1) * FACES + 4]
    for xy in range(columns):
        at = slice(xy * CDOF, (xy + 1) * CDOF)
        outer_ref[8, at] = rows_scr[xy * FACES + 5, :CDOF]
        outer_ref[9, at] = rows_scr[xy * FACES + 6, DOF - CDOF :]

    copies[1].wait()
    copies[2].wait()
    aggs = (agg_ref[...] + 1).reshape(nx * ny, nz).astype(F32).astype(BF16)
    width = 5 * LANES
    z_row, z_lane = iota((nz, width), 0), iota((nz, width), 1)
    kind, place = z_lane // LANES, z_lane % LANES
    slot, face = place // CDOF % 4, place // DOF
    z_off = jnp.where(kind == 0, slot, jnp.where(kind == 1, slot + 1, slot - 1))
    z_off = jnp.where(kind == 3, face * (bz - 1), jnp.where(kind == 4, face * (bz + 1) - 1, z_off))
    by_lane = dot(aggs, ones_where(z_row == gz * bz + z_off)).astype(BF16)
    count = 24
    r = iota((count, nx * ny), 0)
    own_x, own_y = r // 2 % 2, r % 2
    group = r // 4
    dx = jnp.where(group == 1, 1 - own_x, own_x)
    dy = jnp.where(group == 2, 1 - own_y, own_y)
    dx = jnp.where(group == 4, own_x * (bx + 1) - 1, jnp.where(group == 5, own_y, dx))
    dy = jnp.where(group == 4, own_y, jnp.where(group == 5, own_x * (by + 1) - 1, dy))
    px, py = gx * bx + dx, gy * by + dy
    inside = (px >= 0) & (px < nx) & (py >= 0) & (py < ny) & (group != 3)
    at = jnp.where(inside, px * ny + py, -1)
    table = dot(ones_where(iota((count, nx * ny), 1) == at), by_lane).astype(jnp.int32)
    owners = owner_ref[0]
    slots = iota((1, AGGS), 1)
    rank = jnp.zeros((1, AGGS), jnp.int32)
    for a in range(AGGS - 1):
        rank += jnp.where((slots > a) & (owners == owners[:, a : a + 1]), 1, 0)
    own = table[:16]
    owner = jnp.zeros_like(own)
    ranks = jnp.zeros_like(own)
    for a in range(AGGS):
        owner = jnp.where(own == a + 1, owners[:, a : a + 1], owner)
        ranks = jnp.where(own == a + 1, rank[:, a : a + 1], ranks)
    inner_base = owner * (AGGS * rows_each) + ranks
    outer_base = owner * (AGGS * AGGS) + gz * rows_each + ranks

    def cut(array, row, part):
        return array[row : row + 1, part * LANES : (part + 1) * LANES]

    first_half = iota((1, LANES), 1) < DOF
    level = iota((1, LANES), 1) // CDOF % 4

    def pair(array, one, two, part=0):
        return jnp.where(first_half, cut(array, one, part), cut(array, two, part))

    labels = []
    for row, part, valid in ((0, 0, None), (4, 0, None), (8, 0, None), (0, 1, level < bz - 1), (0, 2, level > 0)):
        for x in range(bx):
            label = pair(inner_base, row + 2 * x, row + 2 * x + 1, part)
            label += (pair(table, 2 * x, 2 * x + 1) - 1) * rows_each
            labels.append(label if valid is None else jnp.where(valid, label, -1))
    outer_labels = []
    for k, pick in enumerate(((0, 1), (2, 3), (0, 2), (1, 3))):
        other = pair(table, 16 + 2 * k, 17 + 2 * k)
        label = pair(outer_base, *pick) + (other - 1) * AGGS
        outer_labels.append(jnp.where(other > 0, label, -1))

    def by_column(array, part):
        value = cut(array, 0, part)
        for xy in range(1, columns):
            value = jnp.where(level == xy, cut(array, xy, part), value)
        return value

    other = by_column(table, 4)
    label = by_column(outer_base + owner * (AGGS * AGGS), 3) + (other - 1) * AGGS
    label += jnp.where(first_half, 0, AGGS * AGGS)
    outer_labels.append(jnp.where(other > 0, label, -1))
    label_ref[...] = rows_of(outer_labels + [jnp.full((3, LANES), -1, jnp.int32)]).astype(F32)

    pieces = [[] for _ in range(5)]
    for x in range(bx):
        for y in range(by):
            xy = x * by + y
            sources = (
                (xy * FACES, 0),
                (((1 - x) * by + y) * FACES + (2 if x else 1), 0),
                ((x * by + 1 - y) * FACES + (4 if y else 3), 0),
                (xy * FACES + 5, -1),
                (xy * FACES + 6, 1),
            )
            product = blocks_of(rows_of([rows_scr[index] for index, _ in sources]), factors[xy])
            for i, (_, shift) in enumerate(sources):
                pieces[i].append(diagonal(product[i * DOF : (i + 1) * DOF], shift))
    half = iota((CDOF, LANES), 1) < DOF
    packs = [jnp.where(half, p[2 * x], p[2 * x + 1]) for p in pieces for x in range(bx)]
    flat = flatten(packs)
    chosen = [choose(label, 0, AGGS * AGGS) for label in labels]
    inner_ref[...] = dot(lanes_of([c for c in chosen for _ in range(2)]), rows_of(flat))


def outer_kernel(group_size, links, outer_ref, inner_ref, label_ref, *refs):
    halos, sends = refs[:links], refs[links:]
    low_x, high_x, low_y, high_y = halos[:4]
    low_z, high_z = halos[4], halos[-1]
    gz = lax.axis_index("gz")
    sources = ((low_x, 2), (low_x, 3), (high_x, 0), (high_x, 1), (low_y, 1), (low_y, 3), (high_y, 0), (high_y, 2))
    picked = dot(column_picker(), lanes_of([h for ref, xy in sources for h in split(ref[xy])]))
    picked = [picked[:, i * WIDE : (i + 1) * WIDE] for i in range(len(sources))]
    for ref, z in ((low_z, 3), (high_z, 0)):
        picked.append(dot(layer_picker(z), lanes_of(split(ref[...].reshape(LANES, LANES)))))
    factors = prolong_weights(picked)
    pieces = [diagonal(blocks_of(outer_ref[i], factors[i]), 0) for i in range(len(factors))]
    half = iota((CDOF, LANES), 1) < DOF
    packs = [jnp.where(half, pieces[i], pieces[i + 1]) for i in range(0, len(pieces), 2)]
    tail = rows_of(packs + [label_ref[...]])
    count = AGGS * AGGS // group_size
    for shift, send in enumerate(sends, 1):
        target = lax.rem(gz + shift, group_size)
        block = inner_ref[pl.ds(pl.multiple_of(target * count, count), count)]
        send[:count] = block[:, :LANES]
        send[count : 2 * count] = block[:, LANES:]
        send[2 * count :] = tail


def outer_sums(tails, gz):
    count = len(tails)
    packs = [tail[k * CDOF : (k + 1) * CDOF] for k in range(5) for tail in tails]
    flat = flatten(packs)
    labels = [tail[5 * CDOF :].astype(jnp.int32) for tail in tails]
    sums = []
    for k in range(5):
        rows = (2 if k == 4 else 1) * AGGS * AGGS
        chosen = [choose(label[k : k + 1], gz * rows, rows) for label in labels for _ in range(2)]
        sums.append(dot(lanes_of(chosen), rows_of(flat[k * count : (k + 1) * count])))
    return sums


def own_kernel(group_size, inner_ref, send_ref, out_ref):
    gz = lax.axis_index("gz")
    rows_each = AGGS // group_size
    count = AGGS * AGGS // group_size
    mine = iota((AGGS, WIDE), 0) // rows_each == gz
    block = inner_ref[pl.ds(pl.multiple_of(gz * count, count), count)]
    for c in range(AGGS):
        part = rows_of([block[c * rows_each : (c + 1) * rows_each]] * group_size)
        out_ref[:, c * WIDE : (c + 1) * WIDE] = jnp.where(mine, part, 0.0)
    at = AGGS
    for value in outer_sums([send_ref[2 * count :]], gz):
        for c in range(value.shape[0] // AGGS):
            out_ref[:, at * WIDE : (at + 1) * WIDE] = value[c * AGGS : (c + 1) * AGGS]
            at += 1


def final_kernel(group_size, own_ref, *refs):
    received, out_hbm, out_ref, sems = refs[:-3], refs[-3], refs[-2], refs[-1]
    gz = lax.axis_index("gz")
    rows_each = AGGS // group_size
    count = AGGS * AGGS // group_size
    copies = []

    def send_out(face):
        part = pl.ds(face * AGGS * WIDE, AGGS * WIDE)
        copies.append(pltpu.make_async_copy(out_ref.at[:, part], out_hbm.at[:, part], sems.at[face]))
        copies[-1].start()

    brick = iota((AGGS, LANES), 0) // rows_each
    for c in range(AGGS):
        for h in range(2):
            at = slice((2 * c + h) * LANES, (2 * c + h + 1) * LANES)
            value = own_ref[:, at]
            for shift, ref in enumerate(received, 1):
                part = ref[h * count + c * rows_each : h * count + (c + 1) * rows_each]
                theirs = lax.rem(gz - shift + group_size, group_size)
                value = jnp.where(brick == theirs, rows_of([part] * group_size), value)
            out_ref[:, at] = value
    send_out(0)
    at = AGGS
    for value in outer_sums([ref[2 * count :] for ref in received], gz):
        for c in range(value.shape[0] // AGGS):
            cut = slice(at * WIDE, (at + 1) * WIDE)
            out_ref[:, cut] = own_ref[:, cut] + value[c * AGGS : (c + 1) * AGGS]
            at += 1
            if at % AGGS == 0:
                send_out(at // AGGS - 1)
    for copy in copies:
        copy.wait()


def rotation(count, step):
    return [(i, (i + step) % count) for i in range(count)]


def shards(fine_blocks, prolong, agg_map, owner_map):
    bx, by, bz = fine_blocks.shape[:3]
    columns = bx * by
    group_size = lax.axis_size("gz")
    fine = fine_blocks.transpose(0, 1, 3, 2, 4).reshape(columns * FACES, bz, 32, LANES)
    fine = fine.transpose(0, 2, 1, 3).reshape(columns * FACES, 32 * bz, LANES)
    base = prolong.reshape(columns, bz, 8, LANES).transpose(0, 2, 1, 3).reshape(columns, 8 * bz, LANES)
    halos = []
    for axis in ("gx", "gy", "gz"):
        count = lax.axis_size(axis)
        halos.append(lax.ppermute(base, axis, rotation(count, 1)))
        if axis != "gz" or count > 2:
            halos.append(lax.ppermute(base, axis, rotation(count, -1)))
    params = pltpu.CompilerParams(vmem_limit_bytes=32 * 1024 * 1024)
    shape = jax.ShapeDtypeStruct
    outer, inner, labels = pl.pallas_call(
        functools.partial(local_kernel, (bx, by, bz), group_size),
        out_shape=[shape((10, DOF, WIDE), BF16), shape((AGGS * AGGS, WIDE), F32), shape((8, LANES), F32)],
        in_specs=[HBM] * 4,
        out_specs=[VMEM] * 3,
        scratch_shapes=[
            pltpu.VMEM(agg_map.shape, jnp.int32),
            pltpu.VMEM(owner_map.shape, jnp.int32),
            pltpu.VMEM(base.shape, F32),
            pltpu.VMEM(fine.shape, F32),
            pltpu.VMEM((columns * FACES, DOF, WIDE), BF16),
            pltpu.SemaphoreType.DMA((3 + columns,)),
        ],
        compiler_params=params,
        cost_estimate=pl.CostEstimate(flops=int(2e9), bytes_accessed=int(4e6), transcendentals=0),
    )(*(pltpu.with_memory_space_constraint(a, pltpu.HBM) for a in (agg_map, owner_map, base, fine)))
    size = 2 * AGGS * AGGS // group_size + 5 * CDOF + 8
    sends = pl.pallas_call(
        functools.partial(outer_kernel, group_size, len(halos)),
        out_shape=[shape((size, LANES), F32)] * (group_size - 1),
        in_specs=[VMEM] * (3 + len(halos)),
        out_specs=[VMEM] * (group_size - 1),
        compiler_params=params,
    )(outer, inner, labels, *halos)
    received = [
        lax.ppermute(send, "gz", rotation(group_size, shift)) for shift, send in enumerate(sends, 1)
    ]
    full = shape((AGGS, FACES * AGGS * CDOF * CDOF), F32)
    own = pl.pallas_call(
        functools.partial(own_kernel, group_size),
        out_shape=full,
        in_specs=[VMEM, VMEM],
        out_specs=VMEM,
        compiler_params=params,
        cost_estimate=pl.CostEstimate(flops=int(1e9), bytes_accessed=int(2e6), transcendentals=0),
    )(inner, sends[0])
    out = pl.pallas_call(
        functools.partial(final_kernel, group_size),
        out_shape=full,
        in_specs=[VMEM] * group_size,
        out_specs=HBM,
        scratch_shapes=[pltpu.VMEM(full.shape, F32), pltpu.SemaphoreType.DMA((FACES,))],
        compiler_params=params,
    )(own, *received)
    return out[None, None]


def solution(mesh):
    placed = (P("gx", "gy", "gz", None, None), P("gx", "gy", "gz", None), P(), P("gx", "gy", "gz"))
    return jax.shard_map(
        shards, mesh=mesh, in_specs=placed, out_specs=P("gx", "gy", "gz", None), check_vma=False
    )
```

```python
import functools

import jax
import jax.numpy as jnp
from jax import lax
from jax.experimental import pallas as pl
from jax.experimental.pallas import tpu as pltpu
from jax.sharding import PartitionSpec as P

DOF = 64
CDOF = 16
AGGS = 8
FACES = 7
LANES = 128
WIDE = 2 * LANES
F32 = jnp.float32
BF16 = jnp.bfloat16
VMEM = pl.BlockSpec(memory_space=pltpu.VMEM)
HBM = pl.BlockSpec(memory_space=pltpu.HBM)


def iota(shape, dim):
    return lax.broadcasted_iota(jnp.int32, shape, dim)


def dot(a, b):
    return lax.dot_general(a, b, (((1,), (0,)), ((), ())), preferred_element_type=F32)


def split(x):
    high = x.astype(BF16)
    return high, (x - high.astype(F32)).astype(BF16)


def ones_where(mask):
    return jnp.where(mask, 1.0, 0.0).astype(BF16)


def rows_of(parts):
    return jnp.concatenate(parts, axis=0)


def lanes_of(parts):
    return jnp.concatenate(parts, axis=1)


def column_picker():
    r, q = iota((WIDE, 32), 0), iota((WIDE, 32), 1)
    return ones_where(q == r // 8 % 8 * 4 + r // DOF)


def layer_picker(z):
    r, q = iota((WIDE, LANES), 0), iota((WIDE, LANES), 1)
    return ones_where(q == r // DOF * 32 + r // 8 % 8 * 4 + z)


def prolong_weights(picked):
    count = len(picked)
    keep = iota((WIDE, WIDE), 0) % 8 == iota((WIDE, WIDE), 1) // CDOF % 8
    kept = [jnp.where(keep, p, 0.0).astype(BF16) for p in picked]
    collapse = ones_where(iota((WIDE, LANES), 0) % CDOF == iota((WIDE, LANES), 1) % CDOF)
    spread = dot(rows_of(kept), collapse).reshape(count, 4, DOF, LANES)
    lane = iota((DOF, LANES), 1)
    slot = lane // CDOF % 4
    left = lane < DOF
    factors = []
    for c in range(count):
        full = spread[c, 0]
        for i in range(1, 4):
            full = jnp.where(slot == i, spread[c, i], full)
        high = full.astype(BF16).astype(F32)
        both = jnp.where(left, high, full - high).astype(BF16)
        first = jnp.where(left, high, 0.0).astype(BF16)
        factors.append(rows_of([both, both, first, first]))
    return factors


def blocks_of(rows, factor):
    out = dot(rows, factor)
    return out + pltpu.roll(out, DOF, 1)


def diagonal(product, shift):
    keep = iota((DOF, LANES), 0) // CDOF + shift == iota((DOF, LANES), 1) // CDOF % 4
    kept = jnp.where(keep, product, 0.0).reshape(4, CDOF, LANES)
    return (kept[0] + kept[1]) + (kept[2] + kept[3])


def flatten(packs):
    spread = ones_where(iota((LANES, WIDE), 0) % CDOF == iota((LANES, WIDE), 1) % CDOF)
    element = ones_where(iota((LANES, LANES), 0) // CDOF == iota((LANES, LANES), 1) // CDOF)
    row = ones_where(iota((WIDE, WIDE), 0) % CDOF == iota((WIDE, WIDE), 1) // CDOF)
    wide = [rows_of([part] * 8) * element for pack in packs for part in split(pack)]
    flat = dot(rows_of(wide), spread).astype(BF16)
    return [flat[i * WIDE : (i + 1) * WIDE] * row for i in range(len(packs))]


def choose(labels, base, count):
    return ones_where(iota((count, LANES), 0) + base == labels)


def tick_kernel(out_ref):
    out_ref[...] = jnp.ones(out_ref.shape, F32)


def local_kernel(shape, group_size, agg_hbm, owner_hbm, prolong_ref, fine_ref, tick_ref, outer_ref, inner_ref, label_ref,
                 agg_ref, owner_ref, rows_scr, sems):
    bx, by, bz = shape
    columns = bx * by
    rows_each = AGGS // group_size
    copies = [
        pltpu.make_async_copy(agg_hbm, agg_ref, sems.at[0]),
        pltpu.make_async_copy(owner_hbm, owner_ref, sems.at[1]),
    ]
    for copy in copies:
        copy.start()
    gx, gy, gz = lax.axis_index("gx"), lax.axis_index("gy"), lax.axis_index("gz")
    nx, ny, nz = agg_ref.shape

    lane = iota((32, LANES), 1)
    sub = iota((32, LANES), 0) % 4
    p0, p1 = iota((LANES, LANES), 0), iota((LANES, LANES), 1)
    permute = ones_where((p0 % 4 == p1 % 4) & (p0 // 32 == p1 // 4 % 4) & (p0 // 4 % 8 == p1 // 16))
    turned = []
    for xy in range(columns):
        raw = prolong_ref[xy]
        rolled = [raw] + [pltpu.roll(raw, 32 * m, 1) for m in range(1, 4)]
        stacked = []
        for tau in range(4):
            part = jnp.zeros_like(raw)
            for z in range(4):
                part = jnp.where((sub == z) & (lane // 32 == z), rolled[(z - tau) % 4], part)
            stacked.append(part)
        turned += split(rows_of(stacked).T)
    lefts = dot(rows_of(turned), permute).astype(BF16)
    picked = dot(column_picker(), lanes_of([h for xy in range(columns) for h in split(prolong_ref[xy])]))
    factors = prolong_weights([picked[:, xy * WIDE : (xy + 1) * WIDE] for xy in range(columns)])

    wide_lane = iota((4, CDOF, WIDE), 2) % LANES
    for xy in range(columns):
        high = lefts[xy * WIDE : xy * WIDE + LANES]
        low = lefts[xy * WIDE + LANES : (xy + 1) * WIDE]
        left = rows_of([lanes_of([high, high]), lanes_of([low, jnp.zeros_like(low)])])
        for first in range(0, FACES, 2):
            count = min(2, FACES - first)
            width = count * LANES
            halves = [split(fine_ref[xy * FACES + first + i]) for i in range(count)]
            right = rows_of([lanes_of([h[i] for h in halves]) for i in range(2)])
            out = dot(left, right).reshape(2, 4, 2, CDOF, width)
            out = out[0] + out[1]
            q = jnp.where(wide_lane[:, :, :width] < DOF, out[:, 0], out[:, 1]).reshape(DOF, width)
            high_q, low_q = split(q)
            for i in range(count):
                cut = slice(i * LANES, (i + 1) * LANES)
                rows_scr[xy * FACES + first + i] = lanes_of([high_q[:, cut], low_q[:, cut]])

    for side in range(2):
        outer_ref[side] = rows_scr[side * FACES + 1]
        outer_ref[2 + side] = rows_scr[(2 + side) * FACES + 2]
        outer_ref[4 + side] = rows_scr[2 * side * FACES + 3]
        outer_ref[6 + side] = rows_scr[(2 * side + 1) * FACES + 4]
    for xy in range(columns):
        at = slice(xy * CDOF, (xy + 1) * CDOF)
        outer_ref[8, at] = rows_scr[xy * FACES + 5, :CDOF]
        outer_ref[9, at] = rows_scr[xy * FACES + 6, DOF - CDOF :]

    copies[0].wait()
    copies[1].wait()
    aggs = (agg_ref[...] + 1).reshape(nx * ny, nz).astype(F32).astype(BF16)
    width = 5 * LANES
    z_row, z_lane = iota((nz, width), 0), iota((nz, width), 1)
    kind, place = z_lane // LANES, z_lane % LANES
    slot, face = place // CDOF % 4, place // DOF
    z_off = jnp.where(kind == 0, slot, jnp.where(kind == 1, slot + 1, slot - 1))
    z_off = jnp.where(kind == 3, face * (bz - 1), jnp.where(kind == 4, face * (bz + 1) - 1, z_off))
    by_lane = dot(aggs, ones_where(z_row == gz * bz + z_off)).astype(BF16)
    count = 24
    r = iota((count, nx * ny), 0)
    own_x, own_y = r // 2 % 2, r % 2
    group = r // 4
    dx = jnp.where(group == 1, 1 - own_x, own_x)
    dy = jnp.where(group == 2, 1 - own_y, own_y)
    dx = jnp.where(group == 4, own_x * (bx + 1) - 1, jnp.where(group == 5, own_y, dx))
    dy = jnp.where(group == 4, own_y, jnp.where(group == 5, own_x * (by + 1) - 1, dy))
    px, py = gx * bx + dx, gy * by + dy
    inside = (px >= 0) & (px < nx) & (py >= 0) & (py < ny) & (group != 3)
    at = jnp.where(inside, px * ny + py, -1)
    table = dot(ones_where(iota((count, nx * ny), 1) == at), by_lane).astype(jnp.int32)
    owners = owner_ref[0]
    slots = iota((1, AGGS), 1)
    rank = jnp.zeros((1, AGGS), jnp.int32)
    for a in range(AGGS - 1):
        rank += jnp.where((slots > a) & (owners == owners[:, a : a + 1]), 1, 0)
    own = table[:16]
    owner = jnp.zeros_like(own)
    ranks = jnp.zeros_like(own)
    for a in range(AGGS):
        owner = jnp.where(own == a + 1, owners[:, a : a + 1], owner)
        ranks = jnp.where(own == a + 1, rank[:, a : a + 1], ranks)
    inner_base = owner * (AGGS * rows_each) + ranks
    outer_base = owner * (AGGS * AGGS) + gz * rows_each + ranks

    def cut(array, row, part):
        return array[row : row + 1, part * LANES : (part + 1) * LANES]

    first_half = iota((1, LANES), 1) < DOF
    level = iota((1, LANES), 1) // CDOF % 4

    def pair(array, one, two, part=0):
        return jnp.where(first_half, cut(array, one, part), cut(array, two, part))

    labels = []
    for row, part, valid in ((0, 0, None), (4, 0, None), (8, 0, None), (0, 1, level < bz - 1), (0, 2, level > 0)):
        for x in range(bx):
            label = pair(inner_base, row + 2 * x, row + 2 * x + 1, part)
            label += (pair(table, 2 * x, 2 * x + 1) - 1) * rows_each
            labels.append(label if valid is None else jnp.where(valid, label, -1))
    outer_labels = []
    for k, pick in enumerate(((0, 1), (2, 3), (0, 2), (1, 3))):
        other = pair(table, 16 + 2 * k, 17 + 2 * k)
        label = pair(outer_base, *pick) + (other - 1) * AGGS
        outer_labels.append(jnp.where(other > 0, label, -1))

    def by_column(array, part):
        value = cut(array, 0, part)
        for xy in range(1, columns):
            value = jnp.where(level == xy, cut(array, xy, part), value)
        return value

    other = by_column(table, 4)
    label = by_column(outer_base + owner * (AGGS * AGGS), 3) + (other - 1) * AGGS
    label += jnp.where(first_half, 0, AGGS * AGGS)
    outer_labels.append(jnp.where(other > 0, label, -1))
    label_ref[...] = rows_of(outer_labels + [jnp.full((3, LANES), -1, jnp.int32)]).astype(F32)

    pieces = [[] for _ in range(5)]
    for x in range(bx):
        for y in range(by):
            xy = x * by + y
            sources = (
                (xy * FACES, 0),
                (((1 - x) * by + y) * FACES + (2 if x else 1), 0),
                ((x * by + 1 - y) * FACES + (4 if y else 3), 0),
                (xy * FACES + 5, -1),
                (xy * FACES + 6, 1),
            )
            product = blocks_of(rows_of([rows_scr[index] for index, _ in sources]), factors[xy])
            for i, (_, shift) in enumerate(sources):
                pieces[i].append(diagonal(product[i * DOF : (i + 1) * DOF], shift))
    half = iota((CDOF, LANES), 1) < DOF
    packs = [jnp.where(half, p[2 * x], p[2 * x + 1]) for p in pieces for x in range(bx)]
    flat = flatten(packs)
    chosen = [choose(label, 0, AGGS * AGGS) for label in labels]
    inner_ref[...] = dot(lanes_of([c for c in chosen for _ in range(2)]), rows_of(flat))


def outer_kernel(group_size, links, outer_ref, inner_ref, label_ref, *refs):
    halos, sends = refs[:links], refs[links:]
    low_z, high_z = halos[4], halos[-1]
    gz = lax.axis_index("gz")
    values = []
    for axis, (even, odd), low, high in (("gx", halos[:2], (2, 3), (0, 1)), ("gy", halos[2:4], (1, 3), (0, 2))):
        second = lax.rem(lax.axis_index(axis), 2) == 1
        values += [jnp.where(second, even[xy], odd[xy]) for xy in low]
        values += [jnp.where(second, odd[xy], even[xy]) for xy in high]
    picked = dot(column_picker(), lanes_of([h for value in values for h in split(value)]))
    picked = [picked[:, i * WIDE : (i + 1) * WIDE] for i in range(len(values))]
    for ref, z in ((low_z, 3), (high_z, 0)):
        picked.append(dot(layer_picker(z), lanes_of(split(ref[...].reshape(LANES, LANES)))))
    factors = prolong_weights(picked)
    pieces = [diagonal(blocks_of(outer_ref[i], factors[i]), 0) for i in range(len(factors))]
    half = iota((CDOF, LANES), 1) < DOF
    packs = [jnp.where(half, pieces[i], pieces[i + 1]) for i in range(0, len(pieces), 2)]
    tail = rows_of(packs + [label_ref[...]])
    count = AGGS * AGGS // group_size
    for shift, send in enumerate(sends, 1):
        target = lax.rem(gz + shift, group_size)
        block = inner_ref[pl.ds(pl.multiple_of(target * count, count), count)]
        send[:count] = block[:, :LANES]
        send[count : 2 * count] = block[:, LANES:]
        send[2 * count :] = tail


def outer_sums(tails, gz):
    count = len(tails)
    packs = [tail[k * CDOF : (k + 1) * CDOF] for k in range(5) for tail in tails]
    flat = flatten(packs)
    labels = [tail[5 * CDOF :].astype(jnp.int32) for tail in tails]
    sums = []
    for k in range(5):
        rows = (2 if k == 4 else 1) * AGGS * AGGS
        chosen = [choose(label[k : k + 1], gz * rows, rows) for label in labels for _ in range(2)]
        sums.append(dot(lanes_of(chosen), rows_of(flat[k * count : (k + 1) * count])))
    return sums


def own_kernel(group_size, inner_ref, send_ref, out_ref):
    gz = lax.axis_index("gz")
    rows_each = AGGS // group_size
    count = AGGS * AGGS // group_size
    mine = iota((AGGS, WIDE), 0) // rows_each == gz
    block = inner_ref[pl.ds(pl.multiple_of(gz * count, count), count)]
    for c in range(AGGS):
        part = rows_of([block[c * rows_each : (c + 1) * rows_each]] * group_size)
        out_ref[:, c * WIDE : (c + 1) * WIDE] = jnp.where(mine, part, 0.0)
    at = AGGS
    for value in outer_sums([send_ref[2 * count :]], gz):
        for c in range(value.shape[0] // AGGS):
            out_ref[:, at * WIDE : (at + 1) * WIDE] = value[c * AGGS : (c + 1) * AGGS]
            at += 1


def final_kernel(group_size, own_ref, *refs):
    received, out_hbm, out_ref, sems = refs[:-3], refs[-3], refs[-2], refs[-1]
    gz = lax.axis_index("gz")
    rows_each = AGGS // group_size
    count = AGGS * AGGS // group_size
    copies = []

    def send_out(face):
        part = pl.ds(face * AGGS * WIDE, AGGS * WIDE)
        copies.append(pltpu.make_async_copy(out_ref.at[:, part], out_hbm.at[:, part], sems.at[face]))
        copies[-1].start()

    brick = iota((AGGS, LANES), 0) // rows_each
    for c in range(AGGS):
        for h in range(2):
            at = slice((2 * c + h) * LANES, (2 * c + h + 1) * LANES)
            value = own_ref[:, at]
            for shift, ref in enumerate(received, 1):
                part = ref[h * count + c * rows_each : h * count + (c + 1) * rows_each]
                theirs = lax.rem(gz - shift + group_size, group_size)
                value = jnp.where(brick == theirs, rows_of([part] * group_size), value)
            out_ref[:, at] = value
    send_out(0)
    at = AGGS
    for value in outer_sums([ref[2 * count :] for ref in received], gz):
        for c in range(value.shape[0] // AGGS):
            cut = slice(at * WIDE, (at + 1) * WIDE)
            out_ref[:, cut] = own_ref[:, cut] + value[c * AGGS : (c + 1) * AGGS]
            at += 1
            if at % AGGS == 0:
                send_out(at // AGGS - 1)
    for copy in copies:
        copy.wait()


def matching(sizes, along, first):
    def partner(place):
        i = (place[along] - first) ^ 1
        moved = list(place)
        if 0 <= i + first < sizes[along] and place[along] >= first:
            moved[along] = i + first
        elif place[1 - along] ^ 1 < sizes[1 - along]:
            moved[1 - along] = place[1 - along] ^ 1
        return moved[0] * sizes[1] + moved[1]

    return [(x * sizes[1] + y, partner((x, y))) for x in range(sizes[0]) for y in range(sizes[1])]


def rotation(count, step):
    return [(i, (i + step) % count) for i in range(count)]


def shards(fine_blocks, prolong, agg_map, owner_map):
    bx, by, bz = fine_blocks.shape[:3]
    columns = bx * by
    group_size = lax.axis_size("gz")
    fine = fine_blocks.transpose(0, 1, 3, 2, 4).reshape(columns * FACES, bz, 32, LANES)
    fine = fine.transpose(0, 2, 1, 3).reshape(columns * FACES, 32 * bz, LANES)
    base = prolong.reshape(columns, bz, 8, LANES).transpose(0, 2, 1, 3).reshape(columns, 8 * bz, LANES)
    tick = pl.pallas_call(
        tick_kernel,
        out_shape=pltpu.VMEM((8, LANES), F32),
        out_specs=VMEM,
        cost_estimate=pl.CostEstimate(flops=int(5e9), bytes_accessed=int(5e7), transcendentals=0),
    )()
    sizes = lax.axis_size("gx"), lax.axis_size("gy")
    layers = [lax.ppermute(base, "gz", rotation(group_size, step)) for step in ((1, -1) if group_size > 2 else (1,))]
    halos = [
        lax.ppermute(base, ("gx", "gy"), matching(sizes, along, first)) for along in range(2) for first in range(2)
    ] + layers
    params = pltpu.CompilerParams(vmem_limit_bytes=32 * 1024 * 1024)
    shape = jax.ShapeDtypeStruct
    outer, inner, labels = pl.pallas_call(
        functools.partial(local_kernel, (bx, by, bz), group_size),
        out_shape=[shape((10, DOF, WIDE), BF16), shape((AGGS * AGGS, WIDE), F32), shape((8, LANES), F32)],
        in_specs=[HBM] * 2 + [VMEM] * 3,
        out_specs=[VMEM] * 3,
        scratch_shapes=[
            pltpu.VMEM(agg_map.shape, jnp.int32),
            pltpu.VMEM(owner_map.shape, jnp.int32),
            pltpu.VMEM((columns * FACES, DOF, WIDE), BF16),
            pltpu.SemaphoreType.DMA((2,)),
        ],
        compiler_params=params,
        cost_estimate=pl.CostEstimate(flops=int(2e9), bytes_accessed=int(4e6), transcendentals=0),
    )(
        *(pltpu.with_memory_space_constraint(a, pltpu.HBM) for a in (agg_map, owner_map)),
        *(pltpu.with_memory_space_constraint(a, pltpu.VMEM) for a in (base, fine)),
        tick,
    )
    size = 2 * AGGS * AGGS // group_size + 5 * CDOF + 8
    sends = pl.pallas_call(
        functools.partial(outer_kernel, group_size, len(halos)),
        out_shape=[shape((size, LANES), F32)] * (group_size - 1),
        in_specs=[VMEM] * (3 + len(halos)),
        out_specs=[VMEM] * (group_size - 1),
        compiler_params=params,
    )(outer, inner, labels, *halos)
    received = [
        lax.ppermute(send, "gz", rotation(group_size, shift)) for shift, send in enumerate(sends, 1)
    ]
    full = shape((AGGS, FACES * AGGS * CDOF * CDOF), F32)
    own = pl.pallas_call(
        functools.partial(own_kernel, group_size),
        out_shape=full,
        in_specs=[VMEM, VMEM],
        out_specs=VMEM,
        compiler_params=params,
        cost_estimate=pl.CostEstimate(flops=int(1e9), bytes_accessed=int(2e6), transcendentals=0),
    )(inner, sends[0])
    out = pl.pallas_call(
        functools.partial(final_kernel, group_size),
        out_shape=full,
        in_specs=[VMEM] * group_size,
        out_specs=HBM,
        scratch_shapes=[pltpu.VMEM(full.shape, F32), pltpu.SemaphoreType.DMA((FACES,))],
        compiler_params=params,
    )(own, *received)
    return out[None, None]


def solution(mesh):
    placed = (P("gx", "gy", "gz", None, None), P("gx", "gy", "gz", None), P(), P("gx", "gy", "gz"))
    return jax.shard_map(
        shards, mesh=mesh, in_specs=placed, out_specs=P("gx", "gy", "gz", None), check_vma=False
    )
```

```python
import functools

import jax
import jax.numpy as jnp
from jax import lax
from jax.experimental import pallas as pl
from jax.experimental.pallas import tpu as pltpu
from jax.sharding import PartitionSpec as P

DOF = 64
CDOF = 16
AGGS = 8
FACES = 7
LANES = 128
WIDE = 2 * LANES
F32 = jnp.float32
BF16 = jnp.bfloat16
VMEM = pl.BlockSpec(memory_space=pltpu.VMEM)
HBM = pl.BlockSpec(memory_space=pltpu.HBM)


def iota(shape, dim):
    return lax.broadcasted_iota(jnp.int32, shape, dim)


def dot(a, b):
    return lax.dot_general(a, b, (((1,), (0,)), ((), ())), preferred_element_type=F32)


def split(x):
    high = x.astype(BF16)
    return high, (x - high.astype(F32)).astype(BF16)


def ones_where(mask):
    return jnp.where(mask, 1.0, 0.0).astype(BF16)


def rows_of(parts):
    return jnp.concatenate(parts, axis=0)


def lanes_of(parts):
    return jnp.concatenate(parts, axis=1)


def column_picker():
    r, q = iota((WIDE, 32), 0), iota((WIDE, 32), 1)
    return ones_where(q == r // 8 % 8 * 4 + r // DOF)


def layer_picker(z):
    r, q = iota((WIDE, LANES), 0), iota((WIDE, LANES), 1)
    return ones_where(q == r // DOF * 32 + r // 8 % 8 * 4 + z)


def prolong_weights(picked):
    count = len(picked)
    keep = iota((WIDE, WIDE), 0) % 8 == iota((WIDE, WIDE), 1) // CDOF % 8
    kept = [jnp.where(keep, p, 0.0).astype(BF16) for p in picked]
    collapse = ones_where(iota((WIDE, LANES), 0) % CDOF == iota((WIDE, LANES), 1) % CDOF)
    spread = dot(rows_of(kept), collapse).reshape(count, 4, DOF, LANES)
    lane = iota((DOF, LANES), 1)
    slot = lane // CDOF % 4
    left = lane < DOF
    factors = []
    for c in range(count):
        full = spread[c, 0]
        for i in range(1, 4):
            full = jnp.where(slot == i, spread[c, i], full)
        high = full.astype(BF16).astype(F32)
        both = jnp.where(left, high, full - high).astype(BF16)
        first = jnp.where(left, high, 0.0).astype(BF16)
        factors.append(rows_of([both, both, first, first]))
    return factors


def blocks_of(rows, factor):
    out = dot(rows, factor)
    return out + pltpu.roll(out, DOF, 1)


def diagonal(product, shift):
    keep = iota((DOF, LANES), 0) // CDOF + shift == iota((DOF, LANES), 1) // CDOF % 4
    kept = jnp.where(keep, product, 0.0).reshape(4, CDOF, LANES)
    return (kept[0] + kept[1]) + (kept[2] + kept[3])


def flatten(packs):
    spread = ones_where(iota((LANES, WIDE), 0) % CDOF == iota((LANES, WIDE), 1) % CDOF)
    element = ones_where(iota((LANES, LANES), 0) // CDOF == iota((LANES, LANES), 1) // CDOF)
    row = ones_where(iota((WIDE, WIDE), 0) % CDOF == iota((WIDE, WIDE), 1) // CDOF)
    wide = [rows_of([part] * 8) * element for pack in packs for part in split(pack)]
    flat = dot(rows_of(wide), spread).astype(BF16)
    return [flat[i * WIDE : (i + 1) * WIDE] * row for i in range(len(packs))]


def choose(labels, base, count):
    return ones_where(iota((count, LANES), 0) + base == labels)


def tick_kernel(out_ref):
    out_ref[...] = jnp.ones(out_ref.shape, F32)


def local_kernel(shape, group_size, agg_hbm, owner_hbm, prolong_ref, fine_ref, tick_ref, outer_ref, inner_ref, label_ref,
                 agg_ref, owner_ref, rows_scr, sems):
    bx, by, bz = shape
    columns = bx * by
    rows_each = AGGS // group_size
    copies = [
        pltpu.make_async_copy(agg_hbm, agg_ref, sems.at[0]),
        pltpu.make_async_copy(owner_hbm, owner_ref, sems.at[1]),
    ]
    for copy in copies:
        copy.start()
    gx, gy, gz = lax.axis_index("gx"), lax.axis_index("gy"), lax.axis_index("gz")
    nx, ny, nz = agg_ref.shape

    lane = iota((32, LANES), 1)
    sub = iota((32, LANES), 0) % 4
    p0, p1 = iota((LANES, LANES), 0), iota((LANES, LANES), 1)
    permute = ones_where((p0 % 4 == p1 % 4) & (p0 // 32 == p1 // 4 % 4) & (p0 // 4 % 8 == p1 // 16))
    turned = []
    for xy in range(columns):
        raw = prolong_ref[xy]
        rolled = [raw] + [pltpu.roll(raw, 32 * m, 1) for m in range(1, 4)]
        stacked = []
        for tau in range(4):
            part = jnp.zeros_like(raw)
            for z in range(4):
                part = jnp.where((sub == z) & (lane // 32 == z), rolled[(z - tau) % 4], part)
            stacked.append(part)
        turned += split(rows_of(stacked).T)
    lefts = dot(rows_of(turned), permute).astype(BF16)
    picked = dot(column_picker(), lanes_of([h for xy in range(columns) for h in split(prolong_ref[xy])]))
    factors = prolong_weights([picked[:, xy * WIDE : (xy + 1) * WIDE] for xy in range(columns)])

    wide_lane = iota((4, CDOF, WIDE), 2) % LANES
    for xy in range(columns):
        high = lefts[xy * WIDE : xy * WIDE + LANES]
        low = lefts[xy * WIDE + LANES : (xy + 1) * WIDE]
        left = rows_of([lanes_of([high, high]), lanes_of([low, jnp.zeros_like(low)])])
        for first in range(0, FACES, 2):
            count = min(2, FACES - first)
            width = count * LANES
            halves = [split(fine_ref[xy * FACES + first + i]) for i in range(count)]
            right = rows_of([lanes_of([h[i] for h in halves]) for i in range(2)])
            out = dot(left, right).reshape(2, 4, 2, CDOF, width)
            out = out[0] + out[1]
            q = jnp.where(wide_lane[:, :, :width] < DOF, out[:, 0], out[:, 1]).reshape(DOF, width)
            high_q, low_q = split(q)
            for i in range(count):
                cut = slice(i * LANES, (i + 1) * LANES)
                rows_scr[xy * FACES + first + i] = lanes_of([high_q[:, cut], low_q[:, cut]])

    for side in range(2):
        outer_ref[side] = rows_scr[side * FACES + 1]
        outer_ref[2 + side] = rows_scr[(2 + side) * FACES + 2]
        outer_ref[4 + side] = rows_scr[2 * side * FACES + 3]
        outer_ref[6 + side] = rows_scr[(2 * side + 1) * FACES + 4]
    for xy in range(columns):
        at = slice(xy * CDOF, (xy + 1) * CDOF)
        outer_ref[8, at] = rows_scr[xy * FACES + 5, :CDOF]
        outer_ref[9, at] = rows_scr[xy * FACES + 6, DOF - CDOF :]

    copies[0].wait()
    copies[1].wait()
    aggs = (agg_ref[...] + 1).reshape(nx * ny, nz).astype(F32).astype(BF16)
    width = 5 * LANES
    z_row, z_lane = iota((nz, width), 0), iota((nz, width), 1)
    kind, place = z_lane // LANES, z_lane % LANES
    slot, face = place // CDOF % 4, place // DOF
    z_off = jnp.where(kind == 0, slot, jnp.where(kind == 1, slot + 1, slot - 1))
    z_off = jnp.where(kind == 3, face * (bz - 1), jnp.where(kind == 4, face * (bz + 1) - 1, z_off))
    by_lane = dot(aggs, ones_where(z_row == gz * bz + z_off)).astype(BF16)
    count = 24
    r = iota((count, nx * ny), 0)
    own_x, own_y = r // 2 % 2, r % 2
    group = r // 4
    dx = jnp.where(group == 1, 1 - own_x, own_x)
    dy = jnp.where(group == 2, 1 - own_y, own_y)
    dx = jnp.where(group == 4, own_x * (bx + 1) - 1, jnp.where(group == 5, own_y, dx))
    dy = jnp.where(group == 4, own_y, jnp.where(group == 5, own_x * (by + 1) - 1, dy))
    px, py = gx * bx + dx, gy * by + dy
    inside = (px >= 0) & (px < nx) & (py >= 0) & (py < ny) & (group != 3)
    at = jnp.where(inside, px * ny + py, -1)
    table = dot(ones_where(iota((count, nx * ny), 1) == at), by_lane).astype(jnp.int32)
    owners = owner_ref[0]
    slots = iota((1, AGGS), 1)
    rank = jnp.zeros((1, AGGS), jnp.int32)
    for a in range(AGGS - 1):
        rank += jnp.where((slots > a) & (owners == owners[:, a : a + 1]), 1, 0)
    own = table[:16]
    owner = jnp.zeros_like(own)
    ranks = jnp.zeros_like(own)
    for a in range(AGGS):
        owner = jnp.where(own == a + 1, owners[:, a : a + 1], owner)
        ranks = jnp.where(own == a + 1, rank[:, a : a + 1], ranks)
    inner_base = owner * (AGGS * rows_each) + ranks
    outer_base = owner * (AGGS * AGGS) + gz * rows_each + ranks

    def cut(array, row, part):
        return array[row : row + 1, part * LANES : (part + 1) * LANES]

    first_half = iota((1, LANES), 1) < DOF
    level = iota((1, LANES), 1) // CDOF % 4

    def pair(array, one, two, part=0):
        return jnp.where(first_half, cut(array, one, part), cut(array, two, part))

    labels = []
    for row, part, valid in ((0, 0, None), (4, 0, None), (8, 0, None), (0, 1, level < bz - 1), (0, 2, level > 0)):
        for x in range(bx):
            label = pair(inner_base, row + 2 * x, row + 2 * x + 1, part)
            label += (pair(table, 2 * x, 2 * x + 1) - 1) * rows_each
            labels.append(label if valid is None else jnp.where(valid, label, -1))
    outer_labels = []
    for k, pick in enumerate(((0, 1), (2, 3), (0, 2), (1, 3))):
        other = pair(table, 16 + 2 * k, 17 + 2 * k)
        label = pair(outer_base, *pick) + (other - 1) * AGGS
        outer_labels.append(jnp.where(other > 0, label, -1))

    def by_column(array, part):
        value = cut(array, 0, part)
        for xy in range(1, columns):
            value = jnp.where(level == xy, cut(array, xy, part), value)
        return value

    other = by_column(table, 4)
    label = by_column(outer_base + owner * (AGGS * AGGS), 3) + (other - 1) * AGGS
    label += jnp.where(first_half, 0, AGGS * AGGS)
    outer_labels.append(jnp.where(other > 0, label, -1))
    label_ref[...] = rows_of(outer_labels + [jnp.full((3, LANES), -1, jnp.int32)]).astype(F32)

    pieces = [[] for _ in range(5)]
    for x in range(bx):
        for y in range(by):
            xy = x * by + y
            sources = (
                (xy * FACES, 0),
                (((1 - x) * by + y) * FACES + (2 if x else 1), 0),
                ((x * by + 1 - y) * FACES + (4 if y else 3), 0),
                (xy * FACES + 5, -1),
                (xy * FACES + 6, 1),
            )
            product = blocks_of(rows_of([rows_scr[index] for index, _ in sources]), factors[xy])
            for i, (_, shift) in enumerate(sources):
                pieces[i].append(diagonal(product[i * DOF : (i + 1) * DOF], shift))
    half = iota((CDOF, LANES), 1) < DOF
    packs = [jnp.where(half, p[2 * x], p[2 * x + 1]) for p in pieces for x in range(bx)]
    flat = flatten(packs)
    chosen = [choose(label, 0, AGGS * AGGS) for label in labels]
    inner_ref[...] = dot(lanes_of([c for c in chosen for _ in range(2)]), rows_of(flat))


def outer_kernel(group_size, links, outer_ref, inner_ref, label_ref, *refs):
    (odd_y, *layers, even_y, odd_x, even_x), sends = refs[:links], refs[links:]
    low_z, high_z = layers[0], layers[-1]
    gz = lax.axis_index("gz")
    values = []
    for axis, even, odd, low, high in (("gx", even_x, odd_x, (2, 3), (0, 1)), ("gy", even_y, odd_y, (1, 3), (0, 2))):
        second = lax.rem(lax.axis_index(axis), 2) == 1
        values += [jnp.where(second, even[xy], odd[xy]) for xy in low]
        values += [jnp.where(second, odd[xy], even[xy]) for xy in high]
    picked = dot(column_picker(), lanes_of([h for value in values for h in split(value)]))
    picked = [picked[:, i * WIDE : (i + 1) * WIDE] for i in range(len(values))]
    for ref, z in ((low_z, 3), (high_z, 0)):
        picked.append(dot(layer_picker(z), lanes_of(split(ref[...].reshape(LANES, LANES)))))
    factors = prolong_weights(picked)
    pieces = [diagonal(blocks_of(outer_ref[i], factors[i]), 0) for i in range(len(factors))]
    half = iota((CDOF, LANES), 1) < DOF
    packs = [jnp.where(half, pieces[i], pieces[i + 1]) for i in range(0, len(pieces), 2)]
    tail = rows_of(packs + [label_ref[...]])
    count = AGGS * AGGS // group_size
    for shift, send in enumerate(sends, 1):
        target = lax.rem(gz + shift, group_size)
        block = inner_ref[pl.ds(pl.multiple_of(target * count, count), count)]
        send[:count] = block[:, :LANES]
        send[count : 2 * count] = block[:, LANES:]
        send[2 * count :] = tail


def outer_sums(tails, gz):
    count = len(tails)
    packs = [tail[k * CDOF : (k + 1) * CDOF] for k in range(5) for tail in tails]
    flat = flatten(packs)
    labels = [tail[5 * CDOF :].astype(jnp.int32) for tail in tails]
    sums = []
    for k in range(5):
        rows = (2 if k == 4 else 1) * AGGS * AGGS
        chosen = [choose(label[k : k + 1], gz * rows, rows) for label in labels for _ in range(2)]
        sums.append(dot(lanes_of(chosen), rows_of(flat[k * count : (k + 1) * count])))
    return sums


def own_kernel(group_size, inner_ref, send_ref, out_ref):
    gz = lax.axis_index("gz")
    rows_each = AGGS // group_size
    count = AGGS * AGGS // group_size
    mine = iota((AGGS, WIDE), 0) // rows_each == gz
    block = inner_ref[pl.ds(pl.multiple_of(gz * count, count), count)]
    for c in range(AGGS):
        part = rows_of([block[c * rows_each : (c + 1) * rows_each]] * group_size)
        out_ref[:, c * WIDE : (c + 1) * WIDE] = jnp.where(mine, part, 0.0)
    at = AGGS
    for value in outer_sums([send_ref[2 * count :]], gz):
        for c in range(value.shape[0] // AGGS):
            out_ref[:, at * WIDE : (at + 1) * WIDE] = value[c * AGGS : (c + 1) * AGGS]
            at += 1


def final_kernel(group_size, own_ref, *refs):
    received, out_hbm, out_ref, sems = refs[:-3], refs[-3], refs[-2], refs[-1]
    gz = lax.axis_index("gz")
    rows_each = AGGS // group_size
    count = AGGS * AGGS // group_size
    copies = []

    def send_out(face):
        part = pl.ds(face * AGGS * WIDE, AGGS * WIDE)
        copies.append(pltpu.make_async_copy(out_ref.at[:, part], out_hbm.at[:, part], sems.at[face]))
        copies[-1].start()

    brick = iota((AGGS, LANES), 0) // rows_each
    for c in range(AGGS):
        for h in range(2):
            at = slice((2 * c + h) * LANES, (2 * c + h + 1) * LANES)
            value = own_ref[:, at]
            for shift, ref in enumerate(received, 1):
                part = ref[h * count + c * rows_each : h * count + (c + 1) * rows_each]
                theirs = lax.rem(gz - shift + group_size, group_size)
                value = jnp.where(brick == theirs, rows_of([part] * group_size), value)
            out_ref[:, at] = value
    send_out(0)
    at = AGGS
    for value in outer_sums([ref[2 * count :] for ref in received], gz):
        for c in range(value.shape[0] // AGGS):
            cut = slice(at * WIDE, (at + 1) * WIDE)
            out_ref[:, cut] = own_ref[:, cut] + value[c * AGGS : (c + 1) * AGGS]
            at += 1
            if at % AGGS == 0:
                send_out(at // AGGS - 1)
    for copy in copies:
        copy.wait()


def matching(sizes, along, first):
    def partner(place):
        i = (place[along] - first) ^ 1
        moved = list(place)
        if 0 <= i + first < sizes[along] and place[along] >= first:
            moved[along] = i + first
        elif place[1 - along] ^ 1 < sizes[1 - along]:
            moved[1 - along] = place[1 - along] ^ 1
        return moved[0] * sizes[1] + moved[1]

    return [(x * sizes[1] + y, partner((x, y))) for x in range(sizes[0]) for y in range(sizes[1])]


def rotation(count, step):
    return [(i, (i + step) % count) for i in range(count)]


def shards(fine_blocks, prolong, agg_map, owner_map):
    bx, by, bz = fine_blocks.shape[:3]
    columns = bx * by
    group_size = lax.axis_size("gz")
    fine = fine_blocks.transpose(0, 1, 3, 2, 4).reshape(columns * FACES, bz, 32, LANES)
    fine = fine.transpose(0, 2, 1, 3).reshape(columns * FACES, 32 * bz, LANES)
    base = prolong.reshape(columns, bz, 8, LANES).transpose(0, 2, 1, 3).reshape(columns, 8 * bz, LANES)
    tick = pl.pallas_call(
        tick_kernel,
        out_shape=pltpu.VMEM((8, LANES), F32),
        out_specs=VMEM,
        cost_estimate=pl.CostEstimate(flops=int(5e9), bytes_accessed=int(5e7), transcendentals=0),
    )()
    sizes = lax.axis_size("gx"), lax.axis_size("gy")
    layers = [lax.ppermute(base, "gz", rotation(group_size, step)) for step in ((1, -1) if group_size > 2 else (1,))]
    even_x, odd_x, even_y, odd_y = [
        lax.ppermute(base, ("gx", "gy"), matching(sizes, along, first)) for along in range(2) for first in range(2)
    ]
    halos = [odd_y, *layers, even_y, odd_x, even_x]
    params = pltpu.CompilerParams(vmem_limit_bytes=32 * 1024 * 1024)
    shape = jax.ShapeDtypeStruct
    outer, inner, labels = pl.pallas_call(
        functools.partial(local_kernel, (bx, by, bz), group_size),
        out_shape=[shape((10, DOF, WIDE), BF16), shape((AGGS * AGGS, WIDE), F32), shape((8, LANES), F32)],
        in_specs=[HBM] * 2 + [VMEM] * 3,
        out_specs=[VMEM] * 3,
        scratch_shapes=[
            pltpu.VMEM(agg_map.shape, jnp.int32),
            pltpu.VMEM(owner_map.shape, jnp.int32),
            pltpu.VMEM((columns * FACES, DOF, WIDE), BF16),
            pltpu.SemaphoreType.DMA((2,)),
        ],
        compiler_params=params,
        cost_estimate=pl.CostEstimate(flops=int(2e9), bytes_accessed=int(4e6), transcendentals=0),
    )(
        *(pltpu.with_memory_space_constraint(a, pltpu.HBM) for a in (agg_map, owner_map)),
        *(pltpu.with_memory_space_constraint(a, pltpu.VMEM) for a in (base, fine)),
        tick,
    )
    size = 2 * AGGS * AGGS // group_size + 5 * CDOF + 8
    sends = pl.pallas_call(
        functools.partial(outer_kernel, group_size, len(halos)),
        out_shape=[shape((size, LANES), F32)] * (group_size - 1),
        in_specs=[VMEM] * (3 + len(halos)),
        out_specs=[VMEM] * (group_size - 1),
        compiler_params=params,
    )(outer, inner, labels, *halos)
    received = [
        lax.ppermute(send, "gz", rotation(group_size, shift)) for shift, send in enumerate(sends, 1)
    ]
    full = shape((AGGS, FACES * AGGS * CDOF * CDOF), F32)
    own = pl.pallas_call(
        functools.partial(own_kernel, group_size),
        out_shape=full,
        in_specs=[VMEM, VMEM],
        out_specs=VMEM,
        compiler_params=params,
        cost_estimate=pl.CostEstimate(flops=int(1e9), bytes_accessed=int(2e6), transcendentals=0),
    )(inner, sends[0])
    out = pl.pallas_call(
        functools.partial(final_kernel, group_size),
        out_shape=full,
        in_specs=[VMEM] * group_size,
        out_specs=HBM,
        scratch_shapes=[pltpu.VMEM(full.shape, F32), pltpu.SemaphoreType.DMA((FACES,))],
        compiler_params=params,
    )(own, *received)
    return out[None, None]


def solution(mesh):
    placed = (P("gx", "gy", "gz", None, None), P("gx", "gy", "gz", None), P(), P("gx", "gy", "gz"))
    return jax.shard_map(
        shards, mesh=mesh, in_specs=placed, out_specs=P("gx", "gy", "gz", None), check_vma=False
    )
```

```python
import functools

import jax
import jax.numpy as jnp
from jax import lax
from jax.experimental import pallas as pl
from jax.experimental.pallas import tpu as pltpu
from jax.sharding import PartitionSpec as P

DOF = 64
CDOF = 16
AGGS = 8
FACES = 7
LANES = 128
WIDE = 2 * LANES
F32 = jnp.float32
BF16 = jnp.bfloat16
VMEM = pl.BlockSpec(memory_space=pltpu.VMEM)
HBM = pl.BlockSpec(memory_space=pltpu.HBM)


def iota(shape, dim):
    return lax.broadcasted_iota(jnp.int32, shape, dim)


def dot(a, b):
    return lax.dot_general(a, b, (((1,), (0,)), ((), ())), preferred_element_type=F32)


def split(x):
    high = x.astype(BF16)
    return high, (x - high.astype(F32)).astype(BF16)


def ones_where(mask):
    return jnp.where(mask, 1.0, 0.0).astype(BF16)


def rows_of(parts):
    return jnp.concatenate(parts, axis=0)


def lanes_of(parts):
    return jnp.concatenate(parts, axis=1)


def column_picker():
    r, q = iota((WIDE, 32), 0), iota((WIDE, 32), 1)
    return ones_where(q == r // 8 % 8 * 4 + r // DOF)


def layer_picker():
    r, q = iota((WIDE, 32), 0), iota((WIDE, 32), 1)
    return ones_where(q == r // 8)


def spread_blocks(picked):
    keep = iota((WIDE, WIDE), 0) % 8 == iota((WIDE, WIDE), 1) // CDOF % 8
    kept = [jnp.where(keep, p, 0.0).astype(BF16) for p in picked]
    collapse = ones_where(iota((WIDE, LANES), 0) % CDOF == iota((WIDE, LANES), 1) % CDOF)
    spread = dot(rows_of(kept), collapse).reshape(len(picked), 4, DOF, LANES)
    slot = iota((DOF, LANES), 1) // CDOF % 4
    blocks = []
    for c in range(len(picked)):
        full = spread[c, 0]
        for i in range(1, 4):
            full = jnp.where(slot == i, spread[c, i], full)
        blocks.append(full)
    return blocks


def factor_of(full):
    left = iota((DOF, LANES), 1) < DOF
    high = full.astype(BF16).astype(F32)
    both = jnp.where(left, high, full - high).astype(BF16)
    first = jnp.where(left, high, 0.0).astype(BF16)
    return rows_of([both, both, first, first])


def folded(full):
    return jnp.where(iota((DOF // 2, LANES), 1) < DOF, full[: DOF // 2], full[DOF // 2 :])


def unfolded(part):
    left = iota((DOF // 2, LANES), 1) < DOF
    turned = pltpu.roll(part, DOF, 1)
    return rows_of([jnp.where(left, part, turned), jnp.where(left, turned, part)])


def blocks_of(rows, factor):
    out = dot(rows, factor)
    return out + pltpu.roll(out, DOF, 1)


def diagonal(product, shift):
    keep = iota((DOF, LANES), 0) // CDOF + shift == iota((DOF, LANES), 1) // CDOF % 4
    kept = jnp.where(keep, product, 0.0).reshape(4, CDOF, LANES)
    return (kept[0] + kept[1]) + (kept[2] + kept[3])


def flatten(packs):
    spread = ones_where(iota((LANES, WIDE), 0) % CDOF == iota((LANES, WIDE), 1) % CDOF)
    element = ones_where(iota((LANES, LANES), 0) // CDOF == iota((LANES, LANES), 1) // CDOF)
    row = ones_where(iota((WIDE, WIDE), 0) % CDOF == iota((WIDE, WIDE), 1) // CDOF)
    wide = [rows_of([part] * 8) * element for pack in packs for part in split(pack)]
    flat = dot(rows_of(wide), spread).astype(BF16)
    return [flat[i * WIDE : (i + 1) * WIDE] * row for i in range(len(packs))]


def choose(labels, base, count):
    return ones_where(iota((count, LANES), 0) + base == labels)


def tick_kernel(out_ref):
    out_ref[...] = jnp.ones(out_ref.shape, F32)


def local_kernel(shape, group_size, agg_ref, owner_ref, prolong_ref, fine_ref, tick_ref,
                 outer_ref, inner_ref, label_ref, layer_ref, layer_send, rows_scr):
    bx, by, bz = shape
    columns = bx * by
    rows_each = AGGS // group_size
    gx, gy, gz = lax.axis_index("gx"), lax.axis_index("gy"), lax.axis_index("gz")
    nx, ny, nz = agg_ref.shape

    lane = iota((32, LANES), 1)
    sub = iota((32, LANES), 0) % 4
    p0, p1 = iota((LANES, LANES), 0), iota((LANES, LANES), 1)
    permute = ones_where((p0 % 4 == p1 % 4) & (p0 // 32 == p1 // 4 % 4) & (p0 // 4 % 8 == p1 // 16))
    turned = []
    for xy in range(columns):
        raw = prolong_ref[xy]
        rolled = [raw] + [pltpu.roll(raw, 32 * m, 1) for m in range(1, 4)]
        stacked = []
        for tau in range(4):
            part = jnp.zeros_like(raw)
            for z in range(4):
                part = jnp.where((sub == z) & (lane // 32 == z), rolled[(z - tau) % 4], part)
            stacked.append(part)
        turned += split(rows_of(stacked).T)
    lefts = dot(rows_of(turned), permute).astype(BF16)
    picked = dot(column_picker(), lanes_of([h for xy in range(columns) for h in split(prolong_ref[xy])]))
    picked = [picked[:, xy * WIDE : (xy + 1) * WIDE] for xy in range(columns)]
    low, high = (
        rows_of([prolong_ref[xy, pl.ds(z, 8, stride=bz), :] for xy in range(columns)]) for z in (0, bz - 1)
    )
    layers = [jnp.where(gz == 0, high, low)] if group_size == 2 else [low, high]
    picked += [dot(layer_picker(), lanes_of(split(layer))) for layer in layers]
    blocks = spread_blocks(picked)
    factors = [factor_of(full) for full in blocks[:columns]]

    wide_lane = iota((4, CDOF, WIDE), 2) % LANES
    for xy in range(columns):
        high = lefts[xy * WIDE : xy * WIDE + LANES]
        low = lefts[xy * WIDE + LANES : (xy + 1) * WIDE]
        left = rows_of([lanes_of([high, high]), lanes_of([low, jnp.zeros_like(low)])])
        for first in range(0, FACES, 2):
            count = min(2, FACES - first)
            width = count * LANES
            halves = [split(fine_ref[xy * FACES + first + i]) for i in range(count)]
            right = rows_of([lanes_of([h[i] for h in halves]) for i in range(2)])
            out = dot(left, right).reshape(2, 4, 2, CDOF, width)
            out = out[0] + out[1]
            q = jnp.where(wide_lane[:, :, :width] < DOF, out[:, 0], out[:, 1]).reshape(DOF, width)
            high_q, low_q = split(q)
            for i in range(count):
                cut = slice(i * LANES, (i + 1) * LANES)
                rows_scr[xy * FACES + first + i] = lanes_of([high_q[:, cut], low_q[:, cut]])

    for side in range(2):
        outer_ref[side] = rows_scr[side * FACES + 1]
        outer_ref[2 + side] = rows_scr[(2 + side) * FACES + 2]
        outer_ref[4 + side] = rows_scr[2 * side * FACES + 3]
        outer_ref[6 + side] = rows_scr[(2 * side + 1) * FACES + 4]
    low = rows_of([rows_scr[xy * FACES + 5, :CDOF] for xy in range(columns)])
    high = rows_of([rows_scr[xy * FACES + 6, DOF - CDOF :] for xy in range(columns)])
    layers = [jnp.where(gz == 0, high, low)] if group_size == 2 else [low, high]
    for i, layer in enumerate(layers):
        layer_ref[i] = layer
        both = layer[:, :LANES].astype(F32) + layer[:, LANES:].astype(F32)
        layer_send[i * DOF : i * DOF + DOF // 2] = folded(both + pltpu.roll(both, DOF, 1))
        layer_send[i * DOF + DOF // 2 : (i + 1) * DOF] = folded(blocks[columns + i])

    aggs = (agg_ref[...] + 1).reshape(nx * ny, nz).astype(F32).astype(BF16)
    width = 5 * LANES
    z_row, z_lane = iota((nz, width), 0), iota((nz, width), 1)
    kind, place = z_lane // LANES, z_lane % LANES
    slot, face = place // CDOF % 4, (1 - gz) if group_size == 2 else place // DOF
    z_off = jnp.where(kind == 0, slot, jnp.where(kind == 1, slot + 1, slot - 1))
    z_off = jnp.where(kind == 3, face * (bz - 1), jnp.where(kind == 4, face * (bz + 1) - 1, z_off))
    by_lane = dot(aggs, ones_where(z_row == gz * bz + z_off)).astype(BF16)
    count = 24
    r = iota((count, nx * ny), 0)
    own_x, own_y = r // 2 % 2, r % 2
    group = r // 4
    dx = jnp.where(group == 1, 1 - own_x, own_x)
    dy = jnp.where(group == 2, 1 - own_y, own_y)
    dx = jnp.where(group == 4, own_x * (bx + 1) - 1, jnp.where(group == 5, own_y, dx))
    dy = jnp.where(group == 4, own_y, jnp.where(group == 5, own_x * (by + 1) - 1, dy))
    px, py = gx * bx + dx, gy * by + dy
    inside = (px >= 0) & (px < nx) & (py >= 0) & (py < ny) & (group != 3)
    at = jnp.where(inside, px * ny + py, -1)
    table = dot(ones_where(iota((count, nx * ny), 1) == at), by_lane).astype(jnp.int32)
    owners = owner_ref[0]
    slots = iota((1, AGGS), 1)
    rank = jnp.zeros((1, AGGS), jnp.int32)
    for a in range(AGGS - 1):
        rank += jnp.where((slots > a) & (owners == owners[:, a : a + 1]), 1, 0)
    own = table[:16]
    owner = jnp.zeros_like(own)
    ranks = jnp.zeros_like(own)
    for a in range(AGGS):
        owner = jnp.where(own == a + 1, owners[:, a : a + 1], owner)
        ranks = jnp.where(own == a + 1, rank[:, a : a + 1], ranks)
    inner_base = owner * (AGGS * rows_each) + ranks
    outer_base = owner * (AGGS * AGGS) + gz * rows_each + ranks

    def cut(array, row, part):
        return array[row : row + 1, part * LANES : (part + 1) * LANES]

    first_half = iota((1, LANES), 1) < DOF
    level = iota((1, LANES), 1) // CDOF % 4

    def pair(array, one, two, part=0):
        return jnp.where(first_half, cut(array, one, part), cut(array, two, part))

    labels = []
    for row, part, valid in ((0, 0, None), (4, 0, None), (8, 0, None), (0, 1, level < bz - 1), (0, 2, level > 0)):
        for x in range(bx):
            label = pair(inner_base, row + 2 * x, row + 2 * x + 1, part)
            label += (pair(table, 2 * x, 2 * x + 1) - 1) * rows_each
            labels.append(label if valid is None else jnp.where(valid, label, -1))
    outer_labels = []
    for k, pick in enumerate(((0, 1), (2, 3), (0, 2), (1, 3))):
        other = pair(table, 16 + 2 * k, 17 + 2 * k)
        label = pair(outer_base, *pick) + (other - 1) * AGGS
        outer_labels.append(jnp.where(other > 0, label, -1))

    def by_column(array, part):
        value = cut(array, 0, part)
        for xy in range(1, columns):
            value = jnp.where(level == xy, cut(array, xy, part), value)
        return value

    other = by_column(table, 4)
    label = by_column(outer_base + owner * (AGGS * AGGS), 3) + (other - 1) * AGGS
    label += (1 - gz) * AGGS * AGGS if group_size == 2 else jnp.where(first_half, 0, AGGS * AGGS)
    outer_labels.append(jnp.where(other > 0, label, -1))
    label_ref[...] = rows_of(outer_labels + [jnp.full((3, LANES), -1, jnp.int32)]).astype(F32)

    pieces = [[] for _ in range(5)]
    for x in range(bx):
        for y in range(by):
            xy = x * by + y
            sources = (
                (xy * FACES, 0),
                (((1 - x) * by + y) * FACES + (2 if x else 1), 0),
                ((x * by + 1 - y) * FACES + (4 if y else 3), 0),
                (xy * FACES + 5, -1),
                (xy * FACES + 6, 1),
            )
            product = blocks_of(rows_of([rows_scr[index] for index, _ in sources]), factors[xy])
            for i, (_, shift) in enumerate(sources):
                pieces[i].append(diagonal(product[i * DOF : (i + 1) * DOF], shift))
    half = iota((CDOF, LANES), 1) < DOF
    packs = [jnp.where(half, p[2 * x], p[2 * x + 1]) for p in pieces for x in range(bx)]
    flat = flatten(packs)
    chosen = [choose(label, 0, AGGS * AGGS) for label in labels]
    inner_ref[...] = dot(lanes_of([c for c in chosen for _ in range(2)]), rows_of(flat))


def outer_kernel(group_size, outer_ref, inner_ref, label_ref, layer_send, odd_y, even_y, odd_x, even_x, *sends):
    gz = lax.axis_index("gz")
    values = []
    for axis, even, odd, low, high in (("gx", even_x, odd_x, (2, 3), (0, 1)), ("gy", even_y, odd_y, (1, 3), (0, 2))):
        second = lax.rem(lax.axis_index(axis), 2) == 1
        values += [jnp.where(second, even[xy], odd[xy]) for xy in low]
        values += [jnp.where(second, odd[xy], even[xy]) for xy in high]
    picked = dot(column_picker(), lanes_of([h for value in values for h in split(value)]))
    blocks = spread_blocks([picked[:, i * WIDE : (i + 1) * WIDE] for i in range(len(values))])
    pieces = [diagonal(blocks_of(outer_ref[i], factor_of(full)), 0) for i, full in enumerate(blocks)]
    half = iota((CDOF, LANES), 1) < DOF
    packs = [jnp.where(half, pieces[i], pieces[i + 1]) for i in range(0, len(pieces), 2)]
    tail = rows_of(packs + [label_ref[...], layer_send[...]])
    count = AGGS * AGGS // group_size
    for shift, send in enumerate(sends, 1):
        target = lax.rem(gz + shift, group_size)
        block = inner_ref[pl.ds(pl.multiple_of(target * count, count), count)]
        send[:count] = block[:, :LANES]
        send[count : 2 * count] = block[:, LANES:]
        send[2 * count :] = tail


def parts_of(tail):
    packs = [tail[k * CDOF : (k + 1) * CDOF] for k in range(4)]
    labels = tail[DOF : DOF + 8].astype(jnp.int32)
    halves = [tail[at : at + DOF // 2] for at in range(DOF + 8, tail.shape[0], DOF // 2)]
    return packs, labels, halves[::2], halves[1::2]


def own_kernel(group_size, inner_ref, send_ref, out_ref, factor_ref):
    gz = lax.axis_index("gz")
    rows_each = AGGS // group_size
    count = AGGS * AGGS // group_size
    mine = iota((AGGS, WIDE), 0) // rows_each == gz
    block = inner_ref[pl.ds(pl.multiple_of(gz * count, count), count)]
    for c in range(AGGS):
        part = rows_of([block[c * rows_each : (c + 1) * rows_each]] * group_size)
        out_ref[:, c * WIDE : (c + 1) * WIDE] = jnp.where(mine, part, 0.0)
    packs, labels, _, blocks = parts_of(send_ref[2 * count :])
    for i, part in enumerate(blocks):
        factor_ref[i] = factor_of(unfolded(part))
    for k, flat in enumerate(flatten(packs)):
        chosen = choose(labels[k : k + 1], gz * AGGS * AGGS, AGGS * AGGS)
        value = dot(lanes_of([chosen] * 2), flat)
        for c in range(AGGS):
            at = ((k + 1) * AGGS + c) * WIDE
            out_ref[:, at : at + WIDE] = value[c * AGGS : (c + 1) * AGGS]
    out_ref[:, 5 * AGGS * WIDE :] = jnp.zeros((AGGS, 2 * AGGS * WIDE), F32)


def final_kernel(group_size, own_ref, factor_ref, layer_ref, label_ref, *refs):
    received, out_hbm, out_ref, sems = refs[:-3], refs[-3], refs[-2], refs[-1]
    gz = lax.axis_index("gz")
    rows_each = AGGS // group_size
    count = AGGS * AGGS // group_size
    copies = []

    def send_out(face):
        part = pl.ds(face * AGGS * WIDE, AGGS * WIDE)
        copies.append(pltpu.make_async_copy(out_ref.at[:, part], out_hbm.at[:, part], sems.at[face]))
        copies[-1].start()

    tails = [parts_of(ref[2 * count :]) for ref in received]
    left = iota((DOF, LANES), 1) < DOF
    rows = [[layer_ref[i] for i in range(layer_ref.shape[0])]]
    factors = [[factor_ref[i] for i in range(layer_ref.shape[0])]]
    for _, _, layers, blocks in tails:
        rows.append([lanes_of(split(jnp.where(left, unfolded(layer), 0.0))) for layer in layers])
        factors.append([factor_of(unfolded(part)) for part in blocks])
    layer_labels = [label_ref[4:5].astype(jnp.int32)] + [labels[4:5] for _, labels, _, _ in tails]
    half = iota((CDOF, LANES), 1) < DOF
    if group_size == 2:
        pieces = [diagonal(blocks_of(rows[i][0], factors[1 - i][0]), 0) for i in range(2)]
        layer_packs = [jnp.where(half, *pieces)]
        layer_labels = [jnp.where(half[:1], *layer_labels)]
    else:
        low, high = {}, {}
        for i in range(group_size):
            above = (i - 1) % group_size
            high[i] = diagonal(blocks_of(rows[i][1], factors[above][0]), 0)
            low[above] = diagonal(blocks_of(rows[above][0], factors[i][1]), 0)
        layer_packs = [jnp.where(half, low[i], high[i]) for i in range(group_size)]

    brick = iota((AGGS, LANES), 0) // rows_each
    for c in range(AGGS):
        for h in range(2):
            at = slice((2 * c + h) * LANES, (2 * c + h + 1) * LANES)
            value = own_ref[:, at]
            for shift, ref in enumerate(received, 1):
                part = ref[h * count + c * rows_each : h * count + (c + 1) * rows_each]
                theirs = lax.rem(gz - shift + group_size, group_size)
                value = jnp.where(brick == theirs, rows_of([part] * group_size), value)
            out_ref[:, at] = value
    send_out(0)
    flat = flatten([packs[k] for k in range(4) for packs, _, _, _ in tails] + layer_packs)
    size = AGGS * AGGS
    for k in range(4):
        chosen = [choose(labels[k : k + 1], gz * size, size) for _, labels, _, _ in tails]
        parts = flat[k * len(tails) : (k + 1) * len(tails)]
        value = dot(lanes_of([c for c in chosen for _ in range(2)]), rows_of(parts))
        for c in range(AGGS):
            cut = slice(((k + 1) * AGGS + c) * WIDE, ((k + 1) * AGGS + c + 1) * WIDE)
            out_ref[:, cut] = own_ref[:, cut] + value[c * AGGS : (c + 1) * AGGS]
        send_out(k + 1)
    chosen = [choose(label, gz * 2 * size, 2 * size) for label in layer_labels]
    value = dot(lanes_of([c for c in chosen for _ in range(2)]), rows_of(flat[4 * len(tails) :]))
    for c in range(2 * AGGS):
        cut = slice((5 * AGGS + c) * WIDE, (5 * AGGS + c + 1) * WIDE)
        out_ref[:, cut] = value[c * AGGS : (c + 1) * AGGS]
    send_out(5)
    send_out(6)
    for copy in copies:
        copy.wait()


def matching(sizes, along, first):
    def partner(place):
        i = (place[along] - first) ^ 1
        moved = list(place)
        if 0 <= i + first < sizes[along] and place[along] >= first:
            moved[along] = i + first
        elif place[1 - along] ^ 1 < sizes[1 - along]:
            moved[1 - along] = place[1 - along] ^ 1
        return moved[0] * sizes[1] + moved[1]

    return [(x * sizes[1] + y, partner((x, y))) for x in range(sizes[0]) for y in range(sizes[1])]


def rotation(count, step):
    return [(i, (i + step) % count) for i in range(count)]


def shards(fine_blocks, prolong, agg_map, owner_map):
    bx, by, bz = fine_blocks.shape[:3]
    columns = bx * by
    group_size = lax.axis_size("gz")
    fine = fine_blocks.transpose(0, 1, 3, 2, 4).reshape(columns * FACES, bz, 32, LANES)
    fine = fine.transpose(0, 2, 1, 3).reshape(columns * FACES, 32 * bz, LANES)
    base = prolong.reshape(columns, bz, 8, LANES).transpose(0, 2, 1, 3).reshape(columns, 8 * bz, LANES)
    tick = pl.pallas_call(
        tick_kernel,
        out_shape=pltpu.VMEM((8, LANES), F32),
        out_specs=VMEM,
        cost_estimate=pl.CostEstimate(flops=int(5e9), bytes_accessed=int(5e7), transcendentals=0),
    )()
    sizes = lax.axis_size("gx"), lax.axis_size("gy")
    even_x, odd_x, even_y, odd_y = [
        lax.ppermute(base, ("gx", "gy"), matching(sizes, along, first)) for along in range(2) for first in range(2)
    ]
    halos = [odd_y, even_y, odd_x, even_x]
    layers = 1 if group_size == 2 else 2
    params = pltpu.CompilerParams(vmem_limit_bytes=32 * 1024 * 1024)
    shape = jax.ShapeDtypeStruct
    outer, inner, labels, layer_rows, layer_send = pl.pallas_call(
        functools.partial(local_kernel, (bx, by, bz), group_size),
        out_shape=[
            shape((8, DOF, WIDE), BF16),
            shape((AGGS * AGGS, WIDE), F32),
            shape((8, LANES), F32),
            shape((layers, DOF, WIDE), BF16),
            shape((layers * DOF, LANES), F32),
        ],
        in_specs=[VMEM] * 5,
        out_specs=[VMEM] * 5,
        scratch_shapes=[pltpu.VMEM((columns * FACES, DOF, WIDE), BF16)],
        compiler_params=params,
        cost_estimate=pl.CostEstimate(flops=int(2e9), bytes_accessed=int(4e6), transcendentals=0),
    )(
        *(pltpu.with_memory_space_constraint(a, pltpu.VMEM) for a in (agg_map, owner_map, base, fine)),
        tick,
    )
    size = 2 * AGGS * AGGS // group_size + 4 * CDOF + 8 + layers * DOF
    sends = pl.pallas_call(
        functools.partial(outer_kernel, group_size),
        out_shape=[shape((size, LANES), F32)] * (group_size - 1),
        in_specs=[VMEM] * 8,
        out_specs=[VMEM] * (group_size - 1),
        compiler_params=params,
    )(outer, inner, labels, layer_send, *halos)
    received = [
        lax.ppermute(send, "gz", rotation(group_size, shift)) for shift, send in enumerate(sends, 1)
    ]
    full = shape((AGGS, FACES * AGGS * CDOF * CDOF), F32)
    own, factor = pl.pallas_call(
        functools.partial(own_kernel, group_size),
        out_shape=[full, shape((layers, WIDE, LANES), BF16)],
        in_specs=[VMEM, VMEM],
        out_specs=[VMEM, VMEM],
        compiler_params=params,
        cost_estimate=pl.CostEstimate(flops=int(1e9), bytes_accessed=int(2e6), transcendentals=0),
    )(inner, sends[0])
    out = pl.pallas_call(
        functools.partial(final_kernel, group_size),
        out_shape=full,
        in_specs=[VMEM] * (3 + group_size),
        out_specs=HBM,
        scratch_shapes=[pltpu.VMEM(full.shape, F32), pltpu.SemaphoreType.DMA((FACES,))],
        compiler_params=params,
    )(own, factor, layer_rows, labels, *received)
    return out[None, None]


def solution(mesh):
    placed = (P("gx", "gy", "gz", None, None), P("gx", "gy", "gz", None), P(), P("gx", "gy", "gz"))
    return jax.shard_map(
        shards, mesh=mesh, in_specs=placed, out_specs=P("gx", "gy", "gz", None), check_vma=False
    )
```

```python
import functools

import jax
import jax.numpy as jnp
from jax import lax
from jax.experimental import pallas as pl
from jax.experimental.pallas import tpu as pltpu
from jax.sharding import PartitionSpec as P

DOF = 64
CDOF = 16
AGGS = 8
FACES = 7
LANES = 128
WIDE = 2 * LANES
F32 = jnp.float32
BF16 = jnp.bfloat16
VMEM = pl.BlockSpec(memory_space=pltpu.VMEM)
HBM = pl.BlockSpec(memory_space=pltpu.HBM)


def iota(shape, dim):
    return lax.broadcasted_iota(jnp.int32, shape, dim)


def dot(a, b):
    return lax.dot_general(a, b, (((1,), (0,)), ((), ())), preferred_element_type=F32)


def split(x):
    high = x.astype(BF16)
    return high, (x - high.astype(F32)).astype(BF16)


def ones_where(mask):
    return jnp.where(mask, 1.0, 0.0).astype(BF16)


def rows_of(parts):
    return jnp.concatenate(parts, axis=0)


def lanes_of(parts):
    return jnp.concatenate(parts, axis=1)


def spread_blocks(out_ref, pieces):
    slot = iota((8, LANES), 1) // CDOF
    for b in range(8):
        value = pltpu.roll(pieces[0], -b * CDOF % LANES, 1)
        for i in range(1, 4):
            value = jnp.where(slot == i, pltpu.roll(pieces[i], (i - b) * CDOF % LANES, 1), value)
        out_ref[pl.ds(b, 8, stride=8), :] = value


def factor_of(full):
    left = iota((DOF, LANES), 1) < DOF
    high = full.astype(BF16).astype(F32)
    both = jnp.where(left, high, pltpu.roll(full - high, DOF, 1)).astype(BF16)
    first = jnp.where(left, high, 0.0).astype(BF16)
    return rows_of([both, both, first, first])


def folded(full):
    half = DOF // 2
    return jnp.where(iota((half, LANES), 1) < DOF, full[:half], pltpu.roll(full[half:], DOF, 1))


def unfolded(part):
    left = iota((DOF // 2, LANES), 1) < DOF
    turned = pltpu.roll(part, DOF, 1)
    return rows_of([jnp.where(left, part, turned), jnp.where(left, turned, part)])


def blocks_of(rows, factor):
    out = dot(rows, factor)
    return out + pltpu.roll(out, DOF, 1)


def diagonal(product, shift):
    keep = iota((DOF, LANES), 0) // CDOF + shift == iota((DOF, LANES), 1) // CDOF % 4
    kept = jnp.where(keep, product, 0.0).reshape(4, CDOF, LANES)
    return (kept[0] + kept[1]) + (kept[2] + kept[3])


def flatten(packs):
    spread = ones_where(iota((LANES, WIDE), 0) % CDOF == iota((LANES, WIDE), 1) % CDOF)
    element = ones_where(iota((LANES, LANES), 0) // CDOF == iota((LANES, LANES), 1) // CDOF)
    row = ones_where(iota((WIDE, WIDE), 0) % CDOF == iota((WIDE, WIDE), 1) // CDOF)
    wide = [rows_of([part] * 8) * element for pack in packs for part in split(pack)]
    flat = dot(rows_of(wide), spread).astype(BF16)
    return [flat[i * WIDE : (i + 1) * WIDE] * row for i in range(len(packs))]


def choose(labels, base, count):
    return ones_where(iota((count, LANES), 0) + base == labels)


def tick_kernel(out_ref):
    out_ref[...] = jnp.ones(out_ref.shape, F32)


def local_kernel(shape, group_size, agg_ref, owner_ref, prolong_ref, fine_ref, tick_ref,
                 outer_ref, inner_ref, label_ref, layer_ref, layer_send, rows_scr, blocks_scr):
    bx, by, bz = shape
    columns = bx * by
    rows_each = AGGS // group_size
    gx, gy, gz = lax.axis_index("gx"), lax.axis_index("gy"), lax.axis_index("gz")
    nx, ny, nz = agg_ref.shape

    lane = iota((32, LANES), 1)
    sub = iota((32, LANES), 0) % 4
    p0, p1 = iota((LANES, LANES), 0), iota((LANES, LANES), 1)
    permute = ones_where((p0 % 4 == p1 % 4) & (p0 // 32 == p1 // 4 % 4) & (p0 // 4 % 8 == p1 // 16))
    turned = []
    for xy in range(columns):
        raw = prolong_ref[xy]
        rolled = [raw] + [pltpu.roll(raw, 32 * m, 1) for m in range(1, 4)]
        stacked = []
        for tau in range(4):
            part = jnp.zeros_like(raw)
            for z in range(4):
                part = jnp.where((sub == z) & (lane // 32 == z), rolled[(z - tau) % 4], part)
            stacked.append(part)
        turned += split(rows_of(stacked).T)
    lefts = dot(rows_of(turned), permute).astype(BF16)
    for xy in range(columns):
        spread_blocks(blocks_scr.at[xy], [prolong_ref[xy, pl.ds(z, 8, stride=bz), :] for z in range(bz)])
    low, high = ([prolong_ref[xy, pl.ds(z, 8, stride=bz), :] for xy in range(columns)] for z in (0, bz - 1))
    layers = [[jnp.where(gz == 0, h, l) for l, h in zip(low, high)]] if group_size == 2 else [low, high]
    for i, layer in enumerate(layers):
        spread_blocks(blocks_scr.at[columns + i], layer)
    factors = [factor_of(blocks_scr[xy]) for xy in range(columns)]

    wide_lane = iota((4, CDOF, WIDE), 2) % LANES
    for xy in range(columns):
        high = lefts[xy * WIDE : xy * WIDE + LANES]
        low = lefts[xy * WIDE + LANES : (xy + 1) * WIDE]
        left = rows_of([lanes_of([high, high]), lanes_of([low, jnp.zeros_like(low)])])
        for first in range(0, FACES, 2):
            count = min(2, FACES - first)
            width = count * LANES
            halves = [split(fine_ref[xy * FACES + first + i]) for i in range(count)]
            right = rows_of([lanes_of([h[i] for h in halves]) for i in range(2)])
            out = dot(left, right).reshape(2, 4, 2, CDOF, width)
            out = out[0] + out[1]
            q = jnp.where(wide_lane[:, :, :width] < DOF, out[:, 0], out[:, 1]).reshape(DOF, width)
            high_q, low_q = split(q)
            for i in range(count):
                cut = slice(i * LANES, (i + 1) * LANES)
                rows_scr[xy * FACES + first + i] = lanes_of([high_q[:, cut], low_q[:, cut]])

    for side in range(2):
        outer_ref[side] = rows_scr[side * FACES + 1]
        outer_ref[2 + side] = rows_scr[(2 + side) * FACES + 2]
        outer_ref[4 + side] = rows_scr[2 * side * FACES + 3]
        outer_ref[6 + side] = rows_scr[(2 * side + 1) * FACES + 4]
    low = rows_of([rows_scr[xy * FACES + 5, :CDOF] for xy in range(columns)])
    high = rows_of([rows_scr[xy * FACES + 6, DOF - CDOF :] for xy in range(columns)])
    layers = [jnp.where(gz == 0, high, low)] if group_size == 2 else [low, high]
    for i, layer in enumerate(layers):
        layer_ref[i] = layer
        both = layer[:, :LANES].astype(F32) + layer[:, LANES:].astype(F32)
        layer_send[i * DOF : i * DOF + DOF // 2] = folded(both + pltpu.roll(both, DOF, 1))
        layer_send[i * DOF + DOF // 2 : (i + 1) * DOF] = folded(blocks_scr[columns + i])

    aggs = (agg_ref[...] + 1).reshape(nx * ny, nz).astype(F32).astype(BF16)
    width = 5 * LANES
    z_row, z_lane = iota((nz, width), 0), iota((nz, width), 1)
    kind, place = z_lane // LANES, z_lane % LANES
    slot, face = place // CDOF % 4, (1 - gz) if group_size == 2 else place // DOF
    z_off = jnp.where(kind == 0, slot, jnp.where(kind == 1, slot + 1, slot - 1))
    z_off = jnp.where(kind == 3, face * (bz - 1), jnp.where(kind == 4, face * (bz + 1) - 1, z_off))
    by_lane = dot(aggs, ones_where(z_row == gz * bz + z_off)).astype(BF16)
    count = 24
    r = iota((count, nx * ny), 0)
    own_x, own_y = r // 2 % 2, r % 2
    group = r // 4
    dx = jnp.where(group == 1, 1 - own_x, own_x)
    dy = jnp.where(group == 2, 1 - own_y, own_y)
    dx = jnp.where(group == 4, own_x * (bx + 1) - 1, jnp.where(group == 5, own_y, dx))
    dy = jnp.where(group == 4, own_y, jnp.where(group == 5, own_x * (by + 1) - 1, dy))
    px, py = gx * bx + dx, gy * by + dy
    inside = (px >= 0) & (px < nx) & (py >= 0) & (py < ny) & (group != 3)
    at = jnp.where(inside, px * ny + py, -1)
    table = dot(ones_where(iota((count, nx * ny), 1) == at), by_lane).astype(jnp.int32)
    owners = owner_ref[0]
    slots = iota((1, AGGS), 1)
    rank = jnp.zeros((1, AGGS), jnp.int32)
    for a in range(AGGS - 1):
        rank += jnp.where((slots > a) & (owners == owners[:, a : a + 1]), 1, 0)
    own = table[:16]
    owner = jnp.zeros_like(own)
    ranks = jnp.zeros_like(own)
    for a in range(AGGS):
        owner = jnp.where(own == a + 1, owners[:, a : a + 1], owner)
        ranks = jnp.where(own == a + 1, rank[:, a : a + 1], ranks)
    inner_base = owner * (AGGS * rows_each) + ranks
    outer_base = owner * (AGGS * AGGS) + gz * rows_each + ranks

    def cut(array, row, part):
        return array[row : row + 1, part * LANES : (part + 1) * LANES]

    first_half = iota((1, LANES), 1) < DOF
    level = iota((1, LANES), 1) // CDOF % 4

    def pair(array, one, two, part=0):
        return jnp.where(first_half, cut(array, one, part), cut(array, two, part))

    labels = []
    for row, part, valid in ((0, 0, None), (4, 0, None), (8, 0, None), (0, 1, level < bz - 1), (0, 2, level > 0)):
        for x in range(bx):
            label = pair(inner_base, row + 2 * x, row + 2 * x + 1, part)
            label += (pair(table, 2 * x, 2 * x + 1) - 1) * rows_each
            labels.append(label if valid is None else jnp.where(valid, label, -1))
    outer_labels = []
    for k, pick in enumerate(((0, 1), (2, 3), (0, 2), (1, 3))):
        other = pair(table, 16 + 2 * k, 17 + 2 * k)
        label = pair(outer_base, *pick) + (other - 1) * AGGS
        outer_labels.append(jnp.where(other > 0, label, -1))

    def by_column(array, part):
        value = cut(array, 0, part)
        for xy in range(1, columns):
            value = jnp.where(level == xy, cut(array, xy, part), value)
        return value

    other = by_column(table, 4)
    label = by_column(outer_base + owner * (AGGS * AGGS), 3) + (other - 1) * AGGS
    label += (1 - gz) * AGGS * AGGS if group_size == 2 else jnp.where(first_half, 0, AGGS * AGGS)
    outer_labels.append(jnp.where(other > 0, label, -1))
    label_ref[...] = rows_of(outer_labels + [jnp.full((3, LANES), -1, jnp.int32)]).astype(F32)

    pieces = [[] for _ in range(5)]
    for x in range(bx):
        for y in range(by):
            xy = x * by + y
            sources = (
                (xy * FACES, 0),
                (((1 - x) * by + y) * FACES + (2 if x else 1), 0),
                ((x * by + 1 - y) * FACES + (4 if y else 3), 0),
                (xy * FACES + 5, -1),
                (xy * FACES + 6, 1),
            )
            product = blocks_of(rows_of([rows_scr[index] for index, _ in sources]), factors[xy])
            for i, (_, shift) in enumerate(sources):
                pieces[i].append(diagonal(product[i * DOF : (i + 1) * DOF], shift))
    half = iota((CDOF, LANES), 1) < DOF
    packs = [jnp.where(half, p[2 * x], p[2 * x + 1]) for p in pieces for x in range(bx)]
    flat = flatten(packs)
    chosen = [choose(label, 0, AGGS * AGGS) for label in labels]
    inner_ref[...] = dot(lanes_of([c for c in chosen for _ in range(2)]), rows_of(flat))


def outer_kernel(group_size, outer_ref, inner_ref, label_ref, layer_send, odd_y, even_y, odd_x, even_x, *refs):
    gz = lax.axis_index("gz")
    sends, blocks_scr = refs[:-1], refs[-1]
    place = 0
    for axis, even, odd, low, high in (("gx", even_x, odd_x, (2, 3), (0, 1)), ("gy", even_y, odd_y, (1, 3), (0, 2))):
        second = lax.rem(lax.axis_index(axis), 2) == 1
        for one, two, columns in ((even, odd, low), (odd, even, high)):
            for xy in columns:
                rows = [pl.ds(z, 8, stride=4) for z in range(4)]
                spread_blocks(blocks_scr.at[place], [jnp.where(second, one[xy, z, :], two[xy, z, :]) for z in rows])
                place += 1
    pieces = [diagonal(blocks_of(outer_ref[i], factor_of(blocks_scr[i])), 0) for i in range(8)]
    half = iota((CDOF, LANES), 1) < DOF
    packs = [jnp.where(half, pieces[i], pieces[i + 1]) for i in range(0, len(pieces), 2)]
    tail = rows_of(packs + [label_ref[...], layer_send[...]])
    count = AGGS * AGGS // group_size
    for shift, send in enumerate(sends, 1):
        target = lax.rem(gz + shift, group_size)
        block = inner_ref[pl.ds(pl.multiple_of(target * count, count), count)]
        send[:count] = block[:, :LANES]
        send[count : 2 * count] = block[:, LANES:]
        send[2 * count :] = tail


def parts_of(tail):
    packs = [tail[k * CDOF : (k + 1) * CDOF] for k in range(4)]
    labels = tail[DOF : DOF + 8].astype(jnp.int32)
    halves = [tail[at : at + DOF // 2] for at in range(DOF + 8, tail.shape[0], DOF // 2)]
    return packs, labels, halves[::2], halves[1::2]


def own_kernel(group_size, inner_ref, send_ref, out_ref, factor_ref):
    gz = lax.axis_index("gz")
    rows_each = AGGS // group_size
    count = AGGS * AGGS // group_size
    mine = iota((AGGS, WIDE), 0) // rows_each == gz
    block = inner_ref[pl.ds(pl.multiple_of(gz * count, count), count)]
    for c in range(AGGS):
        part = rows_of([block[c * rows_each : (c + 1) * rows_each]] * group_size)
        out_ref[:, c * WIDE : (c + 1) * WIDE] = jnp.where(mine, part, 0.0)
    packs, labels, _, blocks = parts_of(send_ref[2 * count :])
    for i, part in enumerate(blocks):
        factor_ref[i] = factor_of(unfolded(part))
    for k, flat in enumerate(flatten(packs)):
        chosen = choose(labels[k : k + 1], gz * AGGS * AGGS, AGGS * AGGS)
        value = dot(lanes_of([chosen] * 2), flat)
        for c in range(AGGS):
            at = ((k + 1) * AGGS + c) * WIDE
            out_ref[:, at : at + WIDE] = value[c * AGGS : (c + 1) * AGGS]
    out_ref[:, 5 * AGGS * WIDE :] = jnp.zeros((AGGS, 2 * AGGS * WIDE), F32)


def final_kernel(group_size, own_ref, factor_ref, layer_ref, label_ref, *refs):
    received, out_hbm, out_ref, sems = refs[:-3], refs[-3], refs[-2], refs[-1]
    gz = lax.axis_index("gz")
    rows_each = AGGS // group_size
    count = AGGS * AGGS // group_size
    copies = []

    def send_out(face):
        part = pl.ds(face * AGGS * WIDE, AGGS * WIDE)
        copies.append(pltpu.make_async_copy(out_ref.at[:, part], out_hbm.at[:, part], sems.at[face]))
        copies[-1].start()

    tails = [parts_of(ref[2 * count :]) for ref in received]
    left = iota((DOF, LANES), 1) < DOF
    rows = [[layer_ref[i] for i in range(layer_ref.shape[0])]]
    factors = [[factor_ref[i] for i in range(layer_ref.shape[0])]]
    for _, _, layers, blocks in tails:
        rows.append([lanes_of(split(jnp.where(left, unfolded(layer), 0.0))) for layer in layers])
        factors.append([factor_of(unfolded(part)) for part in blocks])
    layer_labels = [label_ref[4:5].astype(jnp.int32)] + [labels[4:5] for _, labels, _, _ in tails]
    half = iota((CDOF, LANES), 1) < DOF
    if group_size == 2:
        pieces = [diagonal(blocks_of(rows[i][0], factors[1 - i][0]), 0) for i in range(2)]
        layer_packs = [jnp.where(half, *pieces)]
        layer_labels = [jnp.where(half[:1], *layer_labels)]
    else:
        low, high = {}, {}
        for i in range(group_size):
            above = (i - 1) % group_size
            high[i] = diagonal(blocks_of(rows[i][1], factors[above][0]), 0)
            low[above] = diagonal(blocks_of(rows[above][0], factors[i][1]), 0)
        layer_packs = [jnp.where(half, low[i], high[i]) for i in range(group_size)]

    brick = iota((AGGS, LANES), 0) // rows_each
    for c in range(AGGS):
        for h in range(2):
            at = slice((2 * c + h) * LANES, (2 * c + h + 1) * LANES)
            value = own_ref[:, at]
            for shift, ref in enumerate(received, 1):
                part = ref[h * count + c * rows_each : h * count + (c + 1) * rows_each]
                theirs = lax.rem(gz - shift + group_size, group_size)
                value = jnp.where(brick == theirs, rows_of([part] * group_size), value)
            out_ref[:, at] = value
    send_out(0)
    flat = flatten([packs[k] for k in range(4) for packs, _, _, _ in tails]) + flatten(layer_packs)
    size = AGGS * AGGS
    for k in range(4):
        chosen = [choose(labels[k : k + 1], gz * size, size) for _, labels, _, _ in tails]
        parts = flat[k * len(tails) : (k + 1) * len(tails)]
        value = dot(lanes_of([c for c in chosen for _ in range(2)]), rows_of(parts))
        for c in range(AGGS):
            cut = slice(((k + 1) * AGGS + c) * WIDE, ((k + 1) * AGGS + c + 1) * WIDE)
            out_ref[:, cut] = own_ref[:, cut] + value[c * AGGS : (c + 1) * AGGS]
        send_out(k + 1)
    chosen = [choose(label, gz * 2 * size, 2 * size) for label in layer_labels]
    value = dot(lanes_of([c for c in chosen for _ in range(2)]), rows_of(flat[4 * len(tails) :]))
    for c in range(2 * AGGS):
        cut = slice((5 * AGGS + c) * WIDE, (5 * AGGS + c + 1) * WIDE)
        out_ref[:, cut] = value[c * AGGS : (c + 1) * AGGS]
    send_out(5)
    send_out(6)
    for copy in copies:
        copy.wait()


def matching(sizes, along, first):
    def partner(place):
        i = (place[along] - first) ^ 1
        moved = list(place)
        if 0 <= i + first < sizes[along] and place[along] >= first:
            moved[along] = i + first
        elif place[1 - along] ^ 1 < sizes[1 - along]:
            moved[1 - along] = place[1 - along] ^ 1
        return moved[0] * sizes[1] + moved[1]

    return [(x * sizes[1] + y, partner((x, y))) for x in range(sizes[0]) for y in range(sizes[1])]


def rotation(count, step):
    return [(i, (i + step) % count) for i in range(count)]


def shards(fine_blocks, prolong, agg_map, owner_map):
    bx, by, bz = fine_blocks.shape[:3]
    columns = bx * by
    group_size = lax.axis_size("gz")
    fine = fine_blocks.transpose(0, 1, 3, 2, 4).reshape(columns * FACES, bz, 32, LANES)
    fine = fine.transpose(0, 2, 1, 3).reshape(columns * FACES, 32 * bz, LANES)
    base = prolong.reshape(columns, bz, 8, LANES).transpose(0, 2, 1, 3).reshape(columns, 8 * bz, LANES)
    tick = pl.pallas_call(
        tick_kernel,
        out_shape=pltpu.VMEM((8, LANES), F32),
        out_specs=VMEM,
        cost_estimate=pl.CostEstimate(flops=int(5e9), bytes_accessed=int(5e7), transcendentals=0),
    )()
    sizes = lax.axis_size("gx"), lax.axis_size("gy")
    even_x, odd_x, even_y, odd_y = [
        lax.ppermute(base, ("gx", "gy"), matching(sizes, along, first)) for along in range(2) for first in range(2)
    ]
    halos = [odd_y, even_y, odd_x, even_x]
    layers = 1 if group_size == 2 else 2
    params = pltpu.CompilerParams(vmem_limit_bytes=32 * 1024 * 1024)
    shape = jax.ShapeDtypeStruct
    outer, inner, labels, layer_rows, layer_send = pl.pallas_call(
        functools.partial(local_kernel, (bx, by, bz), group_size),
        out_shape=[
            shape((8, DOF, WIDE), BF16),
            shape((AGGS * AGGS, WIDE), F32),
            shape((8, LANES), F32),
            shape((layers, DOF, WIDE), BF16),
            shape((layers * DOF, LANES), F32),
        ],
        in_specs=[VMEM] * 5,
        out_specs=[VMEM] * 5,
        scratch_shapes=[
            pltpu.VMEM((columns * FACES, DOF, WIDE), BF16),
            pltpu.VMEM((columns + layers, DOF, LANES), F32),
        ],
        compiler_params=params,
        cost_estimate=pl.CostEstimate(flops=int(2e9), bytes_accessed=int(4e6), transcendentals=0),
    )(
        *(pltpu.with_memory_space_constraint(a, pltpu.VMEM) for a in (agg_map, owner_map, base, fine)),
        tick,
    )
    size = 2 * AGGS * AGGS // group_size + 4 * CDOF + 8 + layers * DOF
    sends = pl.pallas_call(
        functools.partial(outer_kernel, group_size),
        out_shape=[shape((size, LANES), F32)] * (group_size - 1),
        in_specs=[VMEM] * 8,
        out_specs=[VMEM] * (group_size - 1),
        scratch_shapes=[pltpu.VMEM((8, DOF, LANES), F32)],
        compiler_params=params,
    )(outer, inner, labels, layer_send, *halos)
    received = [
        lax.ppermute(send, "gz", rotation(group_size, shift)) for shift, send in enumerate(sends, 1)
    ]
    full = shape((AGGS, FACES * AGGS * CDOF * CDOF), F32)
    own, factor = pl.pallas_call(
        functools.partial(own_kernel, group_size),
        out_shape=[full, shape((layers, WIDE, LANES), BF16)],
        in_specs=[VMEM, VMEM],
        out_specs=[VMEM, VMEM],
        compiler_params=params,
        cost_estimate=pl.CostEstimate(flops=int(1e9), bytes_accessed=int(2e6), transcendentals=0),
    )(inner, sends[0])
    out = pl.pallas_call(
        functools.partial(final_kernel, group_size),
        out_shape=full,
        in_specs=[VMEM] * (3 + group_size),
        out_specs=HBM,
        scratch_shapes=[pltpu.VMEM(full.shape, F32), pltpu.SemaphoreType.DMA((FACES,))],
        compiler_params=params,
    )(own, factor, layer_rows, labels, *received)
    return out[None, None]


def solution(mesh):
    placed = (P("gx", "gy", "gz", None, None), P("gx", "gy", "gz", None), P(), P("gx", "gy", "gz"))
    return jax.shard_map(
        shards, mesh=mesh, in_specs=placed, out_specs=P("gx", "gy", "gz", None), check_vma=False
    )
```

```python
import functools

import jax
import jax.numpy as jnp
from jax import lax
from jax.experimental import pallas as pl
from jax.experimental.pallas import tpu as pltpu
from jax.sharding import PartitionSpec as P

DOF = 64
CDOF = 16
AGGS = 8
FACES = 7
LANES = 128
WIDE = 2 * LANES
F32 = jnp.float32
BF16 = jnp.bfloat16
VMEM = pl.BlockSpec(memory_space=pltpu.VMEM)
HBM = pl.BlockSpec(memory_space=pltpu.HBM)


def iota(shape, dim):
    return lax.broadcasted_iota(jnp.int32, shape, dim)


def dot(a, b):
    return lax.dot_general(a, b, (((1,), (0,)), ((), ())), preferred_element_type=F32)


def split(x):
    high = x.astype(BF16)
    return high, (x - high.astype(F32)).astype(BF16)


def ones_where(mask):
    return jnp.where(mask, 1.0, 0.0).astype(BF16)


def rows_of(parts):
    return jnp.concatenate(parts, axis=0)


def lanes_of(parts):
    return jnp.concatenate(parts, axis=1)


def spread_blocks(out_ref, pieces):
    slot = iota((8, LANES), 1) // CDOF
    for b in range(8):
        value = pltpu.roll(pieces[0], -b * CDOF % LANES, 1)
        for i in range(1, 4):
            value = jnp.where(slot == i, pltpu.roll(pieces[i], (i - b) * CDOF % LANES, 1), value)
        out_ref[pl.ds(b, 8, stride=8), :] = value


def factor_of(full):
    left = iota((DOF, LANES), 1) < DOF
    high = full.astype(BF16).astype(F32)
    both = jnp.where(left, high, pltpu.roll(full - high, DOF, 1)).astype(BF16)
    first = jnp.where(left, high, 0.0).astype(BF16)
    return rows_of([both, both, first, first])


def folded(full):
    half = DOF // 2
    return jnp.where(iota((half, LANES), 1) < DOF, full[:half], pltpu.roll(full[half:], DOF, 1))


def unfolded(part):
    left = iota((DOF // 2, LANES), 1) < DOF
    turned = pltpu.roll(part, DOF, 1)
    return rows_of([jnp.where(left, part, turned), jnp.where(left, turned, part)])


def blocks_of(rows, factor):
    out = dot(rows, factor)
    return out + pltpu.roll(out, DOF, 1)


def diagonal(product, shift):
    keep = iota((DOF, LANES), 0) // CDOF + shift == iota((DOF, LANES), 1) // CDOF % 4
    kept = jnp.where(keep, product, 0.0).reshape(4, CDOF, LANES)
    return (kept[0] + kept[1]) + (kept[2] + kept[3])


def flatten(packs):
    spread = ones_where(iota((LANES, WIDE), 0) % CDOF == iota((LANES, WIDE), 1) % CDOF)
    element = ones_where(iota((LANES, LANES), 0) // CDOF == iota((LANES, LANES), 1) // CDOF)
    row = ones_where(iota((WIDE, WIDE), 0) % CDOF == iota((WIDE, WIDE), 1) // CDOF)
    wide = [rows_of([part] * 8) * element for pack in packs for part in split(pack)]
    flat = dot(rows_of(wide), spread).astype(BF16)
    return [flat[i * WIDE : (i + 1) * WIDE] * row for i in range(len(packs))]


def choose(labels, base, count):
    return ones_where(iota((count, LANES), 0) + base == labels)


def tick_kernel(out_ref):
    out_ref[...] = jnp.ones(out_ref.shape, F32)


def local_kernel(shape, group_size, agg_ref, owner_ref, prolong_ref, fine_ref, tick_ref,
                 outer_ref, inner_ref, layer_ref, *refs):
    bx, by, bz = shape
    columns = bx * by
    rows_each = AGGS // group_size
    sends, (rows_scr, blocks_scr) = refs[:-2], refs[-2:]
    gx, gy, gz = lax.axis_index("gx"), lax.axis_index("gy"), lax.axis_index("gz")
    nx, ny, nz = agg_ref.shape

    lane = iota((32, LANES), 1)
    sub = iota((32, LANES), 0) % 4
    p0, p1 = iota((LANES, LANES), 0), iota((LANES, LANES), 1)
    permute = ones_where((p0 % 4 == p1 % 4) & (p0 // 32 == p1 // 4 % 4) & (p0 // 4 % 8 == p1 // 16))
    turned = []
    for xy in range(columns):
        raw = prolong_ref[xy]
        rolled = [raw] + [pltpu.roll(raw, 32 * m, 1) for m in range(1, 4)]
        stacked = []
        for tau in range(4):
            part = jnp.zeros_like(raw)
            for z in range(4):
                part = jnp.where((sub == z) & (lane // 32 == z), rolled[(z - tau) % 4], part)
            stacked.append(part)
        turned += split(rows_of(stacked).T)
    lefts = dot(rows_of(turned), permute).astype(BF16)
    for xy in range(columns):
        spread_blocks(blocks_scr.at[xy], [prolong_ref[xy, pl.ds(z, 8, stride=bz), :] for z in range(bz)])
    low, high = ([prolong_ref[xy, pl.ds(z, 8, stride=bz), :] for xy in range(columns)] for z in (0, bz - 1))
    layers = [[jnp.where(gz == 0, h, l) for l, h in zip(low, high)]] if group_size == 2 else [low, high]
    for i, layer in enumerate(layers):
        spread_blocks(blocks_scr.at[columns + i], layer)
    factors = [factor_of(blocks_scr[xy]) for xy in range(columns)]

    wide_lane = iota((4, CDOF, WIDE), 2) % LANES
    for xy in range(columns):
        high = lefts[xy * WIDE : xy * WIDE + LANES]
        low = lefts[xy * WIDE + LANES : (xy + 1) * WIDE]
        left = rows_of([lanes_of([high, high]), lanes_of([low, jnp.zeros_like(low)])])
        for first in range(0, FACES, 2):
            count = min(2, FACES - first)
            width = count * LANES
            halves = [split(fine_ref[xy * FACES + first + i]) for i in range(count)]
            right = rows_of([lanes_of([h[i] for h in halves]) for i in range(2)])
            out = dot(left, right).reshape(2, 4, 2, CDOF, width)
            out = out[0] + out[1]
            q = jnp.where(wide_lane[:, :, :width] < DOF, out[:, 0], out[:, 1]).reshape(DOF, width)
            high_q, low_q = split(q)
            for i in range(count):
                cut = slice(i * LANES, (i + 1) * LANES)
                rows_scr[xy * FACES + first + i] = lanes_of([high_q[:, cut], low_q[:, cut]])

    for side in range(2):
        outer_ref[side] = rows_scr[side * FACES + 1]
        outer_ref[2 + side] = rows_scr[(2 + side) * FACES + 2]
        outer_ref[4 + side] = rows_scr[2 * side * FACES + 3]
        outer_ref[6 + side] = rows_scr[(2 * side + 1) * FACES + 4]
    low = rows_of([rows_scr[xy * FACES + 5, :CDOF] for xy in range(columns)])
    high = rows_of([rows_scr[xy * FACES + 6, DOF - CDOF :] for xy in range(columns)])
    layers = [jnp.where(gz == 0, high, low)] if group_size == 2 else [low, high]
    layer_parts = []
    for i, layer in enumerate(layers):
        layer_ref[i] = layer
        both = layer[:, :LANES].astype(F32) + layer[:, LANES:].astype(F32)
        for part in (both + pltpu.roll(both, DOF, 1), blocks_scr[columns + i]):
            layer_parts.append(folded(part))

    aggs = (agg_ref[...] + 1).reshape(nx * ny, nz).astype(F32).astype(BF16)
    width = 5 * LANES
    z_row, z_lane = iota((nz, width), 0), iota((nz, width), 1)
    kind, place = z_lane // LANES, z_lane % LANES
    slot, face = place // CDOF % 4, (1 - gz) if group_size == 2 else place // DOF
    z_off = jnp.where(kind == 0, slot, jnp.where(kind == 1, slot + 1, slot - 1))
    z_off = jnp.where(kind == 3, face * (bz - 1), jnp.where(kind == 4, face * (bz + 1) - 1, z_off))
    by_lane = dot(aggs, ones_where(z_row == gz * bz + z_off)).astype(BF16)
    count = 24
    r = iota((count, nx * ny), 0)
    own_x, own_y = r // 2 % 2, r % 2
    group = r // 4
    dx = jnp.where(group == 1, 1 - own_x, own_x)
    dy = jnp.where(group == 2, 1 - own_y, own_y)
    dx = jnp.where(group == 4, own_x * (bx + 1) - 1, jnp.where(group == 5, own_y, dx))
    dy = jnp.where(group == 4, own_y, jnp.where(group == 5, own_x * (by + 1) - 1, dy))
    px, py = gx * bx + dx, gy * by + dy
    inside = (px >= 0) & (px < nx) & (py >= 0) & (py < ny) & (group != 3)
    at = jnp.where(inside, px * ny + py, -1)
    table = dot(ones_where(iota((count, nx * ny), 1) == at), by_lane).astype(jnp.int32)
    owners = owner_ref[0]
    slots = iota((1, AGGS), 1)
    rank = jnp.zeros((1, AGGS), jnp.int32)
    for a in range(AGGS - 1):
        rank += jnp.where((slots > a) & (owners == owners[:, a : a + 1]), 1, 0)
    own = table[:16]
    owner = jnp.zeros_like(own)
    ranks = jnp.zeros_like(own)
    for a in range(AGGS):
        owner = jnp.where(own == a + 1, owners[:, a : a + 1], owner)
        ranks = jnp.where(own == a + 1, rank[:, a : a + 1], ranks)
    inner_base = owner * (AGGS * rows_each) + ranks
    outer_base = owner * (AGGS * AGGS) + gz * rows_each + ranks

    def cut(array, row, part):
        return array[row : row + 1, part * LANES : (part + 1) * LANES]

    first_half = iota((1, LANES), 1) < DOF
    level = iota((1, LANES), 1) // CDOF % 4

    def pair(array, one, two, part=0):
        return jnp.where(first_half, cut(array, one, part), cut(array, two, part))

    labels = []
    for row, part, valid in ((0, 0, None), (4, 0, None), (8, 0, None), (0, 1, level < bz - 1), (0, 2, level > 0)):
        for x in range(bx):
            label = pair(inner_base, row + 2 * x, row + 2 * x + 1, part)
            label += (pair(table, 2 * x, 2 * x + 1) - 1) * rows_each
            labels.append(label if valid is None else jnp.where(valid, label, -1))
    outer_labels = []
    for k, pick in enumerate(((0, 1), (2, 3), (0, 2), (1, 3))):
        other = pair(table, 16 + 2 * k, 17 + 2 * k)
        label = pair(outer_base, *pick) + (other - 1) * AGGS
        outer_labels.append(jnp.where(other > 0, label, -1))

    def by_column(array, part):
        value = cut(array, 0, part)
        for xy in range(1, columns):
            value = jnp.where(level == xy, cut(array, xy, part), value)
        return value

    other = by_column(table, 4)
    label = by_column(outer_base + owner * (AGGS * AGGS), 3) + (other - 1) * AGGS
    label += (1 - gz) * AGGS * AGGS if group_size == 2 else jnp.where(first_half, 0, AGGS * AGGS)
    outer_labels.append(jnp.where(other > 0, label, -1))
    outer_labels = rows_of(outer_labels + [jnp.full((3, LANES), -1, jnp.int32)]).astype(F32)

    pieces = [[] for _ in range(5)]
    for x in range(bx):
        for y in range(by):
            xy = x * by + y
            sources = (
                (xy * FACES, 0),
                (((1 - x) * by + y) * FACES + (2 if x else 1), 0),
                ((x * by + 1 - y) * FACES + (4 if y else 3), 0),
                (xy * FACES + 5, -1),
                (xy * FACES + 6, 1),
            )
            product = blocks_of(rows_of([rows_scr[index] for index, _ in sources]), factors[xy])
            for i, (_, shift) in enumerate(sources):
                pieces[i].append(diagonal(product[i * DOF : (i + 1) * DOF], shift))
    half = iota((CDOF, LANES), 1) < DOF
    packs = [jnp.where(half, p[2 * x], p[2 * x + 1]) for p in pieces for x in range(bx)]
    flat = flatten(packs)
    chosen = [choose(label, 0, AGGS * AGGS) for label in labels]
    inner_ref[...] = dot(lanes_of([c for c in chosen for _ in range(2)]), rows_of(flat))
    count = AGGS * AGGS // group_size
    for shift, send in enumerate(sends, 1):
        target = lax.rem(gz + shift, group_size)
        block = inner_ref[pl.ds(pl.multiple_of(target * count, count), count)]
        send[:count] = block[:, :LANES]
        send[count : 2 * count] = block[:, LANES:]
        send[2 * count :] = rows_of([outer_labels] + layer_parts)


def outer_kernel(outer_ref, odd_y, even_y, odd_x, even_x, packs_ref, blocks_scr):
    place = 0
    for axis, even, odd, low, high in (("gx", even_x, odd_x, (2, 3), (0, 1)), ("gy", even_y, odd_y, (1, 3), (0, 2))):
        second = lax.rem(lax.axis_index(axis), 2) == 1
        for one, two, columns in ((even, odd, low), (odd, even, high)):
            for xy in columns:
                rows = [pl.ds(z, 8, stride=4) for z in range(4)]
                spread_blocks(blocks_scr.at[place], [jnp.where(second, one[xy, z, :], two[xy, z, :]) for z in rows])
                place += 1
    pieces = [diagonal(blocks_of(outer_ref[i], factor_of(blocks_scr[i])), 0) for i in range(8)]
    half = iota((CDOF, LANES), 1) < DOF
    packs_ref[...] = rows_of([jnp.where(half, pieces[i], pieces[i + 1]) for i in range(0, 8, 2)])


def parts_of(tail):
    halves = [tail[at : at + DOF // 2] for at in range(8, tail.shape[0], DOF // 2)]
    return tail[:8].astype(jnp.int32), halves[::2], halves[1::2]


def own_kernel(group_size, inner_ref, layer_ref, send_ref, packs_ref, *refs):
    received, out_ref = refs[:-1], refs[-1]
    gz = lax.axis_index("gz")
    rows_each = AGGS // group_size
    count = AGGS * AGGS // group_size
    size = AGGS * AGGS
    own_labels, _, own_blocks = parts_of(send_ref[2 * count :])
    tails = [parts_of(ref[2 * count :]) for ref in received]

    left = iota((DOF, LANES), 1) < DOF
    rows = [[layer_ref[i] for i in range(layer_ref.shape[0])]]
    factors = [[factor_of(unfolded(part)) for part in own_blocks]]
    for _, layers, blocks in tails:
        rows.append([lanes_of(split(jnp.where(left, unfolded(layer), 0.0))) for layer in layers])
        factors.append([factor_of(unfolded(part)) for part in blocks])
    layer_labels = [own_labels[4:5]] + [labels[4:5] for labels, _, _ in tails]
    half = iota((CDOF, LANES), 1) < DOF
    if group_size == 2:
        pieces = [diagonal(blocks_of(rows[i][0], factors[1 - i][0]), 0) for i in range(2)]
        layer_packs = [jnp.where(half, *pieces)]
        layer_labels = [jnp.where(half[:1], *layer_labels)]
    else:
        low, high = {}, {}
        for i in range(group_size):
            above = (i - 1) % group_size
            high[i] = diagonal(blocks_of(rows[i][1], factors[above][0]), 0)
            low[above] = diagonal(blocks_of(rows[above][0], factors[i][1]), 0)
        layer_packs = [jnp.where(half, low[i], high[i]) for i in range(group_size)]

    flat = flatten([packs_ref[k * CDOF : (k + 1) * CDOF] for k in range(4)] + layer_packs)
    for k in range(4):
        chosen = choose(own_labels[k : k + 1], gz * size, size)
        value = dot(lanes_of([chosen] * 2), flat[k])
        for c in range(AGGS):
            at = ((k + 1) * AGGS + c) * WIDE
            out_ref[:, at : at + WIDE] = value[c * AGGS : (c + 1) * AGGS]
    chosen = [choose(label, gz * 2 * size, 2 * size) for label in layer_labels]
    value = dot(lanes_of([c for c in chosen for _ in range(2)]), rows_of(flat[4:]))
    for c in range(2 * AGGS):
        at = (5 * AGGS + c) * WIDE
        out_ref[:, at : at + WIDE] = value[c * AGGS : (c + 1) * AGGS]

    block = inner_ref[pl.ds(pl.multiple_of(gz * count, count), count)]
    brick = iota((AGGS, LANES), 0) // rows_each
    for c in range(AGGS):
        at = slice(c * rows_each, (c + 1) * rows_each)
        for h in range(2):
            value = rows_of([block[at, h * LANES : (h + 1) * LANES]] * group_size)
            for shift, ref in enumerate(received, 1):
                part = ref[h * count + c * rows_each : h * count + (c + 1) * rows_each]
                theirs = lax.rem(gz - shift + group_size, group_size)
                value = jnp.where(brick == theirs, rows_of([part] * group_size), value)
            out_ref[:, (2 * c + h) * LANES : (2 * c + h + 1) * LANES] = value


def final_kernel(group_size, own_ref, *refs):
    packs, firsts, (out_hbm, out_ref, sems) = refs[: group_size - 1], refs[group_size - 1 : -3], refs[-3:]
    gz = lax.axis_index("gz")
    count = AGGS * AGGS // group_size
    size = AGGS * AGGS
    copies = []

    def send_out(source, first, last):
        part = pl.ds(first * AGGS * WIDE, (last - first) * AGGS * WIDE)
        copies.append(pltpu.make_async_copy(source.at[:, part], out_hbm.at[:, part], sems.at[first]))
        copies[-1].start()

    send_out(own_ref, 0, 1)
    send_out(own_ref, 5, 7)
    flat = flatten([pack[k * CDOF : (k + 1) * CDOF] for k in range(4) for pack in packs])
    labels = [ref[2 * count : 2 * count + 8].astype(jnp.int32) for ref in firsts]
    for k in range(4):
        chosen = [choose(label[k : k + 1], gz * size, size) for label in labels]
        parts = flat[k * len(packs) : (k + 1) * len(packs)]
        value = dot(lanes_of([c for c in chosen for _ in range(2)]), rows_of(parts))
        for c in range(AGGS):
            cut = slice(((k + 1) * AGGS + c) * WIDE, ((k + 1) * AGGS + c + 1) * WIDE)
            out_ref[:, cut] = own_ref[:, cut] + value[c * AGGS : (c + 1) * AGGS]
        send_out(out_ref, k + 1, k + 2)
    for copy in copies:
        copy.wait()


def matching(sizes, along, first):
    def partner(place):
        i = (place[along] - first) ^ 1
        moved = list(place)
        if 0 <= i + first < sizes[along] and place[along] >= first:
            moved[along] = i + first
        elif place[1 - along] ^ 1 < sizes[1 - along]:
            moved[1 - along] = place[1 - along] ^ 1
        return moved[0] * sizes[1] + moved[1]

    return [(x * sizes[1] + y, partner((x, y))) for x in range(sizes[0]) for y in range(sizes[1])]


def rotation(count, step):
    return [(i, (i + step) % count) for i in range(count)]


def shards(fine_blocks, prolong, agg_map, owner_map):
    bx, by, bz = fine_blocks.shape[:3]
    columns = bx * by
    group_size = lax.axis_size("gz")
    fine = fine_blocks.transpose(0, 1, 3, 2, 4).reshape(columns * FACES, bz, 32, LANES)
    fine = fine.transpose(0, 2, 1, 3).reshape(columns * FACES, 32 * bz, LANES)
    base = prolong.reshape(columns, bz, 8, LANES).transpose(0, 2, 1, 3).reshape(columns, 8 * bz, LANES)
    tick = pl.pallas_call(
        tick_kernel,
        out_shape=pltpu.VMEM((8, LANES), F32),
        out_specs=VMEM,
        cost_estimate=pl.CostEstimate(flops=int(5e9), bytes_accessed=int(5e7), transcendentals=0),
    )()
    sizes = lax.axis_size("gx"), lax.axis_size("gy")
    even_x, odd_x, even_y, odd_y = [
        lax.ppermute(base, ("gx", "gy"), matching(sizes, along, first)) for along in range(2) for first in range(2)
    ]
    halos = [odd_y, even_y, odd_x, even_x]
    layers = 1 if group_size == 2 else 2
    params = pltpu.CompilerParams(vmem_limit_bytes=32 * 1024 * 1024)
    shape = jax.ShapeDtypeStruct
    size = 2 * AGGS * AGGS // group_size + 8 + layers * DOF
    outer, inner, layer_rows, *firsts = pl.pallas_call(
        functools.partial(local_kernel, (bx, by, bz), group_size),
        out_shape=[
            shape((8, DOF, WIDE), BF16),
            shape((AGGS * AGGS, WIDE), F32),
            shape((layers, DOF, WIDE), BF16),
        ]
        + [shape((size, LANES), F32)] * (group_size - 1),
        in_specs=[VMEM] * 5,
        out_specs=[VMEM] * (2 + group_size),
        scratch_shapes=[
            pltpu.VMEM((columns * FACES, DOF, WIDE), BF16),
            pltpu.VMEM((columns + layers, DOF, LANES), F32),
        ],
        compiler_params=params,
        cost_estimate=pl.CostEstimate(flops=int(2e9), bytes_accessed=int(4e6), transcendentals=0),
    )(
        *(pltpu.with_memory_space_constraint(a, pltpu.VMEM) for a in (agg_map, owner_map, base, fine)),
        tick,
    )
    shifts = range(1, group_size)
    others = [lax.ppermute(first, "gz", rotation(group_size, shift)) for shift, first in zip(shifts, firsts)]
    packs = pl.pallas_call(
        outer_kernel,
        out_shape=shape((4 * CDOF, LANES), F32),
        in_specs=[VMEM] * 5,
        out_specs=VMEM,
        scratch_shapes=[pltpu.VMEM((8, DOF, LANES), F32)],
        compiler_params=params,
        cost_estimate=pl.CostEstimate(flops=int(5e10), bytes_accessed=int(5e7), transcendentals=0),
    )(outer, *halos)
    received = [lax.ppermute(packs, "gz", rotation(group_size, shift)) for shift in shifts]
    full = shape((AGGS, FACES * AGGS * CDOF * CDOF), F32)
    own = pl.pallas_call(
        functools.partial(own_kernel, group_size),
        out_shape=full,
        in_specs=[VMEM] * (3 + group_size),
        out_specs=VMEM,
        compiler_params=params,
        cost_estimate=pl.CostEstimate(flops=int(1e9), bytes_accessed=int(2e6), transcendentals=0),
    )(inner, layer_rows, firsts[0], packs, *others)
    out = pl.pallas_call(
        functools.partial(final_kernel, group_size),
        out_shape=full,
        in_specs=[VMEM] * (2 * group_size - 1),
        out_specs=HBM,
        scratch_shapes=[pltpu.VMEM(full.shape, F32), pltpu.SemaphoreType.DMA((FACES,))],
        compiler_params=params,
    )(own, *received, *others)
    return out[None, None]


def solution(mesh):
    placed = (P("gx", "gy", "gz", None, None), P("gx", "gy", "gz", None), P(), P("gx", "gy", "gz"))
    return jax.shard_map(
        shards, mesh=mesh, in_specs=placed, out_specs=P("gx", "gy", "gz", None), check_vma=False
    )
```

```python
import functools

import jax
import jax.numpy as jnp
from jax import lax
from jax.experimental import pallas as pl
from jax.experimental.pallas import tpu as pltpu
from jax.sharding import PartitionSpec as P

DOF = 64
CDOF = 16
AGGS = 8
FACES = 7
LANES = 128
WIDE = 2 * LANES
F32 = jnp.float32
BF16 = jnp.bfloat16
VMEM = pl.BlockSpec(memory_space=pltpu.VMEM)
HBM = pl.BlockSpec(memory_space=pltpu.HBM)


def iota(shape, dim):
    return lax.broadcasted_iota(jnp.int32, shape, dim)


def dot(a, b):
    return lax.dot_general(a, b, (((1,), (0,)), ((), ())), preferred_element_type=F32)


def split(x):
    high = x.astype(BF16)
    return high, (x - high.astype(F32)).astype(BF16)


def ones_where(mask):
    return jnp.where(mask, 1.0, 0.0).astype(BF16)


def rows_of(parts):
    return jnp.concatenate(parts, axis=0)


def lanes_of(parts):
    return jnp.concatenate(parts, axis=1)


def spread_blocks(out_ref, pieces):
    slot = iota((8, LANES), 1) // CDOF
    for b in range(8):
        value = pltpu.roll(pieces[0], -b * CDOF % LANES, 1)
        for i in range(1, 4):
            value = jnp.where(slot == i, pltpu.roll(pieces[i], (i - b) * CDOF % LANES, 1), value)
        out_ref[pl.ds(b, 8, stride=8), :] = value


def factor_of(full):
    left = iota((DOF, LANES), 1) < DOF
    high = full.astype(BF16).astype(F32)
    both = jnp.where(left, high, pltpu.roll(full - high, DOF, 1)).astype(BF16)
    first = jnp.where(left, high, 0.0).astype(BF16)
    return rows_of([both, both, first, first])


def folded(full):
    half = DOF // 2
    return jnp.where(iota((half, LANES), 1) < DOF, full[:half], pltpu.roll(full[half:], DOF, 1))


def unfolded(part):
    left = iota((DOF // 2, LANES), 1) < DOF
    turned = pltpu.roll(part, DOF, 1)
    return rows_of([jnp.where(left, part, turned), jnp.where(left, turned, part)])


def blocks_of(rows, factor):
    out = dot(rows, factor)
    return out + pltpu.roll(out, DOF, 1)


def diagonal(product, shift):
    keep = iota((DOF, LANES), 0) // CDOF + shift == iota((DOF, LANES), 1) // CDOF % 4
    kept = jnp.where(keep, product, 0.0).reshape(4, CDOF, LANES)
    return (kept[0] + kept[1]) + (kept[2] + kept[3])


def flatten(packs):
    spread = ones_where(iota((WIDE, WIDE), 0) % CDOF == iota((WIDE, WIDE), 1) % CDOF)
    element = ones_where(iota((LANES, WIDE), 0) // CDOF == iota((LANES, WIDE), 1) // CDOF % 8)
    row = iota((LANES, WIDE), 0) % CDOF == iota((LANES, WIDE), 1) // CDOF
    wide = [rows_of([lanes_of(split(pack))] * 8) * element for pack in packs]
    flat = dot(rows_of(wide), spread)
    out = []
    for i in range(len(packs)):
        out.append(rows_of(split(jnp.where(row, flat[i * LANES : (i + 1) * LANES], 0.0))))
    return out


def choose(labels, base, count):
    return ones_where(iota((count, LANES), 0) + base == labels)


def tick_kernel(out_ref):
    out_ref[...] = jnp.ones(out_ref.shape, F32)


def local_kernel(shape, group_size, agg_ref, owner_ref, prolong_ref, fine_ref, tick_ref,
                 outer_ref, inner_ref, layer_ref, *refs):
    bx, by, bz = shape
    columns = bx * by
    rows_each = AGGS // group_size
    sends, (rows_scr, blocks_scr, left_scr) = refs[:-3], refs[-3:]
    gx, gy, gz = lax.axis_index("gx"), lax.axis_index("gy"), lax.axis_index("gz")
    nx, ny, nz = agg_ref.shape

    band = iota((8, LANES), 1) // 32
    lefts = []
    for xy in range(columns):
        for z in range(bz):
            piece = prolong_ref[xy, pl.ds(z, 8, stride=bz), :]
            for tau in range(4):
                turned = pltpu.roll(piece, 32 * ((z - tau) % 4), 1) if z != tau else piece
                left_scr[xy, pl.ds(tau * 4 + z, 8, stride=16), :] = jnp.where(band == z, turned, 0.0)
        lefts.append(split(left_scr[xy].T))
    for xy in range(columns):
        spread_blocks(blocks_scr.at[xy], [prolong_ref[xy, pl.ds(z, 8, stride=bz), :] for z in range(bz)])
    low, high = ([prolong_ref[xy, pl.ds(z, 8, stride=bz), :] for xy in range(columns)] for z in (0, bz - 1))
    layers = [[jnp.where(gz == 0, h, l) for l, h in zip(low, high)]] if group_size == 2 else [low, high]
    for i, layer in enumerate(layers):
        spread_blocks(blocks_scr.at[columns + i], layer)
    factors = [factor_of(blocks_scr[xy]) for xy in range(columns)]

    wide_lane = iota((4, CDOF, WIDE), 2) % LANES
    for xy in range(columns):
        high, low = lefts[xy]
        left = rows_of([lanes_of([high, high]), lanes_of([low, jnp.zeros_like(low)])])
        for first in range(0, FACES, 2):
            count = min(2, FACES - first)
            width = count * LANES
            halves = [split(fine_ref[xy * FACES + first + i]) for i in range(count)]
            right = rows_of([lanes_of([h[i] for h in halves]) for i in range(2)])
            out = dot(left, right).reshape(2, 4, 2, CDOF, width)
            out = out[0] + out[1]
            q = jnp.where(wide_lane[:, :, :width] < DOF, out[:, 0], out[:, 1]).reshape(DOF, width)
            high_q, low_q = split(q)
            for i in range(count):
                cut = slice(i * LANES, (i + 1) * LANES)
                rows_scr[xy * FACES + first + i] = lanes_of([high_q[:, cut], low_q[:, cut]])

    for side in range(2):
        outer_ref[side] = rows_scr[side * FACES + 1]
        outer_ref[2 + side] = rows_scr[(2 + side) * FACES + 2]
        outer_ref[4 + side] = rows_scr[2 * side * FACES + 3]
        outer_ref[6 + side] = rows_scr[(2 * side + 1) * FACES + 4]
    low = rows_of([rows_scr[xy * FACES + 5, :CDOF] for xy in range(columns)])
    high = rows_of([rows_scr[xy * FACES + 6, DOF - CDOF :] for xy in range(columns)])
    layers = [jnp.where(gz == 0, high, low)] if group_size == 2 else [low, high]
    layer_parts = []
    for i, layer in enumerate(layers):
        layer_ref[i] = layer
        both = layer[:, :LANES].astype(F32) + layer[:, LANES:].astype(F32)
        for part in (both + pltpu.roll(both, DOF, 1), blocks_scr[columns + i]):
            layer_parts.append(folded(part))

    aggs = (agg_ref[...] + 1).reshape(nx * ny, nz).astype(F32).astype(BF16)
    width = 5 * LANES
    z_row, z_lane = iota((nz, width), 0), iota((nz, width), 1)
    kind, place = z_lane // LANES, z_lane % LANES
    slot, face = place // CDOF % 4, (1 - gz) if group_size == 2 else place // DOF
    z_off = jnp.where(kind == 0, slot, jnp.where(kind == 1, slot + 1, slot - 1))
    z_off = jnp.where(kind == 3, face * (bz - 1), jnp.where(kind == 4, face * (bz + 1) - 1, z_off))
    by_lane = dot(aggs, ones_where(z_row == gz * bz + z_off)).astype(BF16)
    count = 24
    r = iota((count, nx * ny), 0)
    own_x, own_y = r // 2 % 2, r % 2
    group = r // 4
    dx = jnp.where(group == 1, 1 - own_x, own_x)
    dy = jnp.where(group == 2, 1 - own_y, own_y)
    dx = jnp.where(group == 4, own_x * (bx + 1) - 1, jnp.where(group == 5, own_y, dx))
    dy = jnp.where(group == 4, own_y, jnp.where(group == 5, own_x * (by + 1) - 1, dy))
    px, py = gx * bx + dx, gy * by + dy
    inside = (px >= 0) & (px < nx) & (py >= 0) & (py < ny) & (group != 3)
    at = jnp.where(inside, px * ny + py, -1)
    table = dot(ones_where(iota((count, nx * ny), 1) == at), by_lane).astype(jnp.int32)
    owners = owner_ref[0]
    slots = iota((1, AGGS), 1)
    rank = jnp.zeros((1, AGGS), jnp.int32)
    for a in range(AGGS - 1):
        rank += jnp.where((slots > a) & (owners == owners[:, a : a + 1]), 1, 0)
    own = table[:16]
    owner = jnp.zeros_like(own)
    ranks = jnp.zeros_like(own)
    for a in range(AGGS):
        owner = jnp.where(own == a + 1, owners[:, a : a + 1], owner)
        ranks = jnp.where(own == a + 1, rank[:, a : a + 1], ranks)
    inner_base = owner * (AGGS * rows_each) + ranks
    outer_base = owner * (AGGS * AGGS) + gz * rows_each + ranks

    def cut(array, row, part):
        return array[row : row + 1, part * LANES : (part + 1) * LANES]

    first_half = iota((1, LANES), 1) < DOF
    level = iota((1, LANES), 1) // CDOF % 4

    def pair(array, one, two, part=0):
        return jnp.where(first_half, cut(array, one, part), cut(array, two, part))

    labels = []
    for row, part, valid in ((0, 0, None), (4, 0, None), (8, 0, None), (0, 1, level < bz - 1), (0, 2, level > 0)):
        for x in range(bx):
            label = pair(inner_base, row + 2 * x, row + 2 * x + 1, part)
            label += (pair(table, 2 * x, 2 * x + 1) - 1) * rows_each
            labels.append(label if valid is None else jnp.where(valid, label, -1))
    outer_labels = []
    for k, pick in enumerate(((0, 1), (2, 3), (0, 2), (1, 3))):
        other = pair(table, 16 + 2 * k, 17 + 2 * k)
        label = pair(outer_base, *pick) + (other - 1) * AGGS
        outer_labels.append(jnp.where(other > 0, label, -1))

    def by_column(array, part):
        value = cut(array, 0, part)
        for xy in range(1, columns):
            value = jnp.where(level == xy, cut(array, xy, part), value)
        return value

    other = by_column(table, 4)
    label = by_column(outer_base + owner * (AGGS * AGGS), 3) + (other - 1) * AGGS
    label += (1 - gz) * AGGS * AGGS if group_size == 2 else jnp.where(first_half, 0, AGGS * AGGS)
    outer_labels.append(jnp.where(other > 0, label, -1))
    outer_labels = rows_of(outer_labels + [jnp.full((3, LANES), -1, jnp.int32)]).astype(F32)

    pieces = [[] for _ in range(5)]
    for x in range(bx):
        for y in range(by):
            xy = x * by + y
            sources = (
                (xy * FACES, 0),
                (((1 - x) * by + y) * FACES + (2 if x else 1), 0),
                ((x * by + 1 - y) * FACES + (4 if y else 3), 0),
                (xy * FACES + 5, -1),
                (xy * FACES + 6, 1),
            )
            product = blocks_of(rows_of([rows_scr[index] for index, _ in sources]), factors[xy])
            for i, (_, shift) in enumerate(sources):
                pieces[i].append(diagonal(product[i * DOF : (i + 1) * DOF], shift))
    half = iota((CDOF, LANES), 1) < DOF
    packs = [jnp.where(half, p[2 * x], p[2 * x + 1]) for p in pieces for x in range(bx)]
    flat = flatten(packs)
    chosen = [choose(label, 0, AGGS * AGGS) for label in labels]
    inner_ref[...] = dot(lanes_of([c for c in chosen for _ in range(2)]), rows_of(flat))
    count = AGGS * AGGS // group_size
    for shift, send in enumerate(sends, 1):
        target = lax.rem(gz + shift, group_size)
        block = inner_ref[pl.ds(pl.multiple_of(target * count, count), count)]
        send[:count] = block[:, :LANES]
        send[count : 2 * count] = block[:, LANES:]
        send[2 * count :] = rows_of([outer_labels] + layer_parts)


def outer_kernel(outer_ref, odd_y, even_y, odd_x, even_x, packs_ref, blocks_scr):
    place = 0
    for axis, even, odd, low, high in (("gx", even_x, odd_x, (2, 3), (0, 1)), ("gy", even_y, odd_y, (1, 3), (0, 2))):
        second = lax.rem(lax.axis_index(axis), 2) == 1
        for one, two, columns in ((even, odd, low), (odd, even, high)):
            for xy in columns:
                rows = [pl.ds(z, 8, stride=4) for z in range(4)]
                spread_blocks(blocks_scr.at[place], [jnp.where(second, one[xy, z, :], two[xy, z, :]) for z in rows])
                place += 1
    pieces = [diagonal(blocks_of(outer_ref[i], factor_of(blocks_scr[i])), 0) for i in range(8)]
    half = iota((CDOF, LANES), 1) < DOF
    packs_ref[...] = rows_of([jnp.where(half, pieces[i], pieces[i + 1]) for i in range(0, 8, 2)])


def parts_of(tail):
    halves = [tail[at : at + DOF // 2] for at in range(8, tail.shape[0], DOF // 2)]
    return tail[:8].astype(jnp.int32), halves[::2], halves[1::2]


def own_kernel(group_size, inner_ref, layer_ref, send_ref, packs_ref, *refs):
    received, out_ref = refs[:-1], refs[-1]
    gz = lax.axis_index("gz")
    rows_each = AGGS // group_size
    count = AGGS * AGGS // group_size
    size = AGGS * AGGS
    own_labels, _, own_blocks = parts_of(send_ref[2 * count :])
    tails = [parts_of(ref[2 * count :]) for ref in received]

    left = iota((DOF, LANES), 1) < DOF
    rows = [[layer_ref[i] for i in range(layer_ref.shape[0])]]
    factors = [[factor_of(unfolded(part)) for part in own_blocks]]
    for _, layers, blocks in tails:
        rows.append([lanes_of(split(jnp.where(left, unfolded(layer), 0.0))) for layer in layers])
        factors.append([factor_of(unfolded(part)) for part in blocks])
    layer_labels = [own_labels[4:5]] + [labels[4:5] for labels, _, _ in tails]
    half = iota((CDOF, LANES), 1) < DOF
    if group_size == 2:
        pieces = [diagonal(blocks_of(rows[i][0], factors[1 - i][0]), 0) for i in range(2)]
        layer_packs = [jnp.where(half, *pieces)]
        layer_labels = [jnp.where(half[:1], *layer_labels)]
    else:
        low, high = {}, {}
        for i in range(group_size):
            above = (i - 1) % group_size
            high[i] = diagonal(blocks_of(rows[i][1], factors[above][0]), 0)
            low[above] = diagonal(blocks_of(rows[above][0], factors[i][1]), 0)
        layer_packs = [jnp.where(half, low[i], high[i]) for i in range(group_size)]

    flat = flatten([packs_ref[k * CDOF : (k + 1) * CDOF] for k in range(4)] + layer_packs)
    for k in range(4):
        chosen = choose(own_labels[k : k + 1], gz * size, size)
        value = dot(lanes_of([chosen] * 2), flat[k])
        for c in range(AGGS):
            at = ((k + 1) * AGGS + c) * WIDE
            out_ref[:, at : at + WIDE] = value[c * AGGS : (c + 1) * AGGS]
    chosen = [choose(label, gz * 2 * size, 2 * size) for label in layer_labels]
    value = dot(lanes_of([c for c in chosen for _ in range(2)]), rows_of(flat[4:]))
    for c in range(2 * AGGS):
        at = (5 * AGGS + c) * WIDE
        out_ref[:, at : at + WIDE] = value[c * AGGS : (c + 1) * AGGS]

    block = inner_ref[pl.ds(pl.multiple_of(gz * count, count), count)]
    brick = iota((AGGS, LANES), 0) // rows_each
    for c in range(AGGS):
        at = slice(c * rows_each, (c + 1) * rows_each)
        for h in range(2):
            value = rows_of([block[at, h * LANES : (h + 1) * LANES]] * group_size)
            for shift, ref in enumerate(received, 1):
                part = ref[h * count + c * rows_each : h * count + (c + 1) * rows_each]
                theirs = lax.rem(gz - shift + group_size, group_size)
                value = jnp.where(brick == theirs, rows_of([part] * group_size), value)
            out_ref[:, (2 * c + h) * LANES : (2 * c + h + 1) * LANES] = value


def final_kernel(group_size, own_ref, *refs):
    packs, firsts, (out_hbm, out_ref, sems) = refs[: group_size - 1], refs[group_size - 1 : -3], refs[-3:]
    gz = lax.axis_index("gz")
    count = AGGS * AGGS // group_size
    size = AGGS * AGGS
    copies = []

    def send_out(source, first, last):
        part = pl.ds(first * AGGS * WIDE, (last - first) * AGGS * WIDE)
        copies.append(pltpu.make_async_copy(source.at[:, part], out_hbm.at[:, part], sems.at[first]))
        copies[-1].start()

    send_out(own_ref, 0, 1)
    send_out(own_ref, 5, 7)
    flat = flatten([pack[k * CDOF : (k + 1) * CDOF] for k in range(4) for pack in packs])
    labels = [ref[2 * count : 2 * count + 8].astype(jnp.int32) for ref in firsts]
    for k in range(4):
        chosen = [choose(label[k : k + 1], gz * size, size) for label in labels]
        parts = flat[k * len(packs) : (k + 1) * len(packs)]
        value = dot(lanes_of([c for c in chosen for _ in range(2)]), rows_of(parts))
        for c in range(AGGS):
            cut = slice(((k + 1) * AGGS + c) * WIDE, ((k + 1) * AGGS + c + 1) * WIDE)
            out_ref[:, cut] = own_ref[:, cut] + value[c * AGGS : (c + 1) * AGGS]
        send_out(out_ref, k + 1, k + 2)
    for copy in copies:
        copy.wait()


def matching(sizes, along, first):
    def partner(place):
        i = (place[along] - first) ^ 1
        moved = list(place)
        if 0 <= i + first < sizes[along] and place[along] >= first:
            moved[along] = i + first
        elif place[1 - along] ^ 1 < sizes[1 - along]:
            moved[1 - along] = place[1 - along] ^ 1
        return moved[0] * sizes[1] + moved[1]

    return [(x * sizes[1] + y, partner((x, y))) for x in range(sizes[0]) for y in range(sizes[1])]


def rotation(count, step):
    return [(i, (i + step) % count) for i in range(count)]


def shards(fine_blocks, prolong, agg_map, owner_map):
    bx, by, bz = fine_blocks.shape[:3]
    columns = bx * by
    group_size = lax.axis_size("gz")
    fine = fine_blocks.transpose(0, 1, 3, 2, 4).reshape(columns * FACES, bz, 32, LANES)
    fine = fine.transpose(0, 2, 1, 3).reshape(columns * FACES, 32 * bz, LANES)
    base = prolong.reshape(columns, bz, 8, LANES).transpose(0, 2, 1, 3).reshape(columns, 8 * bz, LANES)
    tick = pl.pallas_call(
        tick_kernel,
        out_shape=pltpu.VMEM((8, LANES), F32),
        out_specs=VMEM,
        cost_estimate=pl.CostEstimate(flops=int(5e9), bytes_accessed=int(5e7), transcendentals=0),
    )()
    sizes = lax.axis_size("gx"), lax.axis_size("gy")
    even_x, odd_x, even_y, odd_y = [
        lax.ppermute(base, ("gx", "gy"), matching(sizes, along, first)) for along in range(2) for first in range(2)
    ]
    halos = [odd_y, even_y, odd_x, even_x]
    layers = 1 if group_size == 2 else 2
    params = pltpu.CompilerParams(vmem_limit_bytes=32 * 1024 * 1024)
    shape = jax.ShapeDtypeStruct
    size = 2 * AGGS * AGGS // group_size + 8 + layers * DOF
    outer, inner, layer_rows, *firsts = pl.pallas_call(
        functools.partial(local_kernel, (bx, by, bz), group_size),
        out_shape=[
            shape((8, DOF, WIDE), BF16),
            shape((AGGS * AGGS, WIDE), F32),
            shape((layers, DOF, WIDE), BF16),
        ]
        + [shape((size, LANES), F32)] * (group_size - 1),
        in_specs=[VMEM] * 5,
        out_specs=[VMEM] * (2 + group_size),
        scratch_shapes=[
            pltpu.VMEM((columns * FACES, DOF, WIDE), BF16),
            pltpu.VMEM((columns + layers, DOF, LANES), F32),
            pltpu.VMEM((columns, LANES, LANES), F32),
        ],
        compiler_params=params,
        cost_estimate=pl.CostEstimate(flops=int(2e9), bytes_accessed=int(4e6), transcendentals=0),
    )(
        *(pltpu.with_memory_space_constraint(a, pltpu.VMEM) for a in (agg_map, owner_map, base, fine)),
        tick,
    )
    shifts = range(1, group_size)
    others = [lax.ppermute(first, "gz", rotation(group_size, shift)) for shift, first in zip(shifts, firsts)]
    packs = pl.pallas_call(
        outer_kernel,
        out_shape=shape((4 * CDOF, LANES), F32),
        in_specs=[VMEM] * 5,
        out_specs=VMEM,
        scratch_shapes=[pltpu.VMEM((8, DOF, LANES), F32)],
        compiler_params=params,
        cost_estimate=pl.CostEstimate(flops=int(5e10), bytes_accessed=int(5e7), transcendentals=0),
    )(outer, *halos)
    received = [lax.ppermute(packs, "gz", rotation(group_size, shift)) for shift in shifts]
    full = shape((AGGS, FACES * AGGS * CDOF * CDOF), F32)
    own = pl.pallas_call(
        functools.partial(own_kernel, group_size),
        out_shape=full,
        in_specs=[VMEM] * (3 + group_size),
        out_specs=VMEM,
        compiler_params=params,
        cost_estimate=pl.CostEstimate(flops=int(1e9), bytes_accessed=int(2e6), transcendentals=0),
    )(inner, layer_rows, firsts[0], packs, *others)
    out = pl.pallas_call(
        functools.partial(final_kernel, group_size),
        out_shape=full,
        in_specs=[VMEM] * (2 * group_size - 1),
        out_specs=HBM,
        scratch_shapes=[pltpu.VMEM(full.shape, F32), pltpu.SemaphoreType.DMA((FACES,))],
        compiler_params=params,
    )(own, *received, *others)
    return out[None, None]


def solution(mesh):
    placed = (P("gx", "gy", "gz", None, None), P("gx", "gy", "gz", None), P(), P("gx", "gy", "gz"))
    return jax.shard_map(
        shards, mesh=mesh, in_specs=placed, out_specs=P("gx", "gy", "gz", None), check_vma=False
    )
```

```python
import functools

import jax
import jax.numpy as jnp
from jax import lax
from jax.experimental import pallas as pl
from jax.experimental.pallas import tpu as pltpu
from jax.sharding import PartitionSpec as P

DOF = 64
CDOF = 16
AGGS = 8
FACES = 7
LANES = 128
WIDE = 2 * LANES
F32 = jnp.float32
BF16 = jnp.bfloat16
VMEM = pl.BlockSpec(memory_space=pltpu.VMEM)
HBM = pl.BlockSpec(memory_space=pltpu.HBM)


def iota(shape, dim):
    return lax.broadcasted_iota(jnp.int32, shape, dim)


def dot(a, b):
    return lax.dot_general(a, b, (((1,), (0,)), ((), ())), preferred_element_type=F32)


def split(x):
    high = x.astype(BF16)
    return high, (x - high.astype(F32)).astype(BF16)


def ones_where(mask):
    return jnp.where(mask, 1.0, 0.0).astype(BF16)


def rows_of(parts):
    return jnp.concatenate(parts, axis=0)


def lanes_of(parts):
    return jnp.concatenate(parts, axis=1)


def spread_blocks(out_ref, pieces):
    slot = iota((8, LANES), 1) // CDOF
    for b in range(8):
        value = pltpu.roll(pieces[0], -b * CDOF % LANES, 1)
        for i in range(1, 4):
            value = jnp.where(slot == i, pltpu.roll(pieces[i], (i - b) * CDOF % LANES, 1), value)
        out_ref[pl.ds(b, 8, stride=8), :] = value


def factor_of(full):
    left = iota((DOF, LANES), 1) < DOF
    high = full.astype(BF16).astype(F32)
    both = jnp.where(left, high, pltpu.roll(full - high, DOF, 1)).astype(BF16)
    first = jnp.where(left, high, 0.0).astype(BF16)
    return rows_of([both, both, first, first])


def folded(full):
    half = DOF // 2
    return jnp.where(iota((half, LANES), 1) < DOF, full[:half], pltpu.roll(full[half:], DOF, 1))


def unfolded(part):
    left = iota((DOF // 2, LANES), 1) < DOF
    turned = pltpu.roll(part, DOF, 1)
    return rows_of([jnp.where(left, part, turned), jnp.where(left, turned, part)])


def blocks_of(rows, factor):
    out = dot(rows, factor)
    return out + pltpu.roll(out, DOF, 1)


def diagonal(product, shift):
    keep = iota((DOF, LANES), 0) // CDOF + shift == iota((DOF, LANES), 1) // CDOF % 4
    kept = jnp.where(keep, product, 0.0).reshape(4, CDOF, LANES)
    return (kept[0] + kept[1]) + (kept[2] + kept[3])


def flatten(packs):
    spread = ones_where(iota((WIDE, WIDE), 0) % CDOF == iota((WIDE, WIDE), 1) % CDOF)
    element = ones_where(iota((LANES, WIDE), 0) // CDOF == iota((LANES, WIDE), 1) // CDOF % 8)
    row = iota((LANES, WIDE), 0) % CDOF == iota((LANES, WIDE), 1) // CDOF
    wide = [rows_of([lanes_of(split(pack))] * 8) * element for pack in packs]
    flat = dot(rows_of(wide), spread)
    out = []
    for i in range(len(packs)):
        out.append(rows_of(split(jnp.where(row, flat[i * LANES : (i + 1) * LANES], 0.0))))
    return out


def choose(labels, base, count):
    return ones_where(iota((count, LANES), 0) + base == labels)


def tick_kernel(out_ref):
    out_ref[...] = jnp.ones(out_ref.shape, F32)


def local_kernel(shape, group_size, agg_ref, owner_ref, prolong_ref, fine_ref, tick_ref,
                 outer_ref, inner_ref, layer_ref, *refs):
    bx, by, bz = shape
    columns = bx * by
    rows_each = AGGS // group_size
    sends, (rows_scr, blocks_scr, left_scr) = refs[:-3], refs[-3:]
    gx, gy, gz = lax.axis_index("gx"), lax.axis_index("gy"), lax.axis_index("gz")
    nx, ny, nz = agg_ref.shape

    band = iota((8, LANES), 1) // 32
    lefts = []
    for xy in range(columns):
        for z in range(bz):
            piece = prolong_ref[xy, pl.ds(z, 8, stride=bz), :]
            for tau in range(4):
                turned = pltpu.roll(piece, 32 * ((z - tau) % 4), 1) if z != tau else piece
                left_scr[xy, pl.ds(tau * 4 + z, 8, stride=16), :] = jnp.where(band == z, turned, 0.0)
        lefts.append(split(left_scr[xy].T))
    for xy in range(columns):
        spread_blocks(blocks_scr.at[xy], [prolong_ref[xy, pl.ds(z, 8, stride=bz), :] for z in range(bz)])
    low, high = ([prolong_ref[xy, pl.ds(z, 8, stride=bz), :] for xy in range(columns)] for z in (0, bz - 1))
    layers = [[jnp.where(gz == 0, h, l) for l, h in zip(low, high)]] if group_size == 2 else [low, high]
    for i, layer in enumerate(layers):
        spread_blocks(blocks_scr.at[columns + i], layer)
    factors = [factor_of(blocks_scr[xy]) for xy in range(columns)]

    wide_lane = iota((4, CDOF, WIDE), 2) % LANES
    for xy in range(columns):
        high, low = lefts[xy]
        left = rows_of([lanes_of([high, high]), lanes_of([low, jnp.zeros_like(low)])])
        for first in range(0, FACES, 2):
            count = min(2, FACES - first)
            width = count * LANES
            halves = [split(fine_ref[xy * FACES + first + i]) for i in range(count)]
            right = rows_of([lanes_of([h[i] for h in halves]) for i in range(2)])
            out = dot(left, right).reshape(2, 4, 2, CDOF, width)
            out = out[0] + out[1]
            q = jnp.where(wide_lane[:, :, :width] < DOF, out[:, 0], out[:, 1]).reshape(DOF, width)
            high_q, low_q = split(q)
            for i in range(count):
                cut = slice(i * LANES, (i + 1) * LANES)
                rows_scr[xy * FACES + first + i] = lanes_of([high_q[:, cut], low_q[:, cut]])

    for side in range(2):
        outer_ref[side] = rows_scr[side * FACES + 1]
        outer_ref[2 + side] = rows_scr[(2 + side) * FACES + 2]
        outer_ref[4 + side] = rows_scr[2 * side * FACES + 3]
        outer_ref[6 + side] = rows_scr[(2 * side + 1) * FACES + 4]
    low = rows_of([rows_scr[xy * FACES + 5, :CDOF] for xy in range(columns)])
    high = rows_of([rows_scr[xy * FACES + 6, DOF - CDOF :] for xy in range(columns)])
    layers = [jnp.where(gz == 0, high, low)] if group_size == 2 else [low, high]
    layer_parts = []
    for i, layer in enumerate(layers):
        layer_ref[i] = layer
        both = layer[:, :LANES].astype(F32) + layer[:, LANES:].astype(F32)
        for part in (both + pltpu.roll(both, DOF, 1), blocks_scr[columns + i]):
            layer_parts.append(folded(part))

    aggs = (agg_ref[...] + 1).reshape(nx * ny, nz).astype(F32).astype(BF16)
    width = 5 * LANES
    z_row, z_lane = iota((nz, width), 0), iota((nz, width), 1)
    kind, place = z_lane // LANES, z_lane % LANES
    slot, face = place // CDOF % 4, (1 - gz) if group_size == 2 else place // DOF
    z_off = jnp.where(kind == 0, slot, jnp.where(kind == 1, slot + 1, slot - 1))
    z_off = jnp.where(kind == 3, face * (bz - 1), jnp.where(kind == 4, face * (bz + 1) - 1, z_off))
    by_lane = dot(aggs, ones_where(z_row == gz * bz + z_off)).astype(BF16)
    count = 24
    r = iota((count, nx * ny), 0)
    own_x, own_y = r // 2 % 2, r % 2
    group = r // 4
    dx = jnp.where(group == 1, 1 - own_x, own_x)
    dy = jnp.where(group == 2, 1 - own_y, own_y)
    dx = jnp.where(group == 4, own_x * (bx + 1) - 1, jnp.where(group == 5, own_y, dx))
    dy = jnp.where(group == 4, own_y, jnp.where(group == 5, own_x * (by + 1) - 1, dy))
    px, py = gx * bx + dx, gy * by + dy
    inside = (px >= 0) & (px < nx) & (py >= 0) & (py < ny) & (group != 3)
    at = jnp.where(inside, px * ny + py, -1)
    table = dot(ones_where(iota((count, nx * ny), 1) == at), by_lane).astype(jnp.int32)
    owners = owner_ref[0]
    slots = iota((1, AGGS), 1)
    rank = jnp.zeros((1, AGGS), jnp.int32)
    for a in range(AGGS - 1):
        rank += jnp.where((slots > a) & (owners == owners[:, a : a + 1]), 1, 0)
    own = table[:16]
    owner = jnp.zeros_like(own)
    ranks = jnp.zeros_like(own)
    for a in range(AGGS):
        owner = jnp.where(own == a + 1, owners[:, a : a + 1], owner)
        ranks = jnp.where(own == a + 1, rank[:, a : a + 1], ranks)
    inner_base = owner * (AGGS * rows_each) + ranks
    outer_base = owner * (AGGS * AGGS) + gz * rows_each + ranks

    def cut(array, row, part):
        return array[row : row + 1, part * LANES : (part + 1) * LANES]

    first_half = iota((1, LANES), 1) < DOF
    level = iota((1, LANES), 1) // CDOF % 4

    def pair(array, one, two, part=0):
        return jnp.where(first_half, cut(array, one, part), cut(array, two, part))

    labels = []
    for row, part, valid in ((0, 0, None), (4, 0, None), (8, 0, None), (0, 1, level < bz - 1), (0, 2, level > 0)):
        for x in range(bx):
            label = pair(inner_base, row + 2 * x, row + 2 * x + 1, part)
            label += (pair(table, 2 * x, 2 * x + 1) - 1) * rows_each
            labels.append(label if valid is None else jnp.where(valid, label, -1))
    outer_labels = []
    for k, pick in enumerate(((0, 1), (2, 3), (0, 2), (1, 3))):
        other = pair(table, 16 + 2 * k, 17 + 2 * k)
        label = pair(outer_base, *pick) + (other - 1) * AGGS
        outer_labels.append(jnp.where(other > 0, label, -1))

    def by_column(array, part):
        value = cut(array, 0, part)
        for xy in range(1, columns):
            value = jnp.where(level == xy, cut(array, xy, part), value)
        return value

    other = by_column(table, 4)
    label = by_column(outer_base + owner * (AGGS * AGGS), 3) + (other - 1) * AGGS
    label += (1 - gz) * AGGS * AGGS if group_size == 2 else jnp.where(first_half, 0, AGGS * AGGS)
    outer_labels.append(jnp.where(other > 0, label, -1))
    outer_labels = rows_of(outer_labels + [jnp.full((3, LANES), -1, jnp.int32)]).astype(F32)

    pieces = [[] for _ in range(5)]
    for x in range(bx):
        for y in range(by):
            xy = x * by + y
            sources = (
                (xy * FACES, 0),
                (((1 - x) * by + y) * FACES + (2 if x else 1), 0),
                ((x * by + 1 - y) * FACES + (4 if y else 3), 0),
                (xy * FACES + 5, -1),
                (xy * FACES + 6, 1),
            )
            product = blocks_of(rows_of([rows_scr[index] for index, _ in sources]), factors[xy])
            for i, (_, shift) in enumerate(sources):
                pieces[i].append(diagonal(product[i * DOF : (i + 1) * DOF], shift))
    half = iota((CDOF, LANES), 1) < DOF
    packs = [jnp.where(half, p[2 * x], p[2 * x + 1]) for p in pieces for x in range(bx)]
    flat = flatten(packs)
    chosen = [choose(label, 0, AGGS * AGGS) for label in labels]
    inner_ref[...] = dot(lanes_of([c for c in chosen for _ in range(2)]), rows_of(flat))
    count = AGGS * AGGS // group_size
    for shift, send in enumerate(sends, 1):
        target = lax.rem(gz + shift, group_size)
        block = inner_ref[pl.ds(pl.multiple_of(target * count, count), count)]
        send[:count] = block[:, :LANES]
        send[count : 2 * count] = block[:, LANES:]
        send[2 * count :] = rows_of([outer_labels] + layer_parts)


def outer_kernel(outer_ref, odd_y, even_y, odd_x, even_x, packs_ref, blocks_scr):
    place = 0
    for axis, even, odd, low, high in (("gx", even_x, odd_x, (2, 3), (0, 1)), ("gy", even_y, odd_y, (1, 3), (0, 2))):
        second = lax.rem(lax.axis_index(axis), 2) == 1
        for one, two, columns in ((even, odd, low), (odd, even, high)):
            for xy in columns:
                rows = [pl.ds(z, 8, stride=4) for z in range(4)]
                spread_blocks(blocks_scr.at[place], [jnp.where(second, one[xy, z, :], two[xy, z, :]) for z in rows])
                place += 1
    pieces = [diagonal(blocks_of(outer_ref[i], factor_of(blocks_scr[i])), 0) for i in range(8)]
    half = iota((CDOF, LANES), 1) < DOF
    packs_ref[...] = rows_of([jnp.where(half, pieces[i], pieces[i + 1]) for i in range(0, 8, 2)])


def parts_of(tail):
    halves = [tail[at : at + DOF // 2] for at in range(8, tail.shape[0], DOF // 2)]
    return tail[:8].astype(jnp.int32), halves[::2], halves[1::2]


def own_kernel(group_size, inner_ref, layer_ref, send_ref, packs_ref, *refs):
    received, out_ref = refs[:-1], refs[-1]
    gz = lax.axis_index("gz")
    rows_each = AGGS // group_size
    count = AGGS * AGGS // group_size
    size = AGGS * AGGS
    own_labels, _, own_blocks = parts_of(send_ref[2 * count :])
    tails = [parts_of(ref[2 * count :]) for ref in received]

    left = iota((DOF, LANES), 1) < DOF
    rows = [[layer_ref[i] for i in range(layer_ref.shape[0])]]
    factors = [[factor_of(unfolded(part)) for part in own_blocks]]
    for _, layers, blocks in tails:
        rows.append([lanes_of(split(jnp.where(left, unfolded(layer), 0.0))) for layer in layers])
        factors.append([factor_of(unfolded(part)) for part in blocks])
    layer_labels = [own_labels[4:5]] + [labels[4:5] for labels, _, _ in tails]
    half = iota((CDOF, LANES), 1) < DOF
    if group_size == 2:
        pieces = [diagonal(blocks_of(rows[i][0], factors[1 - i][0]), 0) for i in range(2)]
        layer_packs = [jnp.where(half, *pieces)]
        layer_labels = [jnp.where(half[:1], *layer_labels)]
    else:
        low, high = {}, {}
        for i in range(group_size):
            above = (i - 1) % group_size
            high[i] = diagonal(blocks_of(rows[i][1], factors[above][0]), 0)
            low[above] = diagonal(blocks_of(rows[above][0], factors[i][1]), 0)
        layer_packs = [jnp.where(half, low[i], high[i]) for i in range(group_size)]

    flat = flatten([packs_ref[k * CDOF : (k + 1) * CDOF] for k in range(4)] + layer_packs)
    for k in range(4):
        chosen = choose(own_labels[k : k + 1], gz * size, size)
        value = dot(lanes_of([chosen] * 2), flat[k])
        for c in range(AGGS):
            at = ((k + 1) * AGGS + c) * WIDE
            out_ref[:, at : at + WIDE] = value[c * AGGS : (c + 1) * AGGS]
    chosen = [choose(label, gz * 2 * size, 2 * size) for label in layer_labels]
    value = dot(lanes_of([c for c in chosen for _ in range(2)]), rows_of(flat[4:]))
    for c in range(2 * AGGS):
        at = (5 * AGGS + c) * WIDE
        out_ref[:, at : at + WIDE] = value[c * AGGS : (c + 1) * AGGS]

    block = inner_ref[pl.ds(pl.multiple_of(gz * count, count), count)]
    brick = iota((AGGS, LANES), 0) // rows_each
    for c in range(AGGS):
        at = slice(c * rows_each, (c + 1) * rows_each)
        for h in range(2):
            value = rows_of([block[at, h * LANES : (h + 1) * LANES]] * group_size)
            for shift, ref in enumerate(received, 1):
                part = ref[h * count + c * rows_each : h * count + (c + 1) * rows_each]
                theirs = lax.rem(gz - shift + group_size, group_size)
                value = jnp.where(brick == theirs, rows_of([part] * group_size), value)
            out_ref[:, (2 * c + h) * LANES : (2 * c + h + 1) * LANES] = value


def final_kernel(group_size, own_ref, *refs):
    packs, firsts, (out_hbm, out_ref, sems) = refs[: group_size - 1], refs[group_size - 1 : -3], refs[-3:]
    gz = lax.axis_index("gz")
    count = AGGS * AGGS // group_size
    size = AGGS * AGGS
    copies = []

    def send_out(source, first, last):
        part = pl.ds(first * AGGS * WIDE, (last - first) * AGGS * WIDE)
        copies.append(pltpu.make_async_copy(source.at[:, part], out_hbm.at[:, part], sems.at[first]))
        copies[-1].start()

    send_out(own_ref, 0, 1)
    send_out(own_ref, 5, 7)
    flat = [f for k in range(4) for f in flatten([pack[k * CDOF : (k + 1) * CDOF] for pack in packs])]
    labels = [ref[2 * count : 2 * count + 8].astype(jnp.int32) for ref in firsts]
    for k in range(4):
        chosen = [choose(label[k : k + 1], gz * size, size) for label in labels]
        parts = flat[k * len(packs) : (k + 1) * len(packs)]
        value = dot(lanes_of([c for c in chosen for _ in range(2)]), rows_of(parts))
        for c in range(AGGS):
            cut = slice(((k + 1) * AGGS + c) * WIDE, ((k + 1) * AGGS + c + 1) * WIDE)
            out_ref[:, cut] = own_ref[:, cut] + value[c * AGGS : (c + 1) * AGGS]
        send_out(out_ref, k + 1, k + 2)
    for copy in copies:
        copy.wait()


def matching(sizes, along, first):
    def partner(place):
        i = (place[along] - first) ^ 1
        moved = list(place)
        if 0 <= i + first < sizes[along] and place[along] >= first:
            moved[along] = i + first
        elif place[1 - along] ^ 1 < sizes[1 - along]:
            moved[1 - along] = place[1 - along] ^ 1
        return moved[0] * sizes[1] + moved[1]

    return [(x * sizes[1] + y, partner((x, y))) for x in range(sizes[0]) for y in range(sizes[1])]


def rotation(count, step):
    return [(i, (i + step) % count) for i in range(count)]


def shards(fine_blocks, prolong, agg_map, owner_map):
    bx, by, bz = fine_blocks.shape[:3]
    columns = bx * by
    group_size = lax.axis_size("gz")
    fine = fine_blocks.transpose(0, 1, 3, 2, 4).reshape(columns * FACES, bz, 32, LANES)
    fine = fine.transpose(0, 2, 1, 3).reshape(columns * FACES, 32 * bz, LANES)
    base = prolong.reshape(columns, bz, 8, LANES).transpose(0, 2, 1, 3).reshape(columns, 8 * bz, LANES)
    tick = pl.pallas_call(
        tick_kernel,
        out_shape=pltpu.VMEM((8, LANES), F32),
        out_specs=VMEM,
        cost_estimate=pl.CostEstimate(flops=int(5e9), bytes_accessed=int(5e7), transcendentals=0),
    )()
    sizes = lax.axis_size("gx"), lax.axis_size("gy")
    even_x, odd_x, even_y, odd_y = [
        lax.ppermute(base, ("gx", "gy"), matching(sizes, along, first)) for along in range(2) for first in range(2)
    ]
    halos = [odd_y, even_y, odd_x, even_x]
    layers = 1 if group_size == 2 else 2
    params = pltpu.CompilerParams(vmem_limit_bytes=32 * 1024 * 1024)
    shape = jax.ShapeDtypeStruct
    size = 2 * AGGS * AGGS // group_size + 8 + layers * DOF
    outer, inner, layer_rows, *firsts = pl.pallas_call(
        functools.partial(local_kernel, (bx, by, bz), group_size),
        out_shape=[
            shape((8, DOF, WIDE), BF16),
            shape((AGGS * AGGS, WIDE), F32),
            shape((layers, DOF, WIDE), BF16),
        ]
        + [shape((size, LANES), F32)] * (group_size - 1),
        in_specs=[VMEM] * 5,
        out_specs=[VMEM] * (2 + group_size),
        scratch_shapes=[
            pltpu.VMEM((columns * FACES, DOF, WIDE), BF16),
            pltpu.VMEM((columns + layers, DOF, LANES), F32),
            pltpu.VMEM((columns, LANES, LANES), F32),
        ],
        compiler_params=params,
        cost_estimate=pl.CostEstimate(flops=int(2e9), bytes_accessed=int(4e6), transcendentals=0),
    )(
        *(pltpu.with_memory_space_constraint(a, pltpu.VMEM) for a in (agg_map, owner_map, base, fine)),
        tick,
    )
    shifts = range(1, group_size)
    others = [lax.ppermute(first, "gz", rotation(group_size, shift)) for shift, first in zip(shifts, firsts)]
    packs = pl.pallas_call(
        outer_kernel,
        out_shape=shape((4 * CDOF, LANES), F32),
        in_specs=[VMEM] * 5,
        out_specs=VMEM,
        scratch_shapes=[pltpu.VMEM((8, DOF, LANES), F32)],
        compiler_params=params,
        cost_estimate=pl.CostEstimate(flops=int(5e10), bytes_accessed=int(5e7), transcendentals=0),
    )(outer, *halos)
    received = [lax.ppermute(packs, "gz", rotation(group_size, shift)) for shift in shifts]
    full = shape((AGGS, FACES * AGGS * CDOF * CDOF), F32)
    own = pl.pallas_call(
        functools.partial(own_kernel, group_size),
        out_shape=full,
        in_specs=[VMEM] * (3 + group_size),
        out_specs=VMEM,
        compiler_params=params,
        cost_estimate=pl.CostEstimate(flops=int(1e9), bytes_accessed=int(2e6), transcendentals=0),
    )(inner, layer_rows, firsts[0], packs, *others)
    out = pl.pallas_call(
        functools.partial(final_kernel, group_size),
        out_shape=full,
        in_specs=[VMEM] * (2 * group_size - 1),
        out_specs=HBM,
        scratch_shapes=[pltpu.VMEM(full.shape, F32), pltpu.SemaphoreType.DMA((FACES,))],
        compiler_params=params,
    )(own, *received, *others)
    return out[None, None]


def solution(mesh):
    placed = (P("gx", "gy", "gz", None, None), P("gx", "gy", "gz", None), P(), P("gx", "gy", "gz"))
    return jax.shard_map(
        shards, mesh=mesh, in_specs=placed, out_specs=P("gx", "gy", "gz", None), check_vma=False
    )
```
